256 devices in a mesh: gx: 16 (over x, y), gy: 16 (over z, core).
Axes of the slice: x: 4, y: 4, z: 8, core: 2. Of those that a mesh axis runs over, the one named last changes fastest.
Arguments:
- labels: int32 [32, 256, 2048], P(None, 'gx', 'gy'), may hold values from 0 to 2, as said below
- conduct_x: bfloat16 [32, 256, 2048], P(None, 'gx', 'gy'), may hold values from 0.0099487305 to 1
- conduct_y: bfloat16 [32, 256, 2048], P(None, 'gx', 'gy'), may hold values from 0.0099487305 to 1
- conduct_z: bfloat16 [32, 256, 2048], P(None, 'gx', 'gy'), may hold values from 0.0009994507 to 0.099609375
Outputs:
- potential: float32 [32, 256, 2048], P(None, 'gx', 'gy')
The draws below stay inside these ranges and needn't reach their ends.
Inputs may be any that keep to these rules, and one draw needn't show every extreme that they name: `labels`: 0 marks a free voxel, 1 a seed of the first object, 2 a seed of the second.
All inputs are finite; a program needn't handle non-finite values.
Results may differ from the reference program's by a relative error of at most 0.0003.
Values sent between devices are 32-bit elements; how exact they have to be, the bound alone decides.
No kernel may reach another device: no remote copies, remote signals or barrier semaphores. Data moves between devices by JAX's collectives and lax.ppermute only.
A program may use at most 64 MiB of HBM per device.

```python
import math
import jax
import jax.numpy as jnp
from jax import lax

CX = 16
CY = 128
NZ = 32
NU = 4
COARSE_SWEEPS = 24
NX = 256
NY = 2048


def draw_labels(key, part):
    key = jax.random.fold_in(key, 7)
    region_key, sprinkle_key, single_key = jax.random.split(key, 3)
    region_rows = NX // 8
    region_cols = NY // 8
    regions = region_rows * region_cols
    picked = max(1, regions // 32)
    shuffled = jax.random.permutation(region_key, regions)
    region_kind = jnp.zeros((regions,), jnp.int32)
    region_kind = region_kind.at[shuffled[:picked]].set(1)
    region_kind = region_kind.at[shuffled[picked:2 * picked]].set(2)
    region_kind = jnp.repeat(jnp.repeat(region_kind.reshape(region_rows, region_cols), 8, 0), 8, 1)
    sprinkle = jax.random.randint(sprinkle_key, (NZ, NX, NY), 0, 8)
    labels = jnp.where(sprinkle == 0, region_kind[None, :, :], 0)
    places = jax.random.randint(single_key, (2, NX // CX, NY // CY), 0, NZ * CX * CY)
    depth_index = lax.broadcasted_iota(jnp.int32, (NZ, NX, NY), 0)
    row_index = lax.broadcasted_iota(jnp.int32, (NZ, NX, NY), 1)
    col_index = lax.broadcasted_iota(jnp.int32, (NZ, NX, NY), 2)
    local_index = depth_index * (CX * CY) + row_index % CX * CY + col_index % CY
    first_place = jnp.repeat(jnp.repeat(places[0], CX, 0), CY, 1)[None, :, :]
    second_place = jnp.repeat(jnp.repeat(places[1], CX, 0), CY, 1)[None, :, :]
    labels = jnp.where(local_index == first_place, 1, labels)
    labels = jnp.where(local_index == second_place, 2, labels)
    return labels.astype(jnp.int32)


def level_of(own_key, extent, cuts, least, high):
    level, own = 1.0, jax.random.fold_in(own_key, 6)
    for dim, shards_of in cuts:
        heights = jnp.exp(jax.random.uniform(jax.random.fold_in(own, dim), (shards_of,), jnp.float32, least / len(cuts), high / len(cuts)))
        level = level * jnp.repeat(heights, extent[dim] // shards_of).reshape([-1 if axis == dim else 1 for axis in range(len(extent))])
    return level


def setup_inputs(seed: int = 0) -> dict:
    arg_keys = jax.random.split(jax.random.key(seed), 5)
    return {
        "labels": draw_labels(jax.random.fold_in(arg_keys[4], 71), 0),
        "conduct_x": jnp.clip(jnp.exp(math.log(1.0) - 4.61031033 * jax.random.uniform(arg_keys[1], (NZ, NX, NY), jnp.float32) ** level_of(arg_keys[1], (NZ, NX, NY), ((1, 16), (2, 16)), -0.2, 0.2)), 0.0099487305, 1.0).astype(jnp.bfloat16),
        "conduct_y": jnp.clip(jnp.exp(math.log(1.0) - 4.61031033 * jax.random.uniform(arg_keys[2], (NZ, NX, NY), jnp.float32) ** level_of(arg_keys[2], (NZ, NX, NY), ((1, 16), (2, 16)), -0.2, 0.2)), 0.0099487305, 1.0).astype(jnp.bfloat16),
        "conduct_z": jnp.clip(jnp.exp(math.log(0.099609375) - 4.6018058 * jax.random.uniform(arg_keys[3], (NZ, NX, NY), jnp.float32) ** level_of(arg_keys[3], (NZ, NX, NY), ((1, 16), (2, 16)), -0.2, 0.2)), 0.0009994507, 0.099609375).astype(jnp.bfloat16),
    }


OMEGA = 0.8
LEAK = 0.005


def shift_down(field, axis):
    pads = [(0, 0), (0, 0), (0, 0)]
    pads[axis] = (1, 0)
    return lax.slice_in_dim(jnp.pad(field, pads), 0, field.shape[axis], axis=axis)


def apply_operator(field, operator):
    fwd_x, back_x, fwd_y, back_y, fwd_z, back_z, diagonal, divisor = operator
    padded = jnp.pad(field, ((1, 1), (1, 1), (1, 1)))
    beside_all = fwd_x * padded[1:-1, 2:, 1:-1] + back_x * padded[1:-1, :-2, 1:-1]
    beside_all = beside_all + fwd_y * padded[1:-1, 1:-1, 2:] + back_y * padded[1:-1, 1:-1, :-2]
    beside_all = beside_all + fwd_z * padded[2:, 1:-1, 1:-1] + back_z * padded[:-2, 1:-1, 1:-1]
    return diagonal * field - beside_all


def make_operator(fwd_x, fwd_y, fwd_z, extra, free):
    back_x = shift_down(fwd_x, 1)
    back_y = shift_down(fwd_y, 2)
    back_z = shift_down(fwd_z, 0)
    diagonal = fwd_x.astype(jnp.float32) + back_x.astype(jnp.float32)
    diagonal = diagonal + fwd_y.astype(jnp.float32) + back_y.astype(jnp.float32)
    diagonal = diagonal + fwd_z.astype(jnp.float32) + back_z.astype(jnp.float32) + extra
    divisor = diagonal + 1.0 - free
    return (fwd_x, back_x, fwd_y, back_y, fwd_z, back_z, diagonal, divisor)


def blocks(field):
    depth, rows, cols = field.shape
    return field.astype(jnp.float32).reshape(depth, rows // 2, 2, cols // 2, 2)


def coarsen(fwd_x, fwd_y, fwd_z, extra, free):
    return (blocks(fwd_x)[:, :, 1, :, :].sum(3), blocks(fwd_y)[:, :, :, :, 1].sum(2),
            blocks(fwd_z).sum((2, 4)), blocks(extra).sum((2, 4)), blocks(free).max((2, 4)))


def relax(field, rhs, operator):
    return field + OMEGA * (rhs - apply_operator(field, operator)) / operator[7]


def vcycle(level, rhs, operators, masks):
    operator = operators[level]
    field = jnp.zeros_like(rhs)
    if level == 3:
        for sweep in range(COARSE_SWEEPS):
            field = relax(field, rhs, operator)
        return field
    for sweep in range(NU):
        field = relax(field, rhs, operator)
    residual = rhs - apply_operator(field, operator)
    coarse = vcycle(level + 1, blocks(residual).sum((2, 4)), operators, masks)
    field = field + jnp.repeat(jnp.repeat(coarse, 2, 1), 2, 2) * masks[level]
    for sweep in range(NU):
        field = relax(field, rhs, operator)
    return field


def reference(labels, conduct_x, conduct_y, conduct_z):
    free = (labels == 0).astype(jnp.float32)
    first = (labels == 1).astype(jnp.float32)
    cond_x = conduct_x.at[:, -1, :].set(jnp.zeros((), jnp.bfloat16))
    cond_y = conduct_y.at[:, :, -1].set(jnp.zeros((), jnp.bfloat16))
    cond_z = conduct_z.at[-1].set(jnp.zeros((), jnp.bfloat16))
    pad_free = jnp.pad(free, ((1, 1), (1, 1), (1, 1)))
    pad_first = jnp.pad(first, ((1, 1), (1, 1), (1, 1)))
    views = [(slice(1, -1), slice(2, None), slice(1, -1)), (slice(1, -1), slice(None, -2), slice(1, -1)),
             (slice(1, -1), slice(1, -1), slice(2, None)), (slice(1, -1), slice(1, -1), slice(None, -2)),
             (slice(2, None), slice(1, -1), slice(1, -1)), (slice(None, -2), slice(1, -1), slice(1, -1))]
    edges = [cond_x, shift_down(cond_x, 1), cond_y, shift_down(cond_y, 2), cond_z, shift_down(cond_z, 0)]
    extra = jnp.full(free.shape, LEAK, jnp.float32)
    rhs = jnp.zeros(free.shape, jnp.float32)
    for edge, view in zip(edges, views):
        extra = extra + edge.astype(jnp.float32) * (1.0 - pad_free[view])
        rhs = rhs + edge.astype(jnp.float32) * pad_first[view]
    extra = free * extra
    rhs = free * rhs
    fwd_x = cond_x * (free * pad_free[views[0]]).astype(jnp.bfloat16)
    fwd_y = cond_y * (free * pad_free[views[2]]).astype(jnp.bfloat16)
    fwd_z = cond_z * (free * pad_free[views[4]]).astype(jnp.bfloat16)
    level_data = (fwd_x, fwd_y, fwd_z, extra, free)
    operators = []
    masks = []
    for level in range(4):
        operators.append(make_operator(*level_data))
        masks.append(level_data[4])
        if level < 3:
            level_data = coarsen(*level_data)
    return vcycle(0, rhs, operators, masks)
```

```python
import functools

import jax
import jax.numpy as jnp
from jax import lax
from jax.experimental import pallas as pl
from jax.experimental.pallas import tpu as pltpu
from jax.sharding import PartitionSpec as P

NU = 4
COARSE_SWEEPS = 24
OMEGA = 0.8
LEAK = 0.005

NZ = 32
H0 = 13
R0 = 16
N0 = R0 + 2 * H0
GROUPS = (N0 + 7) // 8
H1 = 6
N1 = 8 + 2 * H1
F32 = jnp.float32


def spec():
    return pl.BlockSpec(memory_space=pltpu.VMEM)


def call(kernel, ins, outs, scratch=(), limit=24, apart=()):
    places = [pl.BlockSpec(memory_space=pl.ANY) if i in apart else spec() for i in range(len(ins))]
    return pl.pallas_call(
        kernel,
        out_shape=[jax.ShapeDtypeStruct(s, F32) for s in outs],
        in_specs=places,
        out_specs=[spec() for _ in outs],
        scratch_shapes=[pltpu.VMEM(s, F32) if isinstance(s, tuple) else s for s in scratch],
        compiler_params=pltpu.CompilerParams(vmem_limit_bytes=limit * 1024 * 1024),
    )(*ins)


def lanes(shape):
    return lax.broadcasted_iota(jnp.int32, shape, len(shape) - 1)


def roll(value, shift, axis):
    size = value.shape[axis]
    shift = shift % size
    return value if shift == 0 else pltpu.roll(value, shift, axis)


def planes(lo, hi, body, step=16):
    whole = (hi - lo) // step

    def chunk(i, carry):
        for k in range(step):
            body(lo + i * step + k)
        return carry

    if whole == 1:
        chunk(0, 0)
    elif whole:
        lax.fori_loop(0, whole, chunk, 0)
    for p in range(lo + whole * step, hi):
        body(p)


def ahead_z(v):
    return jnp.concatenate([v[8:], roll(v[:8], -1, 0)], 0)


def behind_z(v):
    return jnp.concatenate([roll(v[24:], 1, 0), v[:24]], 0)


def neighbours(v_ref, fx, fy, fz, p):
    v = v_ref[p]
    s = fx[p] * v_ref[p + 1] + fx[p - 1] * v_ref[p - 1]
    cy = fy[p]
    s = s + cy * roll(v, -1, 1) + roll(cy * v, 1, 1)
    cz = fz[p]
    s = s + cz * ahead_z(v) + behind_z(cz * v)
    return v, s


def sweep(src, dst, f, g, fx, fy, fz, lo, hi, step=16):
    def body(p):
        v, s = neighbours(src, fx, fy, fz, p)
        dst[p] = (1.0 - OMEGA) * v + g[p] * (f[p] + s)

    planes(lo, hi, body, step)


def residual(src, dst, f, d, fx, fy, fz, lo, hi, step=16):
    def body(p):
        v, s = neighbours(src, fx, fy, fz, p)
        dst[p] = f[p] - d[p] * v + s

    planes(lo, hi, body, step)


def diagonal(extra, fx, fy, fz, p):
    cy, cz = fy[p], fz[p]
    return extra + fx[p] + fx[p - 1] + cy + roll(cy, 1, 1) + cz + behind_z(cz)


def scale_of(d):
    free = d > 0.0
    return jnp.where(free, OMEGA / jnp.where(free, d, 1.0), 0.0)


def selection(rows, cols, target, odd=False):
    row = lax.broadcasted_iota(jnp.int32, (rows, cols), 0)
    col = lax.broadcasted_iota(jnp.int32, (rows, cols), 1)
    hit = col == target(row)
    if odd:
        hit = hit & (row % 2 == 1)
    return hit.astype(F32)


def dot(a, matrix):
    matrix = matrix.astype(jnp.bfloat16)
    total = None
    for _ in range(3):
        part = a.astype(jnp.bfloat16)
        a = a - part.astype(F32)
        product = jnp.dot(part, matrix, preferred_element_type=F32)
        total = product if total is None else total + product
    return total


def fetch(pairs, sems):
    copies = [pltpu.make_async_copy(src, dst, sems.at[i]) for i, (src, dst) in enumerate(pairs)]
    for copy in copies:
        copy.start()
    return copies


def stage_kernel(
    in0, in1, in2, in3, own, to_right, to_left, labels, cond_x, cond_y, cond_z, sems
):
    copies = fetch(((in0, labels), (in1, cond_x), (in2, cond_y), (in3, cond_z)), sems)
    last_x = lax.axis_index("gx") == lax.axis_size("gx") - 1
    last_y = lax.axis_index("gy") == lax.axis_size("gy") - 1
    shape = (R0, 8, 128)
    row = lax.broadcasted_iota(jnp.int32, shape, 0)
    for a, ref in enumerate((labels, cond_x, cond_y, cond_z)):
        copies[a].wait()
        for b in range(4):
            value = jnp.stack([ref[4 * s + b].astype(F32) for s in range(8)])
            value = jnp.swapaxes(value, 0, 1)
            if a == 1:
                value = jnp.where(last_x & (row == R0 - 1), 0.0, value)
            if a == 2:
                value = jnp.where(last_y & (lanes(shape) == 127), 0.0, value)
            if a == 3 and b == 3:
                last = lax.broadcasted_iota(jnp.int32, shape, 1) == 7
                value = jnp.where(last, 0.0, value)
            part = slice(8 * b, 8 * b + 8)
            own[a, :, part] = value
            to_right[a, :, part] = value[R0 - H0 :]
            to_left[a, :, part] = value[:H0]


def edge_kernel(own, behind, ahead, to_right, to_left):
    lane = lanes((NZ, 128))

    def plane(a, p):
        if p < H0:
            return behind[a, p]
        if p < H0 + R0:
            return own[a, p - H0]
        return ahead[a, p - H0 - R0]

    for a in range(4):
        for c in range(GROUPS):
            right = left = jnp.zeros((NZ, 128), F32)
            for k in range(8):
                if 8 * c + k < N0:
                    value = roll(plane(a, 8 * c + k), 16 * k + 16, 1)
                    right = jnp.where(lane // 16 == k, value, right)
                    left = jnp.where(lane // 16 == (k + 1) % 8, value, left)
            to_right[a, c] = right
            to_left[a, c] = left


def down_kernel(
    own, behind, ahead, from_left, from_right,
    keep0, ops1, own1, kept_f1, to_right, to_left, own3,
    ext, fx, fy, fz, d, g, f, va, vb, t, t1, d1, f1, va1, vb1, x2, y2, z2, e2,
):
    lane = lanes((NZ, 128))
    for a in range(4):
        ext[a, 0:H0, :, 0:128] = behind[a]
        ext[a, H0 : H0 + R0, :, 0:128] = own[a]
        ext[a, H0 + R0 : N0, :, 0:128] = ahead[a]
        for c in range(GROUPS):
            left, right = from_left[a, c], from_right[a, c]
            for k in range(8):
                if 8 * c + k < N0:
                    both = jnp.where(lane // 16 == k, left, right)
                    ext[a, 8 * c + k, :, 128:256] = roll(both, -16 * k - 16, 1)

    def cut(value, *kinds):
        for kind in kinds:
            value = jnp.where(kind, value, 0.0)
        return value

    fx[0] = cut(ext[1, 0], ext[0, 0] == 0.0, ext[0, 1] == 0.0)

    def operator0(p):
        label, label_up, label_down = ext[0, p], ext[0, p + 1], ext[0, p - 1]
        cx, cx_back, cy, cz = ext[1, p], ext[1, p - 1], ext[2, p], ext[3, p]
        cy_back, cz_back = roll(cy, 1, 1), behind_z(cz)
        y_up, y_down = roll(label, -1, 1), roll(label, 1, 1)
        z_up, z_down = ahead_z(label), behind_z(label)
        free = label == 0.0
        extra, rhs, diag = LEAK, 0.0, LEAK
        edges = (
            (cx, label_up), (cx_back, label_down), (cy, y_up), (cy_back, y_down), (cz, z_up), (cz_back, z_down),
        )
        for edge, across in edges:
            extra = extra + jnp.where(across == 0.0, 0.0, edge)
            rhs = rhs + jnp.where(across == 1.0, edge, 0.0)
            diag = diag + edge
        rhs, diag = cut(rhs, free), cut(diag, free)
        scale = scale_of(diag)
        fx[p] = cut(cx, free, label_up == 0.0)
        fy[p] = cut(cy, free, y_up == 0.0)
        fz[p] = cut(cz, free, z_up == 0.0)
        d[p], g[p], f[p] = diag, scale, rhs
        va[p] = scale * rhs
        t[p] = cut(extra, free)

    planes(1, N0 - 1, operator0, 4)
    src, dst = va, vb
    for s in range(NU - 1):
        sweep(src, dst, f, g, fx, fy, fz, 2 + s, N0 - 2 - s)
        src, dst = dst, src

    lo = H0 - 4
    for i, ref in enumerate((src, f, g, fx, fy, fz)):
        keep0[i] = ref[lo : lo + 24]

    def to1(row):
        return jnp.where(row < 192, row // 2, row // 2 - 128) + 32

    pick, pick_odd = selection(256, 128, to1), selection(256, 128, to1, True)

    def coarsen1(q):
        p = 2 * q + 1
        t1[0, q] = fx[p + 1]
        t1[1, q] = fy[p] + fy[p + 1]
        t1[2, q] = fz[p] + fz[p + 1]
        t1[3, q] = t[p] + t[p + 1]

    planes(0, N1, coarsen1, 4)
    for a in range(4):
        for c in range(0, N1, 4):
            value = t1[a, c : c + 4].reshape(4 * NZ, 256)
            ops1[a, c : c + 4] = dot(value, pick_odd if a == 1 else pick).reshape(4, NZ, 128)

    residual(src, dst, f, d, fx, fy, fz, H0 - 8, H0 + R0 + 8)
    f1[0:2] = jnp.zeros((2, NZ, 128), F32)
    f1[N1 - 2 : N1] = jnp.zeros((2, NZ, 128), F32)
    for c in range(2, N1 - 2, 4):
        value = jnp.stack([dst[2 * q + 1] + dst[2 * q + 2] for q in range(c, c + 4)])
        f1[c : c + 4] = dot(value.reshape(4 * NZ, 256), pick).reshape(4, NZ, 128)

    x1, y1, z1, e1, g1 = (ops1.at[a] for a in range(5))
    g1[0] = jnp.where(e1[0] > 0.0, 1.0, 0.0)

    def operator1(q):
        diag = diagonal(e1[q], x1, y1, z1, q)
        d1[q] = diag
        scale = scale_of(diag)
        g1[q] = scale
        va1[q] = scale * f1[q]

    planes(1, N1, operator1)
    src, dst = va1, vb1
    for s in range(NU - 1):
        sweep(src, dst, f1, g1, x1, y1, z1, 3 + s, N1 - 3 - s)
        src, dst = dst, src
    own1[...] = src[H1 : H1 + 8]
    kept_f1[...] = f1[...]
    residual(src, dst, f1, d1, x1, y1, z1, H1, H1 + 8)

    half, half_odd = (selection(128, 128, lambda row: row // 2, odd) for odd in (False, True))
    q = [H1 + 2 * k for k in range(4)]
    f2 = dot(jnp.concatenate([dst[i] + dst[i + 1] for i in q]), half).reshape(4, NZ, 128)
    x2[...] = dot(jnp.concatenate([x1[i + 1] for i in [H1 - 2] + q]), half).reshape(5, NZ, 128)
    y2[...] = dot(jnp.concatenate([y1[i] + y1[i + 1] for i in q]), half_odd).reshape(4, NZ, 128)
    z2[...] = dot(jnp.concatenate([z1[i] + z1[i + 1] for i in q]), half).reshape(4, NZ, 128)
    e2[...] = dot(jnp.concatenate([e1[i] + e1[i + 1] for i in q]), half).reshape(4, NZ, 128)

    def around(x, x_back, y, z, extra):
        return extra + x + x_back + y + roll(y, 1, 1) + z + behind_z(z)

    for a in range(5):
        for h in range(2):
            pair = []
            for k in (2 * h, 2 * h + 1):
                if a == 4:
                    pair.append(around(x2[k + 1], x2[k], y2[k], z2[k], e2[k]))
                else:
                    pair.append((f2, x2[1:], y2, z2)[a][k])
            both = pair[0] + roll(pair[1], 64, 1)
            to_right[2 * a + h] = both
            to_left[2 * a + h] = both

    right = left = jnp.zeros((NZ, 128), F32)
    for k in range(8):
        here = lane // 8 == k
        right = jnp.where(here, roll(own1[k], 8 * k - 88, 1), right)
        left = jnp.where(here, roll(own1[k], 8 * k - 32, 1), left)
    to_right[10] = right
    to_left[10] = left

    x3 = dot(jnp.concatenate([x2[0], x2[2], x2[4]]), half).reshape(3, NZ, 128)
    y3 = dot(jnp.concatenate([y2[0] + y2[1], y2[2] + y2[3]]), half_odd).reshape(2, NZ, 128)
    z3 = dot(jnp.concatenate([z2[0] + z2[1], z2[2] + z2[3]]), half).reshape(2, NZ, 128)
    e3 = dot(jnp.concatenate([e2[0] + e2[1], e2[2] + e2[3]]), half).reshape(2, NZ, 128)
    total = jnp.zeros((NZ, 128), F32)
    for i in range(2):
        d3 = around(x3[i + 1], x3[i], y3[i], z3[i], e3[i])
        for a, value in enumerate((x3[i + 1], y3[i], z3[i], d3)):
            spot = 32 * a + 16 * i
            total = jnp.where(lane // 16 == spot // 16, roll(value, spot - 8, 1), total)
    own3[...] = total
    to_right[11] = total
    to_left[11] = total


def join_kernel(
    own2, own1, f1, left, right, left3, right3,
    joined2, first2, last2, joined1, to_right, to_left, near3,
):
    lane = lanes((NZ, 128))
    low, high = lane % 64 < 16, lane % 64 >= 48
    for a in range(10):
        value = jnp.where(high, roll(right[a], 32, 1), own2[a])
        value = jnp.where(low, roll(left[a], -32, 1), value)
        joined2[a] = value
        to_right[a] = value
        to_left[a] = value
        (last2 if a % 2 else first2)[a // 2] = value
    low, high = lane // 8 == 3, lane // 8 == 12
    for k in range(8):
        value = jnp.where(low, roll(left[10], 24 - 8 * k, 1), own1[k])
        value = jnp.where(high, roll(right[10], 96 - 8 * k, 1), value)
        joined1[k] = value
        if k >= 8 - H1:
            to_right[10 + k - 8 + H1] = value
        if k < H1:
            to_left[10 + k] = value
    to_right[10 + H1] = f1[H1 + 8 - 5]
    to_left[10 + H1] = f1[H1 + 4]
    for s, value in enumerate((left3[...], left[11], own2[11], right[11], right3[...])):
        near3[s] = value


def rows_of(value, odd):
    return roll(value, 64, 1) if odd else value


def middle_kernel(behind, own, ahead, out, f, fx, fy, fz, d, g, va, vb):
    for j in range(12):
        source = (behind, own, ahead)[j // 4]
        for a, ref in enumerate((f, fx, fy, fz, d)):
            ref[j] = rows_of(source[2 * a + j % 4 // 2], j % 2)
        g[j] = scale_of(d[j])
        va[j] = g[j] * f[j]
    src, dst = va, vb
    for s in range(NU - 1):
        sweep(src, dst, f, g, fx, fy, fz, 1 + s, 11 - s)
        src, dst = dst, src
    residual(src, dst, f, d, fx, fy, fz, 4, 8)
    total = None
    for i in range(2):
        matrix = selection(
            128, 128, lambda row: jnp.where((row >= 16) & (row < 48), (row - 16) // 2 + 16 * i, -99)
        )
        part = dot(dst[4 + 2 * i] + dst[5 + 2 * i], matrix)
        total = part if total is None else total + part
    value = total[:8]
    for b in range(1, 4):
        value = value + roll(total[8 * b : 8 * b + 8], 32 * b, 1)
    out[...] = value


def near_kernel(count, *refs):
    for c in range(count):
        for s in range(5):
            refs[5][c, s] = refs[s][...]


PAD3 = 8


def spread3_kernel(count, gathered, ops3):
    rows = 2 * count
    lo, hi = PAD3, PAD3 + rows
    lane = lanes((NZ, 128))
    for a in range(4):
        ops3[a, 0:lo] = jnp.zeros((PAD3, NZ, 128), F32)
        ops3[a, hi : hi + PAD3] = jnp.zeros((PAD3, NZ, 128), F32)

    def unpack(i, carry):
        for a in range(4):
            for r in range(2):
                total = jnp.zeros((NZ, 128), F32)
                for s in range(5):
                    value = roll(gathered[i, s], 16 * s - 32 * a - 16 * r, 1)
                    total = jnp.where(lane // 16 == s, value, total)
                ops3[a, lo + 2 * i + r] = scale_of(total) if a == 3 else total
        return carry

    lax.fori_loop(0, count, unpack, 0)


def solve_kernel(count, rhs3, ops3, out, f3, va3, vb3):
    rows = 2 * count
    lo, hi = PAD3, PAD3 + rows
    lane8 = lanes((8, 128))
    x3, y3, z3, g3 = (ops3.at[a] for a in range(4))
    for ref in (va3, vb3):
        ref[0:lo] = jnp.zeros((PAD3, NZ, 128), F32)
        ref[hi : hi + PAD3] = jnp.zeros((PAD3, NZ, 128), F32)

    def unpack(i, carry):
        for r in range(2):
            p = lo + 2 * i + r
            for b in range(4):
                total = jnp.zeros((8, 128), F32)
                for s in range(5):
                    value = roll(rhs3[i, s], 16 * s - 32 * b - 16 * r, 1)
                    total = jnp.where(lane8 // 16 == s, value, total)
                f3[p, 8 * b : 8 * b + 8] = total
                va3[p, 8 * b : 8 * b + 8] = total * g3[p, 8 * b : 8 * b + 8]
        return carry

    lax.fori_loop(0, count, unpack, 0)

    def two(i, carry):
        sweep(va3, vb3, f3, g3, x3, y3, z3, lo, hi, 32)
        sweep(vb3, va3, f3, g3, x3, y3, z3, lo, hi, 32)
        return carry

    lax.fori_loop(0, (COARSE_SWEEPS - 1) // 2, two, 0)
    sweep(va3, vb3, f3, g3, x3, y3, z3, lo, hi, 32)
    start = lo + 2 * lax.axis_index("gx") - 4
    out[...] = vb3[pl.ds(start, 10)]


def up_kernel(
    e3, behind3, behind2, behind, joined2, ahead, ahead2, ahead3, joined1, kept_f1, in_ops1, in_keep0,
    out,
    f2, x2, y2, z2, d2, g2, va2, vb2, f1, va1, vb1, va0, vb0, ops1, keep0, sems,
):
    copies = fetch(((in_ops1, ops1), (in_keep0, keep0)), sems)
    sources = [(behind3, None)]
    sources += [(ref, h) for ref in (behind2, behind, joined2, ahead, ahead2) for h in range(2)]
    sources += [(ahead3, None)]
    for n, (source, h) in enumerate(sources):
        for a, ref in enumerate((f2, x2, y2, z2, d2)):
            value = source[a if h is None else 2 * a + h]
            ref[2 * n] = value
            ref[2 * n + 1] = roll(value, 64, 1)

    def operator2(j):
        g2[j] = scale_of(d2[j])
        va2[j] = g2[j] * f2[j]

    planes(0, 24, operator2, 24)
    src, dst = va2, vb2
    for s in range(NU - 1):
        sweep(src, dst, f2, g2, x2, y2, z2, 1 + s, 23 - s, 32)
        src, dst = dst, src
    col = lax.broadcasted_iota(jnp.int32, (128, 128), 1)
    row = lax.broadcasted_iota(jnp.int32, (128, 128), 0)
    spread = ((row == (col + 128 - 16) // 2 - 64 + 32) & (col < 64)).astype(F32)
    coarse = dot(e3[...].reshape(10 * NZ, 128), spread).reshape(10, NZ, 128)
    for r in range(-7, 11):
        j = r + 10
        src[j] = src[j] + jnp.where(g2[j] > 0.0, coarse[r // 2 + 4], 0.0)
    for s in range(NU):
        sweep(src, dst, f2, g2, x2, y2, z2, 4 + s, 20 - s, 32)
        src, dst = dst, src

    copies[0].wait()
    x1, y1, z1, g1 = ops1.at[0], ops1.at[1], ops1.at[2], ops1.at[4]
    f1[...] = kept_f1[...]
    f1[1] = behind[10 + H1]
    f1[N1 - 2] = ahead[10 + H1]
    spread = (row == (col - 32 + 128) // 2 - 64 + 16).astype(F32)
    coarse = dot(src[7:17].reshape(10 * NZ, 128), spread).reshape(10, NZ, 128)
    for q in range(N1):
        if q < H1:
            value = behind[10 + q]
        elif q < H1 + 8:
            value = joined1[q - H1]
        else:
            value = ahead[10 + q - H1 - 8]
        va1[q] = value + jnp.where(g1[q] > 0.0, coarse[q // 2], 0.0)
    src, dst = va1, vb1
    for s in range(NU):
        sweep(src, dst, f1, g1, x1, y1, z1, 1 + s, N1 - 1 - s, 32)
        src, dst = dst, src

    copies[1].wait()
    v0, f0, g0, x0, y0, z0 = (keep0.at[a] for a in range(6))
    col = lax.broadcasted_iota(jnp.int32, (128, 256), 1)
    row = lax.broadcasted_iota(jnp.int32, (128, 256), 0)
    spread = (row == jnp.where(col < 192, col // 2, col // 2 - 128) + 32).astype(F32)
    for c in range(0, 12, 4):
        coarse = dot(src[4 + c : 8 + c].reshape(4 * NZ, 128), spread).reshape(4, NZ, 256)
        for k in range(8):
            i = 2 * c + k
            va0[i] = v0[i] + jnp.where(g0[i] > 0.0, coarse[k // 2], 0.0)
    src, dst = va0, vb0
    for s in range(NU):
        sweep(src, dst, f0, g0, x0, y0, z0, 1 + s, 23 - s)
        src, dst = dst, src
    for b in range(4):
        value = jnp.swapaxes(src[4:20, 8 * b : 8 * b + 8, 0:128], 0, 1)
        for s in range(8):
            out[4 * s + b] = value[s]


def shift(value, axis, distance):
    count = lax.axis_size(axis)
    route = [(i, i + distance) for i in range(count) if 0 <= i + distance < count]
    return lax.ppermute(value, axis, route)


def body(labels, conduct_x, conduct_y, conduct_z):
    count = lax.axis_size("gx")
    side = (NZ, 128)
    wide = (N0, NZ, 256)
    own, to_right, to_left = call(
        stage_kernel,
        (labels, conduct_x, conduct_y, conduct_z),
        [(4, R0, *side), (4, H0, *side), (4, H0, *side)],
        [pltpu.VMEM(labels.shape, labels.dtype)]
        + [pltpu.VMEM(labels.shape, conduct_x.dtype)] * 3
        + [pltpu.SemaphoreType.DMA((4,))],
        apart=(0, 1, 2, 3),
    )
    behind = shift(to_right, "gx", 1)
    ahead = shift(to_left, "gx", -1)
    to_right, to_left = call(edge_kernel, (own, behind, ahead), [(4, GROUPS, *side)] * 2)
    from_left = shift(to_right, "gy", 1)
    from_right = shift(to_left, "gy", -1)
    keep0, ops1, own1, kept_f1, to_right, to_left, own3 = call(
        down_kernel,
        (own, behind, ahead, from_left, from_right),
        [(6, 24, NZ, 256), (5, N1, *side), (8, *side), (N1, *side), (12, *side), (12, *side), side],
        [(4, N0, NZ, 256)]
        + [wide] * 9
        + [(4, N1, NZ, 256)]
        + [(N1, *side)] * 4
        + [(5, *side)]
        + [(4, *side)] * 3,
        limit=44,
    )
    left, right = shift(to_right, "gy", 1), shift(to_left, "gy", -1)
    left3, right3 = shift(own3, "gy", 2), shift(own3, "gy", -2)
    joined2, first2, last2, joined1, to_right, to_left, near3 = call(
        join_kernel,
        (to_right, own1, kept_f1, left, right, left3, right3),
        [(10, *side), (5, *side), (5, *side), (8, *side)]
        + [(11 + H1, *side)] * 2
        + [(5, *side)],
    )
    all3 = lax.all_gather(near3, "gx")
    behind, ahead = shift(to_right, "gx", 1), shift(to_left, "gx", -1)
    (rhs3,) = call(middle_kernel, (behind, joined2, ahead), [(8, 128)], [(12, *side)] * 8)
    rhs3, joined2, first2, last2 = lax.optimization_barrier((rhs3, joined2, first2, last2))
    around = [shift(rhs3, "gy", distance) for distance in (2, 1, -1, -2)]
    behind2, ahead2 = shift(joined2, "gx", 2), shift(joined2, "gx", -2)
    behind3, ahead3 = shift(last2, "gx", 3), shift(first2, "gx", -3)
    (rhs3,) = call(
        functools.partial(near_kernel, count),
        (around[0], around[1], rhs3, around[2], around[3]),
        [(count, 5, 8, 128)],
    )
    rhs3 = lax.all_to_all(rhs3, "gx", 0, 0)
    rows3 = 2 * count + 2 * PAD3
    (ops3,) = call(functools.partial(spread3_kernel, count), (all3,), [(4, rows3, *side)])
    (e3,) = call(
        functools.partial(solve_kernel, count), (rhs3, ops3), [(10, *side)], [(rows3, *side)] * 3
    )
    (out,) = call(
        up_kernel,
        (e3, behind3, behind2, behind, joined2, ahead, ahead2, ahead3, joined1, kept_f1, ops1, keep0),
        [(NZ, R0, 128)],
        [(24, *side)] * 8
        + [(N1, *side)] * 3
        + [(24, NZ, 256)] * 2
        + [(5, N1, *side), (6, 24, NZ, 256)]
        + [pltpu.SemaphoreType.DMA((2,))],
        limit=30,
        apart=(10, 11),
    )
    return out


def solution(mesh):
    in_specs = (P(None, "gx", "gy"),) * 4
    out_specs = P(None, "gx", "gy")
    return jax.shard_map(body, mesh=mesh, in_specs=in_specs, out_specs=out_specs, check_vma=False)
```

```python
import functools

import jax
import jax.numpy as jnp
from jax import lax
from jax.experimental import pallas as pl
from jax.experimental.pallas import tpu as pltpu
from jax.sharding import PartitionSpec as P

NU = 4
COARSE_SWEEPS = 24
OMEGA = 0.8
LEAK = 0.005

NZ = 32
H0 = 13
R0 = 16
N0 = R0 + 2 * H0
GROUPS = (N0 + 7) // 8
H1 = 6
N1 = 8 + 2 * H1
F32 = jnp.float32


def spec():
    return pl.BlockSpec(memory_space=pltpu.VMEM)


def call(kernel, ins, outs, scratch=(), limit=24, apart=(), apart_outs=()):
    def places(count, left):
        return [pl.BlockSpec(memory_space=pl.ANY) if i in left else spec() for i in range(count)]

    return pl.pallas_call(
        kernel,
        out_shape=[jax.ShapeDtypeStruct(s, F32) for s in outs],
        in_specs=places(len(ins), apart),
        out_specs=places(len(outs), apart_outs),
        scratch_shapes=[pltpu.VMEM(s, F32) if isinstance(s, tuple) else s for s in scratch],
        compiler_params=pltpu.CompilerParams(vmem_limit_bytes=limit * 1024 * 1024),
    )(*ins)


def lanes(shape):
    return lax.broadcasted_iota(jnp.int32, shape, len(shape) - 1)


def roll(value, shift, axis):
    size = value.shape[axis]
    shift = shift % size
    return value if shift == 0 else pltpu.roll(value, shift, axis)


def planes(lo, hi, body, step=16):
    whole = (hi - lo) // step

    def chunk(i, carry):
        for k in range(step):
            body(lo + i * step + k)
        return carry

    if whole == 1:
        chunk(0, 0)
    elif whole:
        lax.fori_loop(0, whole, chunk, 0)
    for p in range(lo + whole * step, hi):
        body(p)


def ahead_z(v):
    return jnp.concatenate([v[8:], roll(v[:8], -1, 0)], 0)


def behind_z(v):
    return jnp.concatenate([roll(v[24:], 1, 0), v[:24]], 0)


def neighbours(v_ref, fx, fy, fz, p):
    v = v_ref[p]
    s = fx[p] * v_ref[p + 1] + fx[p - 1] * v_ref[p - 1]
    cy = fy[p]
    s = s + cy * roll(v, -1, 1) + roll(cy * v, 1, 1)
    cz = fz[p]
    s = s + cz * ahead_z(v) + behind_z(cz * v)
    return v, s


def sweep(src, dst, f, g, fx, fy, fz, lo, hi, step=16):
    def body(p):
        v, s = neighbours(src, fx, fy, fz, p)
        dst[p] = (1.0 - OMEGA) * v + g[p] * (f[p] + s)

    planes(lo, hi, body, step)


def residual(src, dst, f, d, fx, fy, fz, lo, hi, step=16):
    def body(p):
        v, s = neighbours(src, fx, fy, fz, p)
        dst[p] = f[p] - d[p] * v + s

    planes(lo, hi, body, step)


def diagonal(extra, fx, fy, fz, p):
    cy, cz = fy[p], fz[p]
    return extra + fx[p] + fx[p - 1] + cy + roll(cy, 1, 1) + cz + behind_z(cz)


def scale_of(d):
    free = d > 0.0
    return jnp.where(free, OMEGA / jnp.where(free, d, 1.0), 0.0)


def selection(rows, cols, target, odd=False):
    row = lax.broadcasted_iota(jnp.int32, (rows, cols), 0)
    col = lax.broadcasted_iota(jnp.int32, (rows, cols), 1)
    hit = col == target(row)
    if odd:
        hit = hit & (row % 2 == 1)
    return hit.astype(F32)


def dot(a, matrix):
    matrix = matrix.astype(jnp.bfloat16)
    total = None
    for _ in range(3):
        part = a.astype(jnp.bfloat16)
        a = a - part.astype(F32)
        product = jnp.dot(part, matrix, preferred_element_type=F32)
        total = product if total is None else total + product
    return total


BEHIND = (0, H0, 2 * H0, 3 * H0 - 1)
AHEAD = (0, H0, 2 * H0 - 1, 3 * H0 - 2)


def fetch(pairs, sems):
    copies = [pltpu.make_async_copy(src, dst, sems.at[i]) for i, (src, dst) in enumerate(pairs)]
    for copy in copies:
        copy.start()
    return copies


def stage_kernel(
    in0, in1, in2, in3, own, to_right, to_left, labels, cond_x, cond_y, cond_z, sems
):
    copies = fetch(((in0, labels), (in1, cond_x), (in2, cond_y), (in3, cond_z)), sems)
    last_x = lax.axis_index("gx") == lax.axis_size("gx") - 1
    last_y = lax.axis_index("gy") == lax.axis_size("gy") - 1
    shape = (R0, 8, 128)
    row = lax.broadcasted_iota(jnp.int32, shape, 0)
    for a, ref in enumerate((labels, cond_x, cond_y, cond_z)):
        copies[a].wait()
        for b in range(4):
            value = jnp.stack([ref[4 * s + b].astype(F32) for s in range(8)])
            value = jnp.swapaxes(value, 0, 1)
            if a == 1:
                value = jnp.where(last_x & (row == R0 - 1), 0.0, value)
            if a == 2:
                value = jnp.where(last_y & (lanes(shape) == 127), 0.0, value)
            if a == 3 and b == 3:
                last = lax.broadcasted_iota(jnp.int32, shape, 1) == 7
                value = jnp.where(last, 0.0, value)
            part = slice(8 * b, 8 * b + 8)
            own[a, :, part] = value
            first, count = R0 - H0 + (a > 1), H0 - (a > 1)
            to_right[BEHIND[a] : BEHIND[a] + count, part] = value[first:]
            count = H0 - (a > 0)
            to_left[AHEAD[a] : AHEAD[a] + count, part] = value[:count]


def edge_kernel(own, behind, ahead, to_right, to_left):
    lane = lanes((NZ, 128))

    def plane(a, p):
        if p < H0:
            return behind[BEHIND[a] + p - (a > 1)] if p or a < 2 else None
        if p < H0 + R0:
            return own[a, p - H0]
        return ahead[AHEAD[a] + p - H0 - R0] if p < N0 - 1 or a == 0 else None

    for a in range(4):
        for c in range(GROUPS):
            right = left = jnp.zeros((NZ, 128), F32)
            for k in range(8):
                value = plane(a, 8 * c + k) if 8 * c + k < N0 else None
                if value is not None:
                    value = roll(value, 16 * k + 16, 1)
                    right = jnp.where(lane // 16 == k, value, right)
                    left = jnp.where(lane // 16 == (k + 1) % 8, value, left)
            to_right[a, c] = right
            to_left[a, c] = left


def down_kernel(
    own, behind, ahead, from_left, from_right,
    keep0, out_ops1, out_f1, own1, edge_f1, to_right, to_left,
    ext, fx, fy, fz, d, g, f, va, vb, t, t1, ops1, d1, f1, va1, vb1, x2, y2, z2, e2, sems,
):
    lane = lanes((NZ, 128))
    for a in range(4):
        skip, count = int(a > 1), H0 - (a > 0)
        ext[a, skip:H0, :, 0:128] = behind[BEHIND[a] : BEHIND[a] + H0 - skip]
        ext[a, H0 : H0 + R0, :, 0:128] = own[a]
        ext[a, H0 + R0 : H0 + R0 + count, :, 0:128] = ahead[AHEAD[a] : AHEAD[a] + count]
        for c in range(GROUPS):
            left, right = from_left[a, c], from_right[a, c]
            for k in range(8):
                if 8 * c + k < N0:
                    both = jnp.where(lane // 16 == k, left, right)
                    ext[a, 8 * c + k, :, 128:256] = roll(both, -16 * k - 16, 1)

    def cut(value, *kinds):
        for kind in kinds:
            value = jnp.where(kind, value, 0.0)
        return value

    fx[0] = cut(ext[1, 0], ext[0, 0] == 0.0, ext[0, 1] == 0.0)

    def operator0(p):
        label, label_up, label_down = ext[0, p], ext[0, p + 1], ext[0, p - 1]
        cx, cx_back, cy, cz = ext[1, p], ext[1, p - 1], ext[2, p], ext[3, p]
        cy_back, cz_back = roll(cy, 1, 1), behind_z(cz)
        y_up, y_down = roll(label, -1, 1), roll(label, 1, 1)
        z_up, z_down = ahead_z(label), behind_z(label)
        free = label == 0.0
        extra, rhs, diag = LEAK, 0.0, LEAK
        edges = (
            (cx, label_up), (cx_back, label_down), (cy, y_up), (cy_back, y_down), (cz, z_up), (cz_back, z_down),
        )
        for edge, across in edges:
            extra = extra + jnp.where(across == 0.0, 0.0, edge)
            rhs = rhs + jnp.where(across == 1.0, edge, 0.0)
            diag = diag + edge
        rhs, diag = cut(rhs, free), cut(diag, free)
        scale = scale_of(diag)
        fx[p] = cut(cx, free, label_up == 0.0)
        fy[p] = cut(cy, free, y_up == 0.0)
        fz[p] = cut(cz, free, z_up == 0.0)
        d[p], g[p], f[p] = diag, scale, rhs
        va[p] = scale * rhs
        t[p] = cut(extra, free)

    planes(1, N0 - 1, operator0, 4)
    src, dst = va, vb
    for s in range(NU - 1):
        sweep(src, dst, f, g, fx, fy, fz, 2 + s, N0 - 2 - s)
        src, dst = dst, src

    part = pl.ds(H0 - 4, 24)
    pairs = [(ref.at[part], keep0.at[i]) for i, ref in enumerate((src, f, g, fx, fy, fz))]
    copies = fetch(pairs, sems)

    def to1(row):
        return jnp.where(row < 192, row // 2, row // 2 - 128) + 32

    pick, pick_odd = selection(256, 128, to1), selection(256, 128, to1, True)

    def coarsen1(q):
        p = 2 * q + 1
        t1[0, q] = fx[p + 1]
        t1[1, q] = fy[p] + fy[p + 1]
        t1[2, q] = fz[p] + fz[p + 1]
        t1[3, q] = t[p] + t[p + 1]

    planes(0, N1, coarsen1, 4)
    for a in range(4):
        for c in range(0, N1, 4):
            value = t1[a, c : c + 4].reshape(4 * NZ, 256)
            ops1[a, c : c + 4] = dot(value, pick_odd if a == 1 else pick).reshape(4, NZ, 128)

    residual(src, dst, f, d, fx, fy, fz, H0 - 8, H0 + R0 + 8)
    f1[0:2] = jnp.zeros((2, NZ, 128), F32)
    f1[N1 - 2 : N1] = jnp.zeros((2, NZ, 128), F32)
    for c in range(2, N1 - 2, 4):
        value = jnp.stack([dst[2 * q + 1] + dst[2 * q + 2] for q in range(c, c + 4)])
        f1[c : c + 4] = dot(value.reshape(4 * NZ, 256), pick).reshape(4, NZ, 128)

    x1, y1, z1, e1, g1 = (ops1.at[a] for a in range(5))
    g1[0] = jnp.where(e1[0] > 0.0, 1.0, 0.0)

    def operator1(q):
        diag = diagonal(e1[q], x1, y1, z1, q)
        d1[q] = diag
        scale = scale_of(diag)
        g1[q] = scale
        va1[q] = scale * f1[q]

    planes(1, N1, operator1)
    copies += fetch(((ops1, out_ops1), (f1, out_f1)), sems.at[pl.ds(6, 2)])
    src, dst = va1, vb1
    for s in range(NU - 1):
        sweep(src, dst, f1, g1, x1, y1, z1, 3 + s, N1 - 3 - s)
        src, dst = dst, src
    own1[...] = src[H1 : H1 + 8]
    edge_f1[0] = f1[H1 + 4]
    edge_f1[1] = f1[H1 + 8 - 5]
    residual(src, dst, f1, d1, x1, y1, z1, H1, H1 + 8)

    half, half_odd = (selection(128, 128, lambda row: row // 2, odd) for odd in (False, True))
    q = [H1 + 2 * k for k in range(4)]
    f2 = dot(jnp.concatenate([dst[i] + dst[i + 1] for i in q]), half).reshape(4, NZ, 128)
    x2[...] = dot(jnp.concatenate([x1[i + 1] for i in [H1 - 2] + q]), half).reshape(5, NZ, 128)
    y2[...] = dot(jnp.concatenate([y1[i] + y1[i + 1] for i in q]), half_odd).reshape(4, NZ, 128)
    z2[...] = dot(jnp.concatenate([z1[i] + z1[i + 1] for i in q]), half).reshape(4, NZ, 128)
    e2[...] = dot(jnp.concatenate([e1[i] + e1[i + 1] for i in q]), half).reshape(4, NZ, 128)

    def around(x, x_back, y, z, extra):
        return extra + x + x_back + y + roll(y, 1, 1) + z + behind_z(z)

    for a in range(5):
        for h in range(2):
            pair = []
            for k in (2 * h, 2 * h + 1):
                if a == 4:
                    pair.append(around(x2[k + 1], x2[k], y2[k], z2[k], e2[k]))
                else:
                    pair.append((f2, x2[1:], y2, z2)[a][k])
            both = pair[0] + roll(pair[1], 64, 1)
            to_right[2 * a + h] = both
            to_left[2 * a + h] = both

    right = left = jnp.zeros((NZ, 128), F32)
    for k in range(8):
        here = lane // 8 == k
        right = jnp.where(here, roll(own1[k], 8 * k - 88, 1), right)
        left = jnp.where(here, roll(own1[k], 8 * k - 32, 1), left)
    to_right[10] = right
    to_left[10] = left

    x3 = dot(jnp.concatenate([x2[0], x2[2], x2[4]]), half).reshape(3, NZ, 128)
    y3 = dot(jnp.concatenate([y2[0] + y2[1], y2[2] + y2[3]]), half_odd).reshape(2, NZ, 128)
    z3 = dot(jnp.concatenate([z2[0] + z2[1], z2[2] + z2[3]]), half).reshape(2, NZ, 128)
    e3 = dot(jnp.concatenate([e2[0] + e2[1], e2[2] + e2[3]]), half).reshape(2, NZ, 128)
    total = jnp.zeros((NZ, 128), F32)
    for i in range(2):
        d3 = around(x3[i + 1], x3[i], y3[i], z3[i], e3[i])
        for a, value in enumerate((x3[i + 1], y3[i], z3[i], d3)):
            spot = 32 * a + 16 * i
            total = jnp.where(lane // 16 == spot // 16, roll(value, spot - 8, 1), total)
    to_right[11] = total
    to_left[11] = total
    for copy in copies:
        copy.wait()


def join_kernel(own2, own1, edge_f1, left, right, joined2, joined1, to_right, to_left):
    lane = lanes((NZ, 128))
    low, high = lane % 64 < 16, lane % 64 >= 48
    for a in range(10):
        value = jnp.where(high, roll(right[a], 32, 1), own2[a])
        value = jnp.where(low, roll(left[a], -32, 1), value)
        joined2[a] = value
        to_right[a] = value
        to_left[a] = value
    low, high = lane // 8 == 3, lane // 8 == 12
    for k in range(8):
        value = jnp.where(low, roll(left[10], 24 - 8 * k, 1), own1[k])
        value = jnp.where(high, roll(right[10], 96 - 8 * k, 1), value)
        joined1[k] = value
        if k >= 8 - H1:
            to_right[10 + k - 8 + H1] = value
        if k < H1:
            to_left[10 + k] = value
    to_right[10 + H1] = edge_f1[1]
    to_left[10 + H1] = edge_f1[0]


def rows_of(value, odd):
    return roll(value, 64, 1) if odd else value


def middle_kernel(
    behind, own, ahead, left, right, to_right, to_left, f, fx, fy, fz, d, g, va, vb
):
    for j in range(12):
        source = (behind, own, ahead)[j // 4]
        for a, ref in enumerate((f, fx, fy, fz, d)):
            ref[j] = rows_of(source[2 * a + j % 4 // 2], j % 2)
        g[j] = scale_of(d[j])
        va[j] = g[j] * f[j]
    src, dst = va, vb
    for s in range(NU - 1):
        sweep(src, dst, f, g, fx, fy, fz, 1 + s, 11 - s)
        src, dst = dst, src
    residual(src, dst, f, d, fx, fy, fz, 4, 8)
    total = None
    for i in range(2):
        matrix = selection(
            128, 128, lambda row: jnp.where((row >= 16) & (row < 48), (row - 16) // 2 + 16 * i, -99)
        )
        part = dot(dst[4 + 2 * i] + dst[5 + 2 * i], matrix)
        total = part if total is None else total + part
    value = total[:8]
    for b in range(1, 4):
        value = value + roll(total[8 * b : 8 * b + 8], 32 * b, 1)
    to_right[0:8] = value
    to_right[8:40] = left[11]
    to_left[0:8] = value
    to_left[8:40] = right[11]


def near_kernel(count, own2, own, left2, right2, left, right, left_far, right_far, out):
    rhs = (left_far[0:8], left[0:8], own[0:8], right[0:8], right_far[0:8])
    ops = (left[8:40], left2[11], own2[11], right2[11], right[8:40])
    for c in range(count):
        for s in range(5):
            out[c, s, 0:8] = rhs[s]
            out[c, s, 8:40] = ops[s]


PAD3 = 8


def turned(parts):
    slot = lanes(parts[0].shape) // 16
    rolled = [roll(part, 16 * s, 1) for s, part in enumerate(parts)]
    results = []
    for m in range(8):
        total = jnp.zeros_like(parts[0])
        for s, value in enumerate(rolled):
            total = jnp.where(slot == (m + s) % 8, value, total)
        results.append(roll(total, -16 * m, 1))
    return results


def solve_kernel(count, gathered, out, ops3, f3, va3, vb3):
    rows = 2 * count
    lo, hi = PAD3, PAD3 + rows
    x3, y3, z3, g3 = (ops3.at[a] for a in range(4))
    for ref in (va3, vb3, x3):
        ref[0:lo] = jnp.zeros((PAD3, NZ, 128), F32)
        ref[hi : hi + PAD3] = jnp.zeros((PAD3, NZ, 128), F32)

    def unpack(i, carry):
        p = lo + 2 * i
        for m, value in enumerate(turned([gathered[i, s, 8:40] for s in range(5)])):
            ops3[m // 2, p + m % 2] = scale_of(value) if m >= 6 else value
        for m, value in enumerate(turned([gathered[i, s, 0:8] for s in range(5)])):
            part = slice(8 * (m // 2), 8 * (m // 2) + 8)
            f3[p + m % 2, part] = value
            va3[p + m % 2, part] = value * g3[p + m % 2, part]
        return carry

    lax.fori_loop(0, count, unpack, 0)

    def two(i, carry):
        sweep(va3, vb3, f3, g3, x3, y3, z3, lo, hi, 32)
        sweep(vb3, va3, f3, g3, x3, y3, z3, lo, hi, 32)
        return carry

    lax.fori_loop(0, (COARSE_SWEEPS - 1) // 2, two, 0)
    sweep(va3, vb3, f3, g3, x3, y3, z3, lo, hi, 32)
    start = lo + 2 * lax.axis_index("gx") - 4
    out[...] = vb3[pl.ds(start, 10)]


def up_kernel(
    e3, all2, in_behind, in_ahead, in_joined1, in_f1, in_ops1, in_keep0,
    out,
    f2, x2, y2, z2, d2, g2, va2, vb2, f1, va1, vb1, va0, vb0,
    wide2, behind, ahead, joined1, ops1, keep0, sems,
):
    me, ends = lax.axis_index("gx"), lax.axis_size("gx") - 1
    pairs = [(all2.at[jnp.clip(me + n - 3, 0, ends)], wide2.at[n]) for n in range(7)]
    rows1 = pl.ds(10, 1 + H1)
    pairs += [(in_behind.at[rows1], behind), (in_ahead.at[rows1], ahead), (in_joined1, joined1)]
    pairs += [(in_f1, f1), (in_ops1, ops1), (in_keep0, keep0)]
    copies = fetch(pairs, sems)
    for n in range(7):
        copies[n].wait()
        inside = (me + n - 3 >= 0) & (me + n - 3 <= ends)
        for h in range(2):
            j = 4 * n + 2 * h - 2
            if 0 <= j < 24:
                for a, ref in enumerate((f2, x2, y2, z2, d2)):
                    value = jnp.where(inside, wide2[n, 2 * a + h], 0.0)
                    ref[j] = value
                    ref[j + 1] = roll(value, 64, 1)

    def operator2(j):
        g2[j] = scale_of(d2[j])
        va2[j] = g2[j] * f2[j]

    planes(0, 24, operator2, 24)
    src, dst = va2, vb2
    for s in range(NU - 1):
        sweep(src, dst, f2, g2, x2, y2, z2, 1 + s, 23 - s, 32)
        src, dst = dst, src
    col = lax.broadcasted_iota(jnp.int32, (128, 128), 1)
    row = lax.broadcasted_iota(jnp.int32, (128, 128), 0)
    spread = ((row == (col + 128 - 16) // 2 - 64 + 32) & (col < 64)).astype(F32)
    coarse = dot(e3[...].reshape(10 * NZ, 128), spread).reshape(10, NZ, 128)
    for r in range(-7, 11):
        j = r + 10
        src[j] = src[j] + jnp.where(g2[j] > 0.0, coarse[r // 2 + 4], 0.0)
    for s in range(NU):
        sweep(src, dst, f2, g2, x2, y2, z2, 4 + s, 20 - s, 32)
        src, dst = dst, src

    for copy in copies[7:12]:
        copy.wait()
    x1, y1, z1, g1 = ops1.at[0], ops1.at[1], ops1.at[2], ops1.at[4]
    f1[1] = behind[H1]
    f1[N1 - 2] = ahead[H1]
    spread = (row == (col - 32 + 128) // 2 - 64 + 16).astype(F32)
    coarse = dot(src[7:17].reshape(10 * NZ, 128), spread).reshape(10, NZ, 128)
    for q in range(N1):
        if q < H1:
            value = behind[q]
        elif q < H1 + 8:
            value = joined1[q - H1]
        else:
            value = ahead[q - H1 - 8]
        va1[q] = value + jnp.where(g1[q] > 0.0, coarse[q // 2], 0.0)
    src, dst = va1, vb1
    for s in range(NU):
        sweep(src, dst, f1, g1, x1, y1, z1, 1 + s, N1 - 1 - s, 32)
        src, dst = dst, src

    copies[12].wait()
    v0, f0, g0, x0, y0, z0 = (keep0.at[a] for a in range(6))
    col = lax.broadcasted_iota(jnp.int32, (128, 256), 1)
    row = lax.broadcasted_iota(jnp.int32, (128, 256), 0)
    spread = (row == jnp.where(col < 192, col // 2, col // 2 - 128) + 32).astype(F32)
    for c in range(0, 12, 4):
        coarse = dot(src[4 + c : 8 + c].reshape(4 * NZ, 128), spread).reshape(4, NZ, 256)
        for k in range(8):
            i = 2 * c + k
            va0[i] = v0[i] + jnp.where(g0[i] > 0.0, coarse[k // 2], 0.0)
    src, dst = va0, vb0
    for s in range(NU):
        sweep(src, dst, f0, g0, x0, y0, z0, 1 + s, 23 - s)
        src, dst = dst, src
    for b in range(4):
        value = jnp.swapaxes(src[4:20, 8 * b : 8 * b + 8, 0:128], 0, 1)
        for s in range(8):
            out[4 * s + b] = value[s]


def shift(value, axis, distance):
    count = lax.axis_size(axis)
    route = [(i, i + distance) for i in range(count) if 0 <= i + distance < count]
    return lax.ppermute(value, axis, route)


def body(labels, conduct_x, conduct_y, conduct_z):
    count = lax.axis_size("gx")
    side = (NZ, 128)
    wide = (N0, NZ, 256)
    own, to_right, to_left = call(
        stage_kernel,
        (labels, conduct_x, conduct_y, conduct_z),
        [(4, R0, *side), (4 * H0 - 2, *side), (4 * H0 - 3, *side)],
        [pltpu.VMEM(labels.shape, labels.dtype)]
        + [pltpu.VMEM(labels.shape, conduct_x.dtype)] * 3
        + [pltpu.SemaphoreType.DMA((4,))],
        limit=58,
        apart=(0, 1, 2, 3),
    )
    behind = shift(to_right, "gx", 1)
    ahead = shift(to_left, "gx", -1)
    to_right, to_left = call(edge_kernel, (own, behind, ahead), [(4, GROUPS, *side)] * 2)
    from_left = shift(to_right, "gy", 1)
    from_right = shift(to_left, "gy", -1)
    keep0, ops1, f1, own1, edge_f1, to_right2, to_left2 = call(
        down_kernel,
        (own, behind, ahead, from_left, from_right),
        [(6, 24, NZ, 256), (5, N1, *side), (N1, *side), (8, *side), (2, *side)]
        + [(12, *side)] * 2,
        [(4, N0, NZ, 256)]
        + [wide] * 9
        + [(4, N1, NZ, 256), (5, N1, *side)]
        + [(N1, *side)] * 4
        + [(5, *side)]
        + [(4, *side)] * 3
        + [pltpu.SemaphoreType.DMA((8,))],
        limit=44,
        apart_outs=(0, 1, 2),
    )
    left2, right2 = shift(to_right2, "gy", 1), shift(to_left2, "gy", -1)
    joined2, joined1, to_right, to_left = call(
        join_kernel,
        (to_right2, own1, edge_f1, left2, right2),
        [(10, *side), (8, *side)] + [(11 + H1, *side)] * 2,
    )
    all2 = lax.all_gather(joined2, "gx")
    behind, ahead = shift(to_right, "gx", 1), shift(to_left, "gx", -1)
    to_right, to_left = call(
        middle_kernel,
        (behind, joined2, ahead, left2, right2),
        [(40, 128)] * 2,
        [(12, *side)] * 8,
    )
    left, right = shift(to_right, "gy", 1), shift(to_left, "gy", -1)
    left_far, right_far = shift(left, "gy", 1), shift(right, "gy", -1)
    (rhs3,) = call(
        functools.partial(near_kernel, count),
        (to_right2, to_right, left2, right2, left, right, left_far, right_far),
        [(count, 5, 40, 128)],
    )
    rhs3 = lax.all_to_all(rhs3, "gx", 0, 0)
    rows3 = 2 * count + 2 * PAD3
    (e3,) = call(
        functools.partial(solve_kernel, count),
        (rhs3,),
        [(10, *side)],
        [(4, rows3, *side)] + [(rows3, *side)] * 3,
    )
    (out,) = call(
        up_kernel,
        (e3, all2, behind, ahead, joined1, f1, ops1, keep0),
        [(NZ, R0, 128)],
        [(24, *side)] * 8
        + [(N1, *side)] * 3
        + [(24, NZ, 256)] * 2
        + [(7, 10, *side), (1 + H1, *side), (1 + H1, *side), (8, *side)]
        + [(5, N1, *side), (6, 24, NZ, 256)]
        + [pltpu.SemaphoreType.DMA((13,))],
        limit=58,
        apart=range(1, 8),
    )
    return out


def solution(mesh):
    in_specs = (P(None, "gx", "gy"),) * 4
    out_specs = P(None, "gx", "gy")
    return jax.shard_map(body, mesh=mesh, in_specs=in_specs, out_specs=out_specs, check_vma=False)
```

```python
import functools

import jax
import jax.numpy as jnp
from jax import lax
from jax.experimental import pallas as pl
from jax.experimental.pallas import tpu as pltpu
from jax.sharding import PartitionSpec as P

NU = 4
COARSE_SWEEPS = 24
OMEGA = 0.8
LEAK = 0.005

NZ = 32
H0 = 13
R0 = 16
N0 = R0 + 2 * H0
GROUPS = (N0 + 7) // 8
H1 = 6
N1 = 8 + 2 * H1
F32 = jnp.float32


def spec():
    return pl.BlockSpec(memory_space=pltpu.VMEM)


def call(kernel, ins, outs, scratch=(), limit=24, apart=(), apart_outs=()):
    def places(count, left):
        return [pl.BlockSpec(memory_space=pl.ANY) if i in left else spec() for i in range(count)]

    return pl.pallas_call(
        kernel,
        out_shape=[jax.ShapeDtypeStruct(s, F32) for s in outs],
        in_specs=places(len(ins), apart),
        out_specs=places(len(outs), apart_outs),
        scratch_shapes=[pltpu.VMEM(s, F32) if isinstance(s, tuple) else s for s in scratch],
        compiler_params=pltpu.CompilerParams(vmem_limit_bytes=limit * 1024 * 1024),
    )(*ins)


def lanes(shape):
    return lax.broadcasted_iota(jnp.int32, shape, len(shape) - 1)


def roll(value, shift, axis):
    size = value.shape[axis]
    shift = shift % size
    return value if shift == 0 else pltpu.roll(value, shift, axis)


def planes(lo, hi, body, step=16):
    whole = (hi - lo) // step

    def chunk(i, carry):
        for k in range(step):
            body(lo + i * step + k)
        return carry

    if whole == 1:
        chunk(0, 0)
    elif whole:
        lax.fori_loop(0, whole, chunk, 0)
    for p in range(lo + whole * step, hi):
        body(p)


def ahead_z(v):
    return jnp.concatenate([v[8:], roll(v[:8], -1, 0)], 0)


def behind_z(v):
    return jnp.concatenate([roll(v[24:], 1, 0), v[:24]], 0)


def neighbours(v_ref, fx, fy, fz, p):
    v = v_ref[p]
    s = fx[p] * v_ref[p + 1] + fx[p - 1] * v_ref[p - 1]
    cy = fy[p]
    s = s + cy * roll(v, -1, 1) + roll(cy * v, 1, 1)
    cz = fz[p]
    s = s + cz * ahead_z(v) + behind_z(cz * v)
    return v, s


def sweep(src, dst, f, g, fx, fy, fz, lo, hi, step=16):
    def body(p):
        v, s = neighbours(src, fx, fy, fz, p)
        dst[p] = (1.0 - OMEGA) * v + g[p] * (f[p] + s)

    planes(lo, hi, body, step)


def residual(src, dst, f, d, fx, fy, fz, lo, hi, step=16):
    def body(p):
        v, s = neighbours(src, fx, fy, fz, p)
        dst[p] = f[p] - d[p] * v + s

    planes(lo, hi, body, step)


def diagonal(extra, fx, fy, fz, p):
    cy, cz = fy[p], fz[p]
    return extra + fx[p] + fx[p - 1] + cy + roll(cy, 1, 1) + cz + behind_z(cz)


def scale_of(d):
    free = d > 0.0
    return jnp.where(free, OMEGA / jnp.where(free, d, 1.0), 0.0)


def selection(rows, cols, target, odd=False):
    row = lax.broadcasted_iota(jnp.int32, (rows, cols), 0)
    col = lax.broadcasted_iota(jnp.int32, (rows, cols), 1)
    hit = col == target(row)
    if odd:
        hit = hit & (row % 2 == 1)
    return hit.astype(F32)


def dot(a, matrix):
    matrix = matrix.astype(jnp.bfloat16)
    total = None
    for _ in range(3):
        part = a.astype(jnp.bfloat16)
        a = a - part.astype(F32)
        product = jnp.dot(part, matrix, preferred_element_type=F32)
        total = product if total is None else total + product
    return total


BEHIND = (0, H0, 2 * H0, 3 * H0 - 1)
AHEAD = (0, H0, 2 * H0 - 1, 3 * H0 - 2)


def fetch(pairs, sems):
    copies = [pltpu.make_async_copy(src, dst, sems.at[i]) for i, (src, dst) in enumerate(pairs)]
    for copy in copies:
        copy.start()
    return copies


def stage_kernel(
    in0, in1, in2, in3, own, to_right, to_left, labels, cond_x, cond_y, cond_z, sems
):
    copies = fetch(((in0, labels), (in1, cond_x), (in2, cond_y), (in3, cond_z)), sems)
    last_x = lax.axis_index("gx") == lax.axis_size("gx") - 1
    last_y = lax.axis_index("gy") == lax.axis_size("gy") - 1
    shape = (R0, 8, 128)
    row = lax.broadcasted_iota(jnp.int32, shape, 0)
    for a, ref in enumerate((labels, cond_x, cond_y, cond_z)):
        copies[a].wait()
        for b in range(4):
            value = jnp.stack([ref[4 * s + b].astype(F32) for s in range(8)])
            value = jnp.swapaxes(value, 0, 1)
            if a == 1:
                value = jnp.where(last_x & (row == R0 - 1), 0.0, value)
            if a == 2:
                value = jnp.where(last_y & (lanes(shape) == 127), 0.0, value)
            if a == 3 and b == 3:
                last = lax.broadcasted_iota(jnp.int32, shape, 1) == 7
                value = jnp.where(last, 0.0, value)
            part = slice(8 * b, 8 * b + 8)
            own[a, :, part] = value
            first, count = R0 - H0 + (a > 1), H0 - (a > 1)
            to_right[BEHIND[a] : BEHIND[a] + count, part] = value[first:]
            count = H0 - (a > 0)
            to_left[AHEAD[a] : AHEAD[a] + count, part] = value[:count]


def edge_kernel(own, behind, ahead, to_right, to_left):
    lane = lanes((NZ, 128))

    def plane(a, p):
        if p < H0:
            return behind[BEHIND[a] + p - (a > 1)] if p or a < 2 else None
        if p < H0 + R0:
            return own[a, p - H0]
        return ahead[AHEAD[a] + p - H0 - R0] if p < N0 - 1 or a == 0 else None

    for a in range(4):
        for c in range(GROUPS):
            right = left = jnp.zeros((NZ, 128), F32)
            for k in range(8):
                value = plane(a, 8 * c + k) if 8 * c + k < N0 else None
                if value is not None:
                    value = roll(value, 16 * k + 16, 1)
                    right = jnp.where(lane // 16 == k, value, right)
                    left = jnp.where(lane // 16 == (k + 1) % 8, value, left)
            to_right[a, c] = right
            to_left[a, c] = left


def down_kernel(
    own, behind, ahead, from_left, from_right,
    keep0, out_ops1, out_f1, own1, edge_f1, to_right, to_left, own3,
    ext, fx, fy, fz, d, g, f, va, vb, t, t1, ops1, d1, f1, va1, vb1, x2, y2, z2, e2, sems,
):
    lane = lanes((NZ, 128))
    for a in range(4):
        skip, count = int(a > 1), H0 - (a > 0)
        ext[a, skip:H0, :, 0:128] = behind[BEHIND[a] : BEHIND[a] + H0 - skip]
        ext[a, H0 : H0 + R0, :, 0:128] = own[a]
        ext[a, H0 + R0 : H0 + R0 + count, :, 0:128] = ahead[AHEAD[a] : AHEAD[a] + count]
        for c in range(GROUPS):
            left, right = from_left[a, c], from_right[a, c]
            for k in range(8):
                if 8 * c + k < N0:
                    both = jnp.where(lane // 16 == k, left, right)
                    ext[a, 8 * c + k, :, 128:256] = roll(both, -16 * k - 16, 1)

    def cut(value, *kinds):
        for kind in kinds:
            value = jnp.where(kind, value, 0.0)
        return value

    fx[0] = cut(ext[1, 0], ext[0, 0] == 0.0, ext[0, 1] == 0.0)

    def operator0(p):
        label, label_up, label_down = ext[0, p], ext[0, p + 1], ext[0, p - 1]
        cx, cx_back, cy, cz = ext[1, p], ext[1, p - 1], ext[2, p], ext[3, p]
        cy_back, cz_back = roll(cy, 1, 1), behind_z(cz)
        y_up, y_down = roll(label, -1, 1), roll(label, 1, 1)
        z_up, z_down = ahead_z(label), behind_z(label)
        free = label == 0.0
        extra, rhs, diag = LEAK, 0.0, LEAK
        edges = (
            (cx, label_up), (cx_back, label_down), (cy, y_up), (cy_back, y_down), (cz, z_up), (cz_back, z_down),
        )
        for edge, across in edges:
            extra = extra + jnp.where(across == 0.0, 0.0, edge)
            rhs = rhs + jnp.where(across == 1.0, edge, 0.0)
            diag = diag + edge
        rhs, diag = cut(rhs, free), cut(diag, free)
        scale = scale_of(diag)
        fx[p] = cut(cx, free, label_up == 0.0)
        fy[p] = cut(cy, free, y_up == 0.0)
        fz[p] = cut(cz, free, z_up == 0.0)
        d[p], g[p], f[p] = diag, scale, rhs
        va[p] = scale * rhs
        t[p] = cut(extra, free)

    planes(1, N0 - 1, operator0, 4)
    src, dst = va, vb
    for s in range(NU - 1):
        sweep(src, dst, f, g, fx, fy, fz, 2 + s, N0 - 2 - s)
        src, dst = dst, src

    part = pl.ds(H0 - 4, 24)
    pairs = [(ref.at[part], keep0.at[i]) for i, ref in enumerate((src, f, g, fx, fy, fz))]
    copies = fetch(pairs, sems)

    def to1(row):
        return jnp.where(row < 192, row // 2, row // 2 - 128) + 32

    pick, pick_odd = selection(256, 128, to1), selection(256, 128, to1, True)

    def coarsen1(q):
        p = 2 * q + 1
        t1[0, q] = fx[p + 1]
        t1[1, q] = fy[p] + fy[p + 1]
        t1[2, q] = fz[p] + fz[p + 1]
        t1[3, q] = t[p] + t[p + 1]

    planes(0, N1, coarsen1, 4)
    for a in range(4):
        for c in range(0, N1, 4):
            value = t1[a, c : c + 4].reshape(4 * NZ, 256)
            ops1[a, c : c + 4] = dot(value, pick_odd if a == 1 else pick).reshape(4, NZ, 128)

    residual(src, dst, f, d, fx, fy, fz, H0 - 8, H0 + R0 + 8)
    f1[0:2] = jnp.zeros((2, NZ, 128), F32)
    f1[N1 - 2 : N1] = jnp.zeros((2, NZ, 128), F32)
    for c in range(2, N1 - 2, 4):
        value = jnp.stack([dst[2 * q + 1] + dst[2 * q + 2] for q in range(c, c + 4)])
        f1[c : c + 4] = dot(value.reshape(4 * NZ, 256), pick).reshape(4, NZ, 128)

    x1, y1, z1, e1, g1 = (ops1.at[a] for a in range(5))
    g1[0] = jnp.where(e1[0] > 0.0, 1.0, 0.0)

    def operator1(q):
        diag = diagonal(e1[q], x1, y1, z1, q)
        d1[q] = diag
        scale = scale_of(diag)
        g1[q] = scale
        va1[q] = scale * f1[q]

    planes(1, N1, operator1)
    copies += fetch(((ops1, out_ops1), (f1, out_f1)), sems.at[pl.ds(6, 2)])
    src, dst = va1, vb1
    for s in range(NU - 1):
        sweep(src, dst, f1, g1, x1, y1, z1, 3 + s, N1 - 3 - s)
        src, dst = dst, src
    own1[...] = src[H1 : H1 + 8]
    edge_f1[0] = f1[H1 + 4]
    edge_f1[1] = f1[H1 + 8 - 5]
    residual(src, dst, f1, d1, x1, y1, z1, H1, H1 + 8)

    half, half_odd = (selection(128, 128, lambda row: row // 2, odd) for odd in (False, True))
    q = [H1 + 2 * k for k in range(4)]
    f2 = dot(jnp.concatenate([dst[i] + dst[i + 1] for i in q]), half).reshape(4, NZ, 128)
    x2[...] = dot(jnp.concatenate([x1[i + 1] for i in [H1 - 2] + q]), half).reshape(5, NZ, 128)
    y2[...] = dot(jnp.concatenate([y1[i] + y1[i + 1] for i in q]), half_odd).reshape(4, NZ, 128)
    z2[...] = dot(jnp.concatenate([z1[i] + z1[i + 1] for i in q]), half).reshape(4, NZ, 128)
    e2[...] = dot(jnp.concatenate([e1[i] + e1[i + 1] for i in q]), half).reshape(4, NZ, 128)

    def around(x, x_back, y, z, extra):
        return extra + x + x_back + y + roll(y, 1, 1) + z + behind_z(z)

    for a in range(5):
        for h in range(2):
            pair = []
            for k in (2 * h, 2 * h + 1):
                if a == 4:
                    pair.append(around(x2[k + 1], x2[k], y2[k], z2[k], e2[k]))
                else:
                    pair.append((f2, x2[1:], y2, z2)[a][k])
            both = pair[0] + roll(pair[1], 64, 1)
            to_right[2 * a + h] = both
            to_left[2 * a + h] = both

    right = left = jnp.zeros((NZ, 128), F32)
    for k in range(8):
        here = lane // 8 == k
        right = jnp.where(here, roll(own1[k], 8 * k - 88, 1), right)
        left = jnp.where(here, roll(own1[k], 8 * k - 32, 1), left)
    to_right[10] = right
    to_left[10] = left

    x3 = dot(jnp.concatenate([x2[0], x2[2], x2[4]]), half).reshape(3, NZ, 128)
    y3 = dot(jnp.concatenate([y2[0] + y2[1], y2[2] + y2[3]]), half_odd).reshape(2, NZ, 128)
    z3 = dot(jnp.concatenate([z2[0] + z2[1], z2[2] + z2[3]]), half).reshape(2, NZ, 128)
    e3 = dot(jnp.concatenate([e2[0] + e2[1], e2[2] + e2[3]]), half).reshape(2, NZ, 128)
    total = jnp.zeros((NZ, 128), F32)
    for i in range(2):
        d3 = around(x3[i + 1], x3[i], y3[i], z3[i], e3[i])
        for a, value in enumerate((x3[i + 1], y3[i], z3[i], d3)):
            spot = 32 * a + 16 * i
            total = jnp.where(lane // 16 == spot // 16, roll(value, spot - 8, 1), total)
    own3[...] = total
    for copy in copies:
        copy.wait()


def join_kernel(own2, own1, edge_f1, left, right, joined2, joined1, to_right, to_left):
    lane = lanes((NZ, 128))
    low, high = lane % 64 < 16, lane % 64 >= 48
    for a in range(10):
        value = jnp.where(high, roll(right[a], 32, 1), own2[a])
        value = jnp.where(low, roll(left[a], -32, 1), value)
        joined2[a] = value
        to_right[a] = value
        to_left[a] = value
    low, high = lane // 8 == 3, lane // 8 == 12
    for k in range(8):
        value = jnp.where(low, roll(left[10], 24 - 8 * k, 1), own1[k])
        value = jnp.where(high, roll(right[10], 96 - 8 * k, 1), value)
        joined1[k] = value
        if k >= 8 - H1:
            to_right[10 + k - 8 + H1] = value
        if k < H1:
            to_left[10 + k] = value
    to_right[10 + H1] = edge_f1[1]
    to_left[10 + H1] = edge_f1[0]


def rows_of(value, odd):
    return roll(value, 64, 1) if odd else value


def middle_kernel(
    count, behind, own, ahead, ops3, message, further, nearer, f, fx, fy, fz, d, g, va, vb
):
    for j in range(12):
        source = (behind, own, ahead)[j // 4]
        for a, ref in enumerate((f, fx, fy, fz, d)):
            ref[j] = rows_of(source[2 * a + j % 4 // 2], j % 2)
        g[j] = scale_of(d[j])
        va[j] = g[j] * f[j]
    src, dst = va, vb
    for s in range(NU - 1):
        sweep(src, dst, f, g, fx, fy, fz, 1 + s, 11 - s)
        src, dst = dst, src
    residual(src, dst, f, d, fx, fy, fz, 4, 8)
    total = None
    for i in range(2):
        matrix = selection(
            128, 128, lambda row: jnp.where((row >= 16) & (row < 48), (row - 16) // 2 + 16 * i, -99)
        )
        part = dot(dst[4 + 2 * i] + dst[5 + 2 * i], matrix)
        total = part if total is None else total + part
    value = total[:8]
    for b in range(1, 4):
        value = value + roll(total[8 * b : 8 * b + 8], 32 * b, 1)
    message[count, 0:8] = value
    message[count, 8:] = jnp.zeros((NZ - 8, 128), F32)
    for i in range(count):
        message[i] = ops3[i]
    further[...] = behind[0:10]
    nearer[...] = ahead[0:10]


def near_kernel(count, own, left, right, left_far, right_far, behind2, ahead2, out, further, nearer):
    rhs = [ref[count, 0:8] for ref in (left_far, left, own, right, right_far)]
    for c in range(count):
        for s in range(5):
            out[c, s] = rhs[s]
    for a in range(5):
        further[a] = behind2[2 * a + 1]
        nearer[a] = ahead2[2 * a]


PAD3 = 8


def turned(parts):
    slot = lanes(parts[0].shape) // 16
    rolled = [roll(part, 16 * s, 1) for s, part in enumerate(parts)]
    results = []
    for m in range(8):
        total = jnp.zeros_like(parts[0])
        for s, value in enumerate(rolled):
            total = jnp.where(slot == (m + s) % 8, value, total)
        results.append(roll(total, -16 * m, 1))
    return results


def solve_kernel(
    count, gathered, own, left, right, left_far, right_far, out, ops3, f3, va3, vb3
):
    rows = 2 * count
    lo, hi = PAD3, PAD3 + rows
    x3, y3, z3, g3 = (ops3.at[a] for a in range(4))
    for ref in (va3, vb3, x3):
        ref[0:lo] = jnp.zeros((PAD3, NZ, 128), F32)
        ref[hi : hi + PAD3] = jnp.zeros((PAD3, NZ, 128), F32)

    def unpack(i, carry):
        p = lo + 2 * i
        for m, value in enumerate(turned([ref[i] for ref in (left_far, left, own, right, right_far)])):
            ops3[m // 2, p + m % 2] = scale_of(value) if m >= 6 else value
        for m, value in enumerate(turned([gathered[i, s] for s in range(5)])):
            part = slice(8 * (m // 2), 8 * (m // 2) + 8)
            f3[p + m % 2, part] = value
            va3[p + m % 2, part] = value * g3[p + m % 2, part]
        return carry

    lax.fori_loop(0, count, unpack, 0)

    def two(i, carry):
        sweep(va3, vb3, f3, g3, x3, y3, z3, lo, hi, 32)
        sweep(vb3, va3, f3, g3, x3, y3, z3, lo, hi, 32)
        return carry

    lax.fori_loop(0, (COARSE_SWEEPS - 1) // 2, two, 0)
    sweep(va3, vb3, f3, g3, x3, y3, z3, lo, hi, 32)
    start = lo + 2 * lax.axis_index("gx") - 4
    out[...] = vb3[pl.ds(start, 10)]


def up_kernel(
    e3, in_behind3, in_behind2, in_behind, in_own, in_ahead, in_ahead2, in_ahead3,
    in_joined1, in_f1, in_ops1, in_keep0,
    out,
    f2, x2, y2, z2, d2, g2, va2, vb2, f1, va1, vb1, va0, vb0,
    behind3, behind2, behind, own, ahead, ahead2, ahead3, joined1, ops1, keep0, sems,
):
    pairs = [
        (in_behind3, behind3), (in_behind2, behind2), (in_behind, behind), (in_own, own),
        (in_ahead, ahead), (in_ahead2, ahead2), (in_ahead3, ahead3),
        (in_joined1, joined1), (in_f1, f1), (in_ops1, ops1), (in_keep0, keep0),
    ]
    copies = fetch(pairs, sems)
    sources = [(behind3, None)]
    sources += [(ref, h) for ref in (behind2, behind, own, ahead, ahead2) for h in range(2)]
    sources += [(ahead3, None)]
    for n, (source, h) in enumerate(sources):
        if n % 2 or n == 0:
            copies[(n + 1) // 2].wait()
        for a, ref in enumerate((f2, x2, y2, z2, d2)):
            value = source[a if h is None else 2 * a + h]
            ref[2 * n] = value
            ref[2 * n + 1] = roll(value, 64, 1)

    def operator2(j):
        g2[j] = scale_of(d2[j])
        va2[j] = g2[j] * f2[j]

    planes(0, 24, operator2, 24)
    src, dst = va2, vb2
    for s in range(NU - 1):
        sweep(src, dst, f2, g2, x2, y2, z2, 1 + s, 23 - s, 32)
        src, dst = dst, src
    col = lax.broadcasted_iota(jnp.int32, (128, 128), 1)
    row = lax.broadcasted_iota(jnp.int32, (128, 128), 0)
    spread = ((row == (col + 128 - 16) // 2 - 64 + 32) & (col < 64)).astype(F32)
    coarse = dot(e3[...].reshape(10 * NZ, 128), spread).reshape(10, NZ, 128)
    for r in range(-7, 11):
        j = r + 10
        src[j] = src[j] + jnp.where(g2[j] > 0.0, coarse[r // 2 + 4], 0.0)
    for s in range(NU):
        sweep(src, dst, f2, g2, x2, y2, z2, 4 + s, 20 - s, 32)
        src, dst = dst, src

    for copy in copies[7:10]:
        copy.wait()
    x1, y1, z1, g1 = ops1.at[0], ops1.at[1], ops1.at[2], ops1.at[4]
    f1[1] = behind[10 + H1]
    f1[N1 - 2] = ahead[10 + H1]
    spread = (row == (col - 32 + 128) // 2 - 64 + 16).astype(F32)
    coarse = dot(src[7:17].reshape(10 * NZ, 128), spread).reshape(10, NZ, 128)
    for q in range(N1):
        if q < H1:
            value = behind[10 + q]
        elif q < H1 + 8:
            value = joined1[q - H1]
        else:
            value = ahead[10 + q - H1 - 8]
        va1[q] = value + jnp.where(g1[q] > 0.0, coarse[q // 2], 0.0)
    src, dst = va1, vb1
    for s in range(NU):
        sweep(src, dst, f1, g1, x1, y1, z1, 1 + s, N1 - 1 - s, 32)
        src, dst = dst, src

    copies[10].wait()
    v0, f0, g0, x0, y0, z0 = (keep0.at[a] for a in range(6))
    col = lax.broadcasted_iota(jnp.int32, (128, 256), 1)
    row = lax.broadcasted_iota(jnp.int32, (128, 256), 0)
    spread = (row == jnp.where(col < 192, col // 2, col // 2 - 128) + 32).astype(F32)
    for c in range(0, 12, 4):
        coarse = dot(src[4 + c : 8 + c].reshape(4 * NZ, 128), spread).reshape(4, NZ, 256)
        for k in range(8):
            i = 2 * c + k
            va0[i] = v0[i] + jnp.where(g0[i] > 0.0, coarse[k // 2], 0.0)
    src, dst = va0, vb0
    for s in range(NU):
        sweep(src, dst, f0, g0, x0, y0, z0, 1 + s, 23 - s)
        src, dst = dst, src
    for b in range(4):
        value = jnp.swapaxes(src[4:20, 8 * b : 8 * b + 8, 0:128], 0, 1)
        for s in range(8):
            out[4 * s + b] = value[s]


def shift(value, axis, distance):
    count = lax.axis_size(axis)
    route = [(i, i + distance) for i in range(count) if 0 <= i + distance < count]
    return lax.ppermute(value, axis, route)


def body(labels, conduct_x, conduct_y, conduct_z):
    count = lax.axis_size("gx")
    side = (NZ, 128)
    wide = (N0, NZ, 256)
    own, to_right, to_left = call(
        stage_kernel,
        (labels, conduct_x, conduct_y, conduct_z),
        [(4, R0, *side), (4 * H0 - 2, *side), (4 * H0 - 3, *side)],
        [pltpu.VMEM(labels.shape, labels.dtype)]
        + [pltpu.VMEM(labels.shape, conduct_x.dtype)] * 3
        + [pltpu.SemaphoreType.DMA((4,))],
        limit=58,
        apart=(0, 1, 2, 3),
    )
    behind = shift(to_right, "gx", 1)
    ahead = shift(to_left, "gx", -1)
    to_right, to_left = call(edge_kernel, (own, behind, ahead), [(4, GROUPS, *side)] * 2)
    from_left = shift(to_right, "gy", 1)
    from_right = shift(to_left, "gy", -1)
    keep0, ops1, f1, own1, edge_f1, to_right2, to_left2, own3 = call(
        down_kernel,
        (own, behind, ahead, from_left, from_right),
        [(6, 24, NZ, 256), (5, N1, *side), (N1, *side), (8, *side), (2, *side)]
        + [(11, *side)] * 2
        + [side],
        [(4, N0, NZ, 256)]
        + [wide] * 9
        + [(4, N1, NZ, 256), (5, N1, *side)]
        + [(N1, *side)] * 4
        + [(5, *side)]
        + [(4, *side)] * 3
        + [pltpu.SemaphoreType.DMA((8,))],
        limit=44,
        apart_outs=(0, 1, 2),
    )
    all3 = lax.all_gather(own3, "gx")
    left, right = shift(to_right2, "gy", 1), shift(to_left2, "gy", -1)
    joined2, joined1, to_right, to_left = call(
        join_kernel,
        (to_right2, own1, edge_f1, left, right),
        [(10, *side), (8, *side)] + [(11 + H1, *side)] * 2,
    )
    behind, ahead = shift(to_right, "gx", 1), shift(to_left, "gx", -1)
    message, further, nearer = call(
        functools.partial(middle_kernel, count),
        (behind, joined2, ahead, all3),
        [(count + 1, *side)] + [(10, *side)] * 2,
        [(12, *side)] * 8,
    )
    left, right = shift(message, "gy", 1), shift(message, "gy", -1)
    behind2, ahead2 = shift(further, "gx", 1), shift(nearer, "gx", -1)
    left_far, right_far = shift(left, "gy", 1), shift(right, "gy", -1)
    near = (message, left, right, left_far, right_far)
    rhs3, further, nearer = call(
        functools.partial(near_kernel, count),
        (*near, behind2, ahead2),
        [(count, 5, 8, 128), (5, *side), (5, *side)],
    )
    rhs3 = lax.all_to_all(rhs3, "gx", 0, 0)
    behind3, ahead3 = shift(further, "gx", 1), shift(nearer, "gx", -1)
    rows3 = 2 * count + 2 * PAD3
    (e3,) = call(
        functools.partial(solve_kernel, count),
        (rhs3, *near),
        [(10, *side)],
        [(4, rows3, *side)] + [(rows3, *side)] * 3,
    )
    (out,) = call(
        up_kernel,
        (e3, behind3, behind2, behind, joined2, ahead, ahead2, ahead3, joined1, f1, ops1, keep0),
        [(NZ, R0, 128)],
        [(24, *side)] * 8
        + [(N1, *side)] * 3
        + [(24, NZ, 256)] * 2
        + [(5, *side), (10, *side), (11 + H1, *side), (10, *side)]
        + [(11 + H1, *side), (10, *side), (5, *side), (8, *side)]
        + [(5, N1, *side), (6, 24, NZ, 256)]
        + [pltpu.SemaphoreType.DMA((11,))],
        limit=58,
        apart=range(1, 12),
    )
    return out


def solution(mesh):
    in_specs = (P(None, "gx", "gy"),) * 4
    out_specs = P(None, "gx", "gy")
    return jax.shard_map(body, mesh=mesh, in_specs=in_specs, out_specs=out_specs, check_vma=False)
```

```python
import functools

import jax
import jax.numpy as jnp
from jax import lax
from jax.experimental import pallas as pl
from jax.experimental.pallas import tpu as pltpu
from jax.sharding import PartitionSpec as P

NU = 4
COARSE_SWEEPS = 24
OMEGA = 0.8
LEAK = 0.005

NZ = 32
H0 = 13
R0 = 16
N0 = R0 + 2 * H0
GROUPS = (N0 + 7) // 8
H1 = 6
N1 = 8 + 2 * H1
F32 = jnp.float32


def spec():
    return pl.BlockSpec(memory_space=pltpu.VMEM)


def call(kernel, ins, outs, scratch=(), limit=10, apart=(), apart_outs=()):
    def places(count, left):
        return [pl.BlockSpec(memory_space=pl.ANY) if i in left else spec() for i in range(count)]

    return pl.pallas_call(
        kernel,
        out_shape=[jax.ShapeDtypeStruct(s, F32) for s in outs],
        in_specs=places(len(ins), apart),
        out_specs=places(len(outs), apart_outs),
        scratch_shapes=[pltpu.VMEM(s, F32) if isinstance(s, tuple) else s for s in scratch],
        compiler_params=pltpu.CompilerParams(vmem_limit_bytes=limit * 1024 * 1024),
    )(*ins)


def lanes(shape):
    return lax.broadcasted_iota(jnp.int32, shape, len(shape) - 1)


def roll(value, shift, axis):
    size = value.shape[axis]
    shift = shift % size
    return value if shift == 0 else pltpu.roll(value, shift, axis)


def planes(lo, hi, body, step=16):
    whole = (hi - lo) // step

    def chunk(i, carry):
        for k in range(step):
            body(lo + i * step + k)
        return carry

    if whole == 1:
        chunk(0, 0)
    elif whole:
        lax.fori_loop(0, whole, chunk, 0)
    for p in range(lo + whole * step, hi):
        body(p)


def ahead_z(v):
    return jnp.concatenate([v[8:], roll(v[:8], -1, 0)], 0)


def behind_z(v):
    return jnp.concatenate([roll(v[24:], 1, 0), v[:24]], 0)


def neighbours(v_ref, fx, fy, fz, p):
    v = v_ref[p]
    s = fx[p] * v_ref[p + 1] + fx[p - 1] * v_ref[p - 1]
    cy = fy[p]
    s = s + cy * roll(v, -1, 1) + roll(cy * v, 1, 1)
    cz = fz[p]
    s = s + cz * ahead_z(v) + behind_z(cz * v)
    return v, s


def sweep(src, dst, f, g, fx, fy, fz, lo, hi, step=16):
    def body(p):
        v, s = neighbours(src, fx, fy, fz, p)
        dst[p] = (1.0 - OMEGA) * v + g[p] * (f[p] + s)

    planes(lo, hi, body, step)


def residual(src, dst, f, d, fx, fy, fz, lo, hi, step=16):
    def body(p):
        v, s = neighbours(src, fx, fy, fz, p)
        dst[p] = f[p] - d[p] * v + s

    planes(lo, hi, body, step)


def diagonal(extra, fx, fy, fz, p):
    cy, cz = fy[p], fz[p]
    return extra + fx[p] + fx[p - 1] + cy + roll(cy, 1, 1) + cz + behind_z(cz)


def scale_of(d):
    free = d > 0.0
    return jnp.where(free, OMEGA / jnp.where(free, d, 1.0), 0.0)


def selection(rows, cols, target, odd=False):
    row = lax.broadcasted_iota(jnp.int32, (rows, cols), 0)
    col = lax.broadcasted_iota(jnp.int32, (rows, cols), 1)
    hit = col == target(row)
    if odd:
        hit = hit & (row % 2 == 1)
    return hit.astype(F32)


def dot(a, matrix):
    matrix = matrix.astype(jnp.bfloat16)
    total = None
    for _ in range(3):
        part = a.astype(jnp.bfloat16)
        a = a - part.astype(F32)
        product = jnp.dot(part, matrix, preferred_element_type=F32)
        total = product if total is None else total + product
    return total


BEHIND = (0, H0, 2 * H0, 3 * H0 - 1)
AHEAD = (0, H0, 2 * H0 - 1, 3 * H0 - 2)


def fetch(pairs, sems):
    copies = [pltpu.make_async_copy(src, dst, sems.at[i]) for i, (src, dst) in enumerate(pairs)]
    for copy in copies:
        copy.start()
    return copies


def stage_kernel(labels, cond_x, cond_y, cond_z, own, to_right, to_left):
    last_x = lax.axis_index("gx") == lax.axis_size("gx") - 1
    last_y = lax.axis_index("gy") == lax.axis_size("gy") - 1
    shape = (R0, 8, 128)
    row = lax.broadcasted_iota(jnp.int32, shape, 0)
    for a, ref in enumerate((labels, cond_x, cond_y, cond_z)):
        for b in range(4):
            value = jnp.stack([ref[4 * s + b].astype(F32) for s in range(8)])
            value = jnp.swapaxes(value, 0, 1)
            if a == 1:
                value = jnp.where(last_x & (row == R0 - 1), 0.0, value)
            if a == 2:
                value = jnp.where(last_y & (lanes(shape) == 127), 0.0, value)
            if a == 3 and b == 3:
                last = lax.broadcasted_iota(jnp.int32, shape, 1) == 7
                value = jnp.where(last, 0.0, value)
            part = slice(8 * b, 8 * b + 8)
            own[a, :, part] = value
            first, count = R0 - H0 + (a > 1), H0 - (a > 1)
            to_right[BEHIND[a] : BEHIND[a] + count, part] = value[first:]
            count = H0 - (a > 0)
            to_left[AHEAD[a] : AHEAD[a] + count, part] = value[:count]


def edge_kernel(own, behind, ahead, to_right, to_left):
    lane = lanes((NZ, 128))

    def plane(a, p):
        if p < H0:
            return behind[BEHIND[a] + p - (a > 1)] if p or a < 2 else None
        if p < H0 + R0:
            return own[a, p - H0]
        return ahead[AHEAD[a] + p - H0 - R0] if p < N0 - 1 or a == 0 else None

    for a in range(4):
        for c in range(GROUPS):
            right = left = jnp.zeros((NZ, 128), F32)
            for k in range(8):
                value = plane(a, 8 * c + k) if 8 * c + k < N0 else None
                if value is not None:
                    value = roll(value, 16 * k + 16, 1)
                    right = jnp.where(lane // 16 == k, value, right)
                    left = jnp.where(lane // 16 == (k + 1) % 8, value, left)
            to_right[a, c] = right
            to_left[a, c] = left


def down_kernel(
    own, behind, ahead, from_left, from_right,
    keep0, out_ops1, out_f1, own1, edge_f1, to_right, to_left, own3,
    ext, fx, fy, fz, d, g, f, va, vb, t, t1, ops1, d1, f1, va1, vb1, x2, y2, z2, e2, sems,
):
    lane = lanes((NZ, 128))
    main, pairs = pl.ds(0, 128), []
    for a in range(4):
        skip, count = int(a > 1), H0 - (a > 0)

        def place(lo, size, a=a):
            return ext.at[a, pl.ds(lo, size), :, main]

        pairs.append((behind.at[pl.ds(BEHIND[a], H0 - skip)], place(skip, H0 - skip)))
        pairs.append((own.at[a], place(H0, R0)))
        pairs.append((ahead.at[pl.ds(AHEAD[a], count)], place(H0 + R0, count)))
    copies = fetch(pairs, sems.at[pl.ds(8, 12)])
    for a in range(4):
        for c in range(GROUPS):
            left, right = from_left[a, c], from_right[a, c]
            for k in range(8):
                if 8 * c + k < N0:
                    both = jnp.where(lane // 16 == k, left, right)
                    ext[a, 8 * c + k, :, 128:256] = roll(both, -16 * k - 16, 1)
    for copy in copies:
        copy.wait()

    def cut(value, *kinds):
        for kind in kinds:
            value = jnp.where(kind, value, 0.0)
        return value

    fx[0] = cut(ext[1, 0], ext[0, 0] == 0.0, ext[0, 1] == 0.0)

    def operator0(p):
        label, label_up, label_down = ext[0, p], ext[0, p + 1], ext[0, p - 1]
        cx, cx_back, cy, cz = ext[1, p], ext[1, p - 1], ext[2, p], ext[3, p]
        cy_back, cz_back = roll(cy, 1, 1), behind_z(cz)
        y_up, y_down = roll(label, -1, 1), roll(label, 1, 1)
        z_up, z_down = ahead_z(label), behind_z(label)
        free = label == 0.0
        extra, rhs, diag = LEAK, 0.0, LEAK
        edges = (
            (cx, label_up), (cx_back, label_down), (cy, y_up), (cy_back, y_down), (cz, z_up), (cz_back, z_down),
        )
        for edge, across in edges:
            extra = extra + jnp.where(across == 0.0, 0.0, edge)
            rhs = rhs + jnp.where(across == 1.0, edge, 0.0)
            diag = diag + edge
        rhs, diag = cut(rhs, free), cut(diag, free)
        scale = scale_of(diag)
        fx[p] = cut(cx, free, label_up == 0.0)
        fy[p] = cut(cy, free, y_up == 0.0)
        fz[p] = cut(cz, free, z_up == 0.0)
        d[p], g[p], f[p] = diag, scale, rhs
        va[p] = scale * rhs
        t[p] = cut(extra, free)

    planes(1, N0 - 1, operator0, 4)
    src, dst = va, vb
    for s in range(NU - 1):
        sweep(src, dst, f, g, fx, fy, fz, 2 + s, N0 - 2 - s)
        src, dst = dst, src

    part = pl.ds(H0 - 4, 24)
    pairs = [(ref.at[part], keep0.at[i]) for i, ref in enumerate((src, f, g, fx, fy, fz))]
    copies = fetch(pairs, sems)

    def to1(row):
        return jnp.where(row < 192, row // 2, row // 2 - 128) + 32

    pick, pick_odd = selection(256, 128, to1), selection(256, 128, to1, True)

    def coarsen1(q):
        p = 2 * q + 1
        t1[0, q] = fx[p + 1]
        t1[1, q] = fy[p] + fy[p + 1]
        t1[2, q] = fz[p] + fz[p + 1]
        t1[3, q] = t[p] + t[p + 1]

    planes(0, N1, coarsen1, 4)
    for a in range(4):
        for c in range(0, N1, 4):
            value = t1[a, c : c + 4].reshape(4 * NZ, 256)
            ops1[a, c : c + 4] = dot(value, pick_odd if a == 1 else pick).reshape(4, NZ, 128)

    residual(src, dst, f, d, fx, fy, fz, H0 - 8, H0 + R0 + 8)
    f1[0:2] = jnp.zeros((2, NZ, 128), F32)
    f1[N1 - 2 : N1] = jnp.zeros((2, NZ, 128), F32)
    for c in range(2, N1 - 2, 4):
        value = jnp.stack([dst[2 * q + 1] + dst[2 * q + 2] for q in range(c, c + 4)])
        f1[c : c + 4] = dot(value.reshape(4 * NZ, 256), pick).reshape(4, NZ, 128)

    x1, y1, z1, e1, g1 = (ops1.at[a] for a in range(5))
    g1[0] = jnp.where(e1[0] > 0.0, 1.0, 0.0)

    def operator1(q):
        diag = diagonal(e1[q], x1, y1, z1, q)
        d1[q] = diag
        scale = scale_of(diag)
        g1[q] = scale
        va1[q] = scale * f1[q]

    planes(1, N1, operator1)
    copies += fetch(((ops1, out_ops1), (f1, out_f1)), sems.at[pl.ds(6, 2)])
    src, dst = va1, vb1
    for s in range(NU - 1):
        sweep(src, dst, f1, g1, x1, y1, z1, 3 + s, N1 - 3 - s)
        src, dst = dst, src
    own1[...] = src[H1 : H1 + 8]
    edge_f1[0] = f1[H1 + 4]
    edge_f1[1] = f1[H1 + 8 - 5]
    residual(src, dst, f1, d1, x1, y1, z1, H1, H1 + 8)

    half, half_odd = (selection(128, 128, lambda row: row // 2, odd) for odd in (False, True))
    q = [H1 + 2 * k for k in range(4)]
    f2 = dot(jnp.concatenate([dst[i] + dst[i + 1] for i in q]), half).reshape(4, NZ, 128)
    x2[...] = dot(jnp.concatenate([x1[i + 1] for i in [H1 - 2] + q]), half).reshape(5, NZ, 128)
    y2[...] = dot(jnp.concatenate([y1[i] + y1[i + 1] for i in q]), half_odd).reshape(4, NZ, 128)
    z2[...] = dot(jnp.concatenate([z1[i] + z1[i + 1] for i in q]), half).reshape(4, NZ, 128)
    e2[...] = dot(jnp.concatenate([e1[i] + e1[i + 1] for i in q]), half).reshape(4, NZ, 128)

    def around(x, x_back, y, z, extra):
        return extra + x + x_back + y + roll(y, 1, 1) + z + behind_z(z)

    for a in range(5):
        for h in range(2):
            pair = []
            for k in (2 * h, 2 * h + 1):
                if a == 4:
                    pair.append(around(x2[k + 1], x2[k], y2[k], z2[k], e2[k]))
                else:
                    pair.append((f2, x2[1:], y2, z2)[a][k])
            both = pair[0] + roll(pair[1], 64, 1)
            to_right[2 * a + h] = both
            to_left[2 * a + h] = both

    right = left = jnp.zeros((NZ, 128), F32)
    for k in range(8):
        here = lane // 8 == k
        right = jnp.where(here, roll(own1[k], 8 * k - 88, 1), right)
        left = jnp.where(here, roll(own1[k], 8 * k - 32, 1), left)
    to_right[10] = right
    to_left[10] = left

    x3 = dot(jnp.concatenate([x2[0], x2[2], x2[4]]), half).reshape(3, NZ, 128)
    y3 = dot(jnp.concatenate([y2[0] + y2[1], y2[2] + y2[3]]), half_odd).reshape(2, NZ, 128)
    z3 = dot(jnp.concatenate([z2[0] + z2[1], z2[2] + z2[3]]), half).reshape(2, NZ, 128)
    e3 = dot(jnp.concatenate([e2[0] + e2[1], e2[2] + e2[3]]), half).reshape(2, NZ, 128)
    total = jnp.zeros((NZ, 128), F32)
    for i in range(2):
        d3 = around(x3[i + 1], x3[i], y3[i], z3[i], e3[i])
        for a, value in enumerate((x3[i + 1], y3[i], z3[i], d3)):
            spot = 32 * a + 16 * i
            total = jnp.where(lane // 16 == spot // 16, roll(value, spot - 8, 1), total)
    for i in range(own3.shape[0]):
        own3[i] = total
    for copy in copies:
        copy.wait()


def join_kernel(own2, own1, edge_f1, left, right, joined2, joined1, to_right, to_left):
    lane = lanes((NZ, 128))
    low, high = lane % 64 < 16, lane % 64 >= 48
    for a in range(10):
        value = jnp.where(high, roll(right[a], 32, 1), own2[a])
        value = jnp.where(low, roll(left[a], -32, 1), value)
        joined2[a] = value
        to_right[a] = value
        to_left[a] = value
    low, high = lane // 8 == 3, lane // 8 == 12
    for k in range(8):
        value = jnp.where(low, roll(left[10], 24 - 8 * k, 1), own1[k])
        value = jnp.where(high, roll(right[10], 96 - 8 * k, 1), value)
        joined1[k] = value
        if k >= 8 - H1:
            to_right[10 + k - 8 + H1] = value
        if k < H1:
            to_left[10 + k] = value
    to_right[10 + H1] = edge_f1[1]
    to_left[10 + H1] = edge_f1[0]


def rows_of(value, odd):
    return roll(value, 64, 1) if odd else value


def middle_kernel(
    count, behind, own, ahead, ops3, message, further, nearer, f, fx, fy, fz, d, g, va, vb
):
    for j in range(12):
        source = (behind, own, ahead)[j // 4]
        for a, ref in enumerate((f, fx, fy, fz, d)):
            ref[j] = rows_of(source[2 * a + j % 4 // 2], j % 2)
        g[j] = scale_of(d[j])
        va[j] = g[j] * f[j]
    src, dst = va, vb
    for s in range(NU - 1):
        sweep(src, dst, f, g, fx, fy, fz, 1 + s, 11 - s)
        src, dst = dst, src
    residual(src, dst, f, d, fx, fy, fz, 4, 8)
    total = None
    for i in range(2):
        matrix = selection(
            128, 128, lambda row: jnp.where((row >= 16) & (row < 48), (row - 16) // 2 + 16 * i, -99)
        )
        part = dot(dst[4 + 2 * i] + dst[5 + 2 * i], matrix)
        total = part if total is None else total + part
    value = total[:8]
    for b in range(1, 4):
        value = value + roll(total[8 * b : 8 * b + 8], 32 * b, 1)
    message[count, 0:8] = value
    message[count, 8:] = jnp.zeros((NZ - 8, 128), F32)
    for i in range(count):
        message[i] = ops3[i]
    further[...] = behind[0:10]
    nearer[...] = ahead[0:10]


def near_kernel(count, own, left, right, left_far, right_far, behind2, ahead2, out, further, nearer):
    rhs = [ref[count, 0:8] for ref in (left_far, left, own, right, right_far)]
    for c in range(count):
        for s in range(5):
            out[c, s] = rhs[s]
    for a in range(5):
        further[a] = behind2[2 * a + 1]
        nearer[a] = ahead2[2 * a]


PAD3 = 8


def turned(parts):
    slot = lanes(parts[0].shape) // 16
    rolled = [roll(part, 16 * s, 1) for s, part in enumerate(parts)]
    results = []
    for m in range(8):
        total = jnp.zeros_like(parts[0])
        for s, value in enumerate(rolled):
            total = jnp.where(slot == (m + s) % 8, value, total)
        results.append(roll(total, -16 * m, 1))
    return results


def solve_kernel(
    count, gathered, own, left, right, left_far, right_far, out, ops3, f3, va3, vb3
):
    rows = 2 * count
    lo, hi = PAD3, PAD3 + rows
    x3, y3, z3, g3 = (ops3.at[a] for a in range(4))
    for ref in (va3, vb3, x3):
        ref[0:lo] = jnp.zeros((PAD3, NZ, 128), F32)
        ref[hi : hi + PAD3] = jnp.zeros((PAD3, NZ, 128), F32)

    def unpack(i, carry):
        p = lo + 2 * i
        for m, value in enumerate(turned([ref[i] for ref in (left_far, left, own, right, right_far)])):
            ops3[m // 2, p + m % 2] = scale_of(value) if m >= 6 else value
        for m, value in enumerate(turned([gathered[i, s] for s in range(5)])):
            part = slice(8 * (m // 2), 8 * (m // 2) + 8)
            f3[p + m % 2, part] = value
            va3[p + m % 2, part] = value * g3[p + m % 2, part]
        return carry

    lax.fori_loop(0, count, unpack, 0)

    def two(i, carry):
        sweep(va3, vb3, f3, g3, x3, y3, z3, lo, hi, 32)
        sweep(vb3, va3, f3, g3, x3, y3, z3, lo, hi, 32)
        return carry

    lax.fori_loop(0, (COARSE_SWEEPS - 1) // 2, two, 0)
    sweep(va3, vb3, f3, g3, x3, y3, z3, lo, hi, 32)
    start = lo + 2 * lax.axis_index("gx") - 4
    out[...] = vb3[pl.ds(start, 10)]


def up_kernel(
    e3, in_behind3, in_behind2, in_behind, in_own, in_ahead, in_ahead2, in_ahead3,
    in_joined1, in_f1, in_ops1, in_keep0,
    out,
    f2, x2, y2, z2, d2, g2, va2, vb2, f1, va1, vb1, va0, vb0,
    behind3, behind2, behind, own, ahead, ahead2, ahead3, joined1, ops1, keep0, sems,
):
    pairs = [
        (in_behind3, behind3), (in_behind2, behind2), (in_behind, behind), (in_own, own),
        (in_ahead, ahead), (in_ahead2, ahead2), (in_ahead3, ahead3),
        (in_joined1, joined1), (in_f1, f1), (in_ops1, ops1), (in_keep0, keep0),
    ]
    copies = fetch(pairs, sems)
    sources = [(behind3, None)]
    sources += [(ref, h) for ref in (behind2, behind, own, ahead, ahead2) for h in range(2)]
    sources += [(ahead3, None)]
    for n, (source, h) in enumerate(sources):
        if n % 2 or n == 0:
            copies[(n + 1) // 2].wait()
        for a, ref in enumerate((f2, x2, y2, z2, d2)):
            value = source[a if h is None else 2 * a + h]
            ref[2 * n] = value
            ref[2 * n + 1] = roll(value, 64, 1)

    def operator2(j):
        g2[j] = scale_of(d2[j])
        va2[j] = g2[j] * f2[j]

    planes(0, 24, operator2, 24)
    src, dst = va2, vb2
    for s in range(NU - 1):
        sweep(src, dst, f2, g2, x2, y2, z2, 1 + s, 23 - s, 32)
        src, dst = dst, src
    col = lax.broadcasted_iota(jnp.int32, (128, 128), 1)
    row = lax.broadcasted_iota(jnp.int32, (128, 128), 0)
    spread = ((row == (col + 128 - 16) // 2 - 64 + 32) & (col < 64)).astype(F32)
    coarse = dot(e3[...].reshape(10 * NZ, 128), spread).reshape(10, NZ, 128)
    for r in range(-7, 11):
        j = r + 10
        src[j] = src[j] + jnp.where(g2[j] > 0.0, coarse[r // 2 + 4], 0.0)
    for s in range(NU):
        sweep(src, dst, f2, g2, x2, y2, z2, 4 + s, 20 - s, 32)
        src, dst = dst, src

    for copy in copies[7:10]:
        copy.wait()
    x1, y1, z1, g1 = ops1.at[0], ops1.at[1], ops1.at[2], ops1.at[4]
    f1[1] = behind[10 + H1]
    f1[N1 - 2] = ahead[10 + H1]
    spread = (row == (col - 32 + 128) // 2 - 64 + 16).astype(F32)
    coarse = dot(src[7:17].reshape(10 * NZ, 128), spread).reshape(10, NZ, 128)
    for q in range(N1):
        if q < H1:
            value = behind[10 + q]
        elif q < H1 + 8:
            value = joined1[q - H1]
        else:
            value = ahead[10 + q - H1 - 8]
        va1[q] = value + jnp.where(g1[q] > 0.0, coarse[q // 2], 0.0)
    src, dst = va1, vb1
    for s in range(NU):
        sweep(src, dst, f1, g1, x1, y1, z1, 1 + s, N1 - 1 - s, 32)
        src, dst = dst, src

    copies[10].wait()
    v0, f0, g0, x0, y0, z0 = (keep0.at[a] for a in range(6))
    col = lax.broadcasted_iota(jnp.int32, (128, 256), 1)
    row = lax.broadcasted_iota(jnp.int32, (128, 256), 0)
    spread = (row == jnp.where(col < 192, col // 2, col // 2 - 128) + 32).astype(F32)
    for c in range(0, 12, 4):
        coarse = dot(src[4 + c : 8 + c].reshape(4 * NZ, 128), spread).reshape(4, NZ, 256)
        for k in range(8):
            i = 2 * c + k
            va0[i] = v0[i] + jnp.where(g0[i] > 0.0, coarse[k // 2], 0.0)
    src, dst = va0, vb0
    for s in range(NU):
        sweep(src, dst, f0, g0, x0, y0, z0, 1 + s, 23 - s)
        src, dst = dst, src
    for b in range(4):
        value = jnp.swapaxes(src[4:20, 8 * b : 8 * b + 8, 0:128], 0, 1)
        for s in range(8):
            out[4 * s + b] = value[s]


def shift(value, axis, distance):
    count = lax.axis_size(axis)
    route = [(i, i + distance) for i in range(count) if 0 <= i + distance < count]
    return lax.ppermute(value, axis, route)


def body(labels, conduct_x, conduct_y, conduct_z):
    count = lax.axis_size("gx")
    side = (NZ, 128)
    wide = (N0, NZ, 256)
    own, to_right, to_left = call(
        stage_kernel,
        (labels, conduct_x, conduct_y, conduct_z),
        [(4, R0, *side), (4 * H0 - 2, *side), (4 * H0 - 3, *side)],
    )
    behind = shift(to_right, "gx", 1)
    ahead = shift(to_left, "gx", -1)
    to_right, to_left = call(edge_kernel, (own, behind, ahead), [(4, GROUPS, *side)] * 2)
    from_left = shift(to_right, "gy", 1)
    from_right = shift(to_left, "gy", -1)
    keep0, ops1, f1, own1, edge_f1, to_right2, to_left2, own3 = call(
        down_kernel,
        (own, behind, ahead, from_left, from_right),
        [(6, 24, NZ, 256), (5, N1, *side), (N1, *side), (8, *side), (2, *side)]
        + [(11, *side)] * 2
        + [(count, *side)],
        [(4, N0, NZ, 256)]
        + [wide] * 9
        + [(4, N1, NZ, 256), (5, N1, *side)]
        + [(N1, *side)] * 4
        + [(5, *side)]
        + [(4, *side)] * 3
        + [pltpu.SemaphoreType.DMA((20,))],
        limit=28,
        apart=(0, 1, 2),
        apart_outs=(0, 1, 2),
    )
    left, right = shift(to_right2, "gy", 1), shift(to_left2, "gy", -1)
    all3 = lax.all_to_all(own3, "gx", 0, 0)
    joined2, joined1, to_right, to_left = call(
        join_kernel,
        (to_right2, own1, edge_f1, left, right),
        [(10, *side), (8, *side)] + [(11 + H1, *side)] * 2,
    )
    behind, ahead = shift(to_right, "gx", 1), shift(to_left, "gx", -1)
    message, further, nearer = call(
        functools.partial(middle_kernel, count),
        (behind, joined2, ahead, all3),
        [(count + 1, *side)] + [(10, *side)] * 2,
        [(12, *side)] * 8,
    )
    left, right = shift(message, "gy", 1), shift(message, "gy", -1)
    behind2, ahead2 = shift(further, "gx", 1), shift(nearer, "gx", -1)
    left_far, right_far = shift(left, "gy", 1), shift(right, "gy", -1)
    near = (message, left, right, left_far, right_far)
    rhs3, further, nearer = call(
        functools.partial(near_kernel, count),
        (*near, behind2, ahead2),
        [(count, 5, 8, 128), (5, *side), (5, *side)],
    )
    rhs3 = lax.all_to_all(rhs3, "gx", 0, 0)
    behind3, ahead3 = shift(further, "gx", 1), shift(nearer, "gx", -1)
    rows3 = 2 * count + 2 * PAD3
    (e3,) = call(
        functools.partial(solve_kernel, count),
        (rhs3, *near),
        [(10, *side)],
        [(4, rows3, *side)] + [(rows3, *side)] * 3,
    )
    (out,) = call(
        up_kernel,
        (e3, behind3, behind2, behind, joined2, ahead, ahead2, ahead3, joined1, f1, ops1, keep0),
        [(NZ, R0, 128)],
        [(24, *side)] * 8
        + [(N1, *side)] * 3
        + [(24, NZ, 256)] * 2
        + [(5, *side), (10, *side), (11 + H1, *side), (10, *side)]
        + [(11 + H1, *side), (10, *side), (5, *side), (8, *side)]
        + [(5, N1, *side), (6, 24, NZ, 256)]
        + [pltpu.SemaphoreType.DMA((11,))],
        limit=18,
        apart=range(1, 12),
    )
    return out


def solution(mesh):
    in_specs = (P(None, "gx", "gy"),) * 4
    out_specs = P(None, "gx", "gy")
    return jax.shard_map(body, mesh=mesh, in_specs=in_specs, out_specs=out_specs, check_vma=False)
```

```python
import functools

import jax
import jax.numpy as jnp
from jax import lax
from jax.experimental import pallas as pl
from jax.experimental.pallas import tpu as pltpu
from jax.sharding import PartitionSpec as P

NU = 4
COARSE_SWEEPS = 24
OMEGA = 0.8
LEAK = 0.005

NZ = 32
H0 = 13
R0 = 16
N0 = R0 + 2 * H0
GROUPS = (N0 + 7) // 8
H1 = 6
N1 = 8 + 2 * H1
F32 = jnp.float32


def spec():
    return pl.BlockSpec(memory_space=pltpu.VMEM)


def call(kernel, ins, outs, scratch=(), limit=10, apart=(), apart_outs=()):
    def places(count, left, space):
        return [pl.BlockSpec(memory_space=space) if i in left else spec() for i in range(count)]

    return pl.pallas_call(
        kernel,
        out_shape=[
            pltpu.HBM(s, F32) if i in apart_outs else jax.ShapeDtypeStruct(s, F32)
            for i, s in enumerate(outs)
        ],
        in_specs=places(len(ins), apart, pl.ANY),
        out_specs=places(len(outs), apart_outs, pltpu.HBM),
        scratch_shapes=[pltpu.VMEM(s, F32) if isinstance(s, tuple) else s for s in scratch],
        compiler_params=pltpu.CompilerParams(vmem_limit_bytes=limit * 1024 * 1024),
    )(*ins)


def lanes(shape):
    return lax.broadcasted_iota(jnp.int32, shape, len(shape) - 1)


def roll(value, shift, axis):
    size = value.shape[axis]
    shift = shift % size
    return value if shift == 0 else pltpu.roll(value, shift, axis)


def planes(lo, hi, body, step=16):
    whole = (hi - lo) // step

    def chunk(i, carry):
        for k in range(step):
            body(lo + i * step + k)
        return carry

    if whole == 1:
        chunk(0, 0)
    elif whole:
        lax.fori_loop(0, whole, chunk, 0)
    for p in range(lo + whole * step, hi):
        body(p)


def ahead_z(v):
    return jnp.concatenate([v[8:], roll(v[:8], -1, 0)], 0)


def behind_z(v):
    return jnp.concatenate([roll(v[24:], 1, 0), v[:24]], 0)


def neighbours(v_ref, fx, fy, fz, p):
    v = v_ref[p]
    s = fx[p] * v_ref[p + 1] + fx[p - 1] * v_ref[p - 1]
    cy = fy[p]
    s = s + cy * roll(v, -1, 1) + roll(cy * v, 1, 1)
    cz = fz[p]
    s = s + cz * ahead_z(v) + behind_z(cz * v)
    return v, s


def sweep(src, dst, f, g, fx, fy, fz, lo, hi, step=16):
    def body(p):
        v, s = neighbours(src, fx, fy, fz, p)
        dst[p] = (1.0 - OMEGA) * v + g[p] * (f[p] + s)

    planes(lo, hi, body, step)


def residual(src, dst, f, d, fx, fy, fz, lo, hi, step=16):
    def body(p):
        v, s = neighbours(src, fx, fy, fz, p)
        dst[p] = f[p] - d[p] * v + s

    planes(lo, hi, body, step)


def diagonal(extra, fx, fy, fz, p):
    cy, cz = fy[p], fz[p]
    return extra + fx[p] + fx[p - 1] + cy + roll(cy, 1, 1) + cz + behind_z(cz)


def scale_of(d):
    free = d > 0.0
    return jnp.where(free, OMEGA / jnp.where(free, d, 1.0), 0.0)


def selection(rows, cols, target, odd=False):
    row = lax.broadcasted_iota(jnp.int32, (rows, cols), 0)
    col = lax.broadcasted_iota(jnp.int32, (rows, cols), 1)
    hit = col == target(row)
    if odd:
        hit = hit & (row % 2 == 1)
    return hit.astype(F32)


def dot(a, matrix):
    matrix = matrix.astype(jnp.bfloat16)
    total = None
    for _ in range(3):
        part = a.astype(jnp.bfloat16)
        a = a - part.astype(F32)
        product = jnp.dot(part, matrix, preferred_element_type=F32)
        total = product if total is None else total + product
    return total


BEHIND = (0, H0, 2 * H0, 3 * H0 - 1)
AHEAD = (0, H0, 2 * H0 - 1, 3 * H0 - 2)


def fetch(pairs, sems):
    copies = [pltpu.make_async_copy(src, dst, sems.at[i]) for i, (src, dst) in enumerate(pairs)]
    for copy in copies:
        copy.start()
    return copies


def stage_kernel(labels, cond_x, cond_y, cond_z, own, to_right, to_left):
    last_x = lax.axis_index("gx") == lax.axis_size("gx") - 1
    last_y = lax.axis_index("gy") == lax.axis_size("gy") - 1
    shape = (R0, 8, 128)
    row = lax.broadcasted_iota(jnp.int32, shape, 0)
    for a, ref in enumerate((labels, cond_x, cond_y, cond_z)):
        for b in range(4):
            value = jnp.stack([ref[4 * s + b].astype(F32) for s in range(8)])
            value = jnp.swapaxes(value, 0, 1)
            if a == 1:
                value = jnp.where(last_x & (row == R0 - 1), 0.0, value)
            if a == 2:
                value = jnp.where(last_y & (lanes(shape) == 127), 0.0, value)
            if a == 3 and b == 3:
                last = lax.broadcasted_iota(jnp.int32, shape, 1) == 7
                value = jnp.where(last, 0.0, value)
            part = slice(8 * b, 8 * b + 8)
            own[a, :, part] = value
            first, count = R0 - H0 + (a > 1), H0 - (a > 1)
            to_right[BEHIND[a] : BEHIND[a] + count, part] = value[first:]
            count = H0 - (a > 0)
            to_left[AHEAD[a] : AHEAD[a] + count, part] = value[:count]


def edge_kernel(own, behind, ahead, to_right, to_left):
    lane = lanes((NZ, 128))

    def plane(a, p):
        if p < H0:
            return behind[BEHIND[a] + p - (a > 1)] if p or a < 2 else None
        if p < H0 + R0:
            return own[a, p - H0]
        return ahead[AHEAD[a] + p - H0 - R0] if p < N0 - 1 or a == 0 else None

    for a in range(4):
        for c in range(GROUPS):
            right = left = jnp.zeros((NZ, 128), F32)
            for k in range(8):
                value = plane(a, 8 * c + k) if 8 * c + k < N0 else None
                if value is not None:
                    value = roll(value, 16 * k + 16, 1)
                    right = jnp.where(lane // 16 == k, value, right)
                    left = jnp.where(lane // 16 == (k + 1) % 8, value, left)
            to_right[a, c] = right
            to_left[a, c] = left


def down_kernel(
    own, behind, ahead, from_left, from_right,
    keep0, out_ops1, out_f1, own1, edge_f1, to_right, to_left, own3,
    ext, fx, fy, fz, d, g, f, va, vb, t, t1, ops1, d1, f1, va1, vb1, x2, y2, z2, e2, sems,
):
    lane = lanes((NZ, 128))
    main, pairs = pl.ds(0, 128), []
    for a in range(4):
        skip, count = int(a > 1), H0 - (a > 0)

        def place(lo, size, a=a):
            return ext.at[a, pl.ds(lo, size), :, main]

        pairs.append((behind.at[pl.ds(BEHIND[a], H0 - skip)], place(skip, H0 - skip)))
        pairs.append((own.at[a], place(H0, R0)))
        pairs.append((ahead.at[pl.ds(AHEAD[a], count)], place(H0 + R0, count)))
    copies = fetch(pairs, sems.at[pl.ds(8, 12)])
    for a in range(4):
        for c in range(GROUPS):
            left, right = from_left[a, c], from_right[a, c]
            for k in range(8):
                if 8 * c + k < N0:
                    both = jnp.where(lane // 16 == k, left, right)
                    ext[a, 8 * c + k, :, 128:256] = roll(both, -16 * k - 16, 1)
    for copy in copies:
        copy.wait()

    def cut(value, *kinds):
        for kind in kinds:
            value = jnp.where(kind, value, 0.0)
        return value

    fx[0] = cut(ext[1, 0], ext[0, 0] == 0.0, ext[0, 1] == 0.0)

    def operator0(p):
        label, label_up, label_down = ext[0, p], ext[0, p + 1], ext[0, p - 1]
        cx, cx_back, cy, cz = ext[1, p], ext[1, p - 1], ext[2, p], ext[3, p]
        cy_back, cz_back = roll(cy, 1, 1), behind_z(cz)
        y_up, y_down = roll(label, -1, 1), roll(label, 1, 1)
        z_up, z_down = ahead_z(label), behind_z(label)
        free = label == 0.0
        extra, rhs, diag = LEAK, 0.0, LEAK
        edges = (
            (cx, label_up), (cx_back, label_down), (cy, y_up), (cy_back, y_down), (cz, z_up), (cz_back, z_down),
        )
        for edge, across in edges:
            extra = extra + jnp.where(across == 0.0, 0.0, edge)
            rhs = rhs + jnp.where(across == 1.0, edge, 0.0)
            diag = diag + edge
        rhs, diag = cut(rhs, free), cut(diag, free)
        scale = scale_of(diag)
        fx[p] = cut(cx, free, label_up == 0.0)
        fy[p] = cut(cy, free, y_up == 0.0)
        fz[p] = cut(cz, free, z_up == 0.0)
        d[p], g[p], f[p] = diag, scale, rhs
        va[p] = scale * rhs
        t[p] = cut(extra, free)

    planes(1, N0 - 1, operator0, 4)
    src, dst = va, vb
    for s in range(NU - 1):
        sweep(src, dst, f, g, fx, fy, fz, 2 + s, N0 - 2 - s)
        src, dst = dst, src

    part = pl.ds(H0 - 4, 24)
    pairs = [(ref.at[part], keep0.at[i]) for i, ref in enumerate((src, f, g, fx, fy, fz))]
    copies = fetch(pairs, sems)

    def to1(row):
        return jnp.where(row < 192, row // 2, row // 2 - 128) + 32

    pick, pick_odd = selection(256, 128, to1), selection(256, 128, to1, True)

    def coarsen1(q):
        p = 2 * q + 1
        t1[0, q] = fx[p + 1]
        t1[1, q] = fy[p] + fy[p + 1]
        t1[2, q] = fz[p] + fz[p + 1]
        t1[3, q] = t[p] + t[p + 1]

    planes(0, N1, coarsen1, 4)
    for a in range(4):
        for c in range(0, N1, 4):
            value = t1[a, c : c + 4].reshape(4 * NZ, 256)
            ops1[a, c : c + 4] = dot(value, pick_odd if a == 1 else pick).reshape(4, NZ, 128)

    residual(src, dst, f, d, fx, fy, fz, H0 - 8, H0 + R0 + 8)
    f1[0:2] = jnp.zeros((2, NZ, 128), F32)
    f1[N1 - 2 : N1] = jnp.zeros((2, NZ, 128), F32)
    for c in range(2, N1 - 2, 4):
        value = jnp.stack([dst[2 * q + 1] + dst[2 * q + 2] for q in range(c, c + 4)])
        f1[c : c + 4] = dot(value.reshape(4 * NZ, 256), pick).reshape(4, NZ, 128)

    x1, y1, z1, e1, g1 = (ops1.at[a] for a in range(5))
    g1[0] = jnp.where(e1[0] > 0.0, 1.0, 0.0)

    def operator1(q):
        diag = diagonal(e1[q], x1, y1, z1, q)
        d1[q] = diag
        scale = scale_of(diag)
        g1[q] = scale
        va1[q] = scale * f1[q]

    planes(1, N1, operator1)
    copies += fetch(((ops1, out_ops1), (f1, out_f1)), sems.at[pl.ds(6, 2)])
    src, dst = va1, vb1
    for s in range(NU - 1):
        sweep(src, dst, f1, g1, x1, y1, z1, 3 + s, N1 - 3 - s)
        src, dst = dst, src
    own1[...] = src[H1 : H1 + 8]
    edge_f1[0] = f1[H1 + 4]
    edge_f1[1] = f1[H1 + 8 - 5]
    residual(src, dst, f1, d1, x1, y1, z1, H1, H1 + 8)

    half, half_odd = (selection(128, 128, lambda row: row // 2, odd) for odd in (False, True))
    q = [H1 + 2 * k for k in range(4)]
    f2 = dot(jnp.concatenate([dst[i] + dst[i + 1] for i in q]), half).reshape(4, NZ, 128)
    x2[...] = dot(jnp.concatenate([x1[i + 1] for i in [H1 - 2] + q]), half).reshape(5, NZ, 128)
    y2[...] = dot(jnp.concatenate([y1[i] + y1[i + 1] for i in q]), half_odd).reshape(4, NZ, 128)
    z2[...] = dot(jnp.concatenate([z1[i] + z1[i + 1] for i in q]), half).reshape(4, NZ, 128)
    e2[...] = dot(jnp.concatenate([e1[i] + e1[i + 1] for i in q]), half).reshape(4, NZ, 128)

    def around(x, x_back, y, z, extra):
        return extra + x + x_back + y + roll(y, 1, 1) + z + behind_z(z)

    for a in range(5):
        for h in range(2):
            pair = []
            for k in (2 * h, 2 * h + 1):
                if a == 4:
                    pair.append(around(x2[k + 1], x2[k], y2[k], z2[k], e2[k]))
                else:
                    pair.append((f2, x2[1:], y2, z2)[a][k])
            both = pair[0] + roll(pair[1], 64, 1)
            to_right[2 * a + h] = both
            to_left[2 * a + h] = both

    right = left = jnp.zeros((NZ, 128), F32)
    for k in range(8):
        here = lane // 8 == k
        right = jnp.where(here, roll(own1[k], 8 * k - 88, 1), right)
        left = jnp.where(here, roll(own1[k], 8 * k - 32, 1), left)
    to_right[10] = right
    to_left[10] = left

    x3 = dot(jnp.concatenate([x2[0], x2[2], x2[4]]), half).reshape(3, NZ, 128)
    y3 = dot(jnp.concatenate([y2[0] + y2[1], y2[2] + y2[3]]), half_odd).reshape(2, NZ, 128)
    z3 = dot(jnp.concatenate([z2[0] + z2[1], z2[2] + z2[3]]), half).reshape(2, NZ, 128)
    e3 = dot(jnp.concatenate([e2[0] + e2[1], e2[2] + e2[3]]), half).reshape(2, NZ, 128)
    total = jnp.zeros((NZ, 128), F32)
    for i in range(2):
        d3 = around(x3[i + 1], x3[i], y3[i], z3[i], e3[i])
        for a, value in enumerate((x3[i + 1], y3[i], z3[i], d3)):
            spot = 32 * a + 16 * i
            total = jnp.where(lane // 16 == spot // 16, roll(value, spot - 8, 1), total)
    for i in range(own3.shape[0]):
        own3[i] = total
    for copy in copies:
        copy.wait()


def join_kernel(own2, own1, edge_f1, left, right, joined2, joined1, to_right, to_left):
    lane = lanes((NZ, 128))
    low, high = lane % 64 < 16, lane % 64 >= 48
    for a in range(10):
        value = jnp.where(high, roll(right[a], 32, 1), own2[a])
        value = jnp.where(low, roll(left[a], -32, 1), value)
        joined2[a] = value
        to_right[a] = value
        to_left[a] = value
    low, high = lane // 8 == 3, lane // 8 == 12
    for k in range(8):
        value = jnp.where(low, roll(left[10], 24 - 8 * k, 1), own1[k])
        value = jnp.where(high, roll(right[10], 96 - 8 * k, 1), value)
        joined1[k] = value
        if k >= 8 - H1:
            to_right[10 + k - 8 + H1] = value
        if k < H1:
            to_left[10 + k] = value
    to_right[10 + H1] = edge_f1[1]
    to_left[10 + H1] = edge_f1[0]


def rows_of(value, odd):
    return roll(value, 64, 1) if odd else value


def middle_kernel(
    count, behind, own, ahead, ops3, message, further, nearer, f, fx, fy, fz, d, g, va, vb
):
    for j in range(12):
        source = (behind, own, ahead)[j // 4]
        for a, ref in enumerate((f, fx, fy, fz, d)):
            ref[j] = rows_of(source[2 * a + j % 4 // 2], j % 2)
        g[j] = scale_of(d[j])
        va[j] = g[j] * f[j]
    src, dst = va, vb
    for s in range(NU - 1):
        sweep(src, dst, f, g, fx, fy, fz, 1 + s, 11 - s)
        src, dst = dst, src
    residual(src, dst, f, d, fx, fy, fz, 4, 8)
    total = None
    for i in range(2):
        matrix = selection(
            128, 128, lambda row: jnp.where((row >= 16) & (row < 48), (row - 16) // 2 + 16 * i, -99)
        )
        part = dot(dst[4 + 2 * i] + dst[5 + 2 * i], matrix)
        total = part if total is None else total + part
    value = total[:8]
    for b in range(1, 4):
        value = value + roll(total[8 * b : 8 * b + 8], 32 * b, 1)
    message[count, 0:8] = value
    message[count, 8:] = jnp.zeros((NZ - 8, 128), F32)
    for i in range(count):
        message[i] = ops3[i]
    further[...] = behind[0:10]
    nearer[...] = ahead[0:10]


def near_kernel(count, own, left, right, left_far, right_far, out):
    rhs = [ref[count, 0:8] for ref in (left_far, left, own, right, right_far)]
    for c in range(count):
        for s in range(5):
            out[c, s] = rhs[s]


PAD3 = 8


def turned(parts):
    slot = lanes(parts[0].shape) // 16
    rolled = [roll(part, 16 * s, 1) for s, part in enumerate(parts)]
    results = []
    for m in range(8):
        total = jnp.zeros_like(parts[0])
        for s, value in enumerate(rolled):
            total = jnp.where(slot == (m + s) % 8, value, total)
        results.append(roll(total, -16 * m, 1))
    return results


def solve_kernel(
    count, gathered, own, left, right, left_far, right_far, out, ops3, f3, va3, vb3
):
    rows = 2 * count
    lo, hi = PAD3, PAD3 + rows
    x3, y3, z3, g3 = (ops3.at[a] for a in range(4))
    for ref in (va3, vb3, x3):
        ref[0:lo] = jnp.zeros((PAD3, NZ, 128), F32)
        ref[hi : hi + PAD3] = jnp.zeros((PAD3, NZ, 128), F32)

    def unpack(i, carry):
        p = lo + 2 * i
        for m, value in enumerate(turned([ref[i] for ref in (left_far, left, own, right, right_far)])):
            ops3[m // 2, p + m % 2] = scale_of(value) if m >= 6 else value
        for m, value in enumerate(turned([gathered[i, s] for s in range(5)])):
            part = slice(8 * (m // 2), 8 * (m // 2) + 8)
            f3[p + m % 2, part] = value
            va3[p + m % 2, part] = value * g3[p + m % 2, part]
        return carry

    lax.fori_loop(0, count, unpack, 0)

    def two(i, carry):
        sweep(va3, vb3, f3, g3, x3, y3, z3, lo, hi, 32)
        sweep(vb3, va3, f3, g3, x3, y3, z3, lo, hi, 32)
        return carry

    lax.fori_loop(0, (COARSE_SWEEPS - 1) // 2, two, 0)
    sweep(va3, vb3, f3, g3, x3, y3, z3, lo, hi, 32)
    start = lo + 2 * lax.axis_index("gx") - 4
    out[...] = vb3[pl.ds(start, 10)]


def up_kernel(
    e3, in_behind3, in_behind2, in_behind, in_own, in_ahead, in_ahead2, in_ahead3,
    in_joined1, in_f1, in_ops1, in_keep0,
    out,
    f2, x2, y2, z2, d2, g2, va2, vb2, f1, va1, vb1, va0, vb0,
    behind3, behind2, behind, own, ahead, ahead2, ahead3, joined1, ops1, keep0, sems,
):
    pairs = [
        (in_behind3, behind3), (in_behind2, behind2), (in_behind, behind), (in_own, own),
        (in_ahead, ahead), (in_ahead2, ahead2), (in_ahead3, ahead3),
        (in_joined1, joined1), (in_f1, f1), (in_ops1, ops1), (in_keep0, keep0),
    ]
    copies = fetch(pairs, sems)
    sources = [(behind3, 1)]
    sources += [(ref, h) for ref in (behind2, behind, own, ahead, ahead2) for h in range(2)]
    sources += [(ahead3, 0)]
    for n, (source, h) in enumerate(sources):
        if n % 2 or n == 0:
            copies[(n + 1) // 2].wait()
        for a, ref in enumerate((f2, x2, y2, z2, d2)):
            value = source[2 * a + h]
            ref[2 * n] = value
            ref[2 * n + 1] = roll(value, 64, 1)

    def operator2(j):
        g2[j] = scale_of(d2[j])
        va2[j] = g2[j] * f2[j]

    planes(0, 24, operator2, 24)
    src, dst = va2, vb2
    for s in range(NU - 1):
        sweep(src, dst, f2, g2, x2, y2, z2, 1 + s, 23 - s, 32)
        src, dst = dst, src
    col = lax.broadcasted_iota(jnp.int32, (128, 128), 1)
    row = lax.broadcasted_iota(jnp.int32, (128, 128), 0)
    spread = ((row == (col + 128 - 16) // 2 - 64 + 32) & (col < 64)).astype(F32)
    coarse = dot(e3[...].reshape(10 * NZ, 128), spread).reshape(10, NZ, 128)
    for r in range(-7, 11):
        j = r + 10
        src[j] = src[j] + jnp.where(g2[j] > 0.0, coarse[r // 2 + 4], 0.0)
    for s in range(NU):
        sweep(src, dst, f2, g2, x2, y2, z2, 4 + s, 20 - s, 32)
        src, dst = dst, src

    for copy in copies[7:10]:
        copy.wait()
    x1, y1, z1, g1 = ops1.at[0], ops1.at[1], ops1.at[2], ops1.at[4]
    f1[1] = behind[10 + H1]
    f1[N1 - 2] = ahead[10 + H1]
    spread = (row == (col - 32 + 128) // 2 - 64 + 16).astype(F32)
    coarse = dot(src[7:17].reshape(10 * NZ, 128), spread).reshape(10, NZ, 128)
    for q in range(N1):
        if q < H1:
            value = behind[10 + q]
        elif q < H1 + 8:
            value = joined1[q - H1]
        else:
            value = ahead[10 + q - H1 - 8]
        va1[q] = value + jnp.where(g1[q] > 0.0, coarse[q // 2], 0.0)
    src, dst = va1, vb1
    for s in range(NU):
        sweep(src, dst, f1, g1, x1, y1, z1, 1 + s, N1 - 1 - s, 32)
        src, dst = dst, src

    copies[10].wait()
    v0, f0, g0, x0, y0, z0 = (keep0.at[a] for a in range(6))
    col = lax.broadcasted_iota(jnp.int32, (128, 256), 1)
    row = lax.broadcasted_iota(jnp.int32, (128, 256), 0)
    spread = (row == jnp.where(col < 192, col // 2, col // 2 - 128) + 32).astype(F32)
    for c in range(0, 12, 4):
        coarse = dot(src[4 + c : 8 + c].reshape(4 * NZ, 128), spread).reshape(4, NZ, 256)
        for k in range(8):
            i = 2 * c + k
            va0[i] = v0[i] + jnp.where(g0[i] > 0.0, coarse[k // 2], 0.0)
    src, dst = va0, vb0
    for s in range(NU):
        sweep(src, dst, f0, g0, x0, y0, z0, 1 + s, 23 - s)
        src, dst = dst, src
    for b in range(4):
        value = jnp.swapaxes(src[4:20, 8 * b : 8 * b + 8, 0:128], 0, 1)
        for s in range(8):
            out[4 * s + b] = value[s]


def shift(value, axis, distance):
    count = lax.axis_size(axis)
    route = [(i, i + distance) for i in range(count) if 0 <= i + distance < count]
    return lax.ppermute(value, axis, route)


def body(labels, conduct_x, conduct_y, conduct_z):
    count = lax.axis_size("gx")
    side = (NZ, 128)
    wide = (N0, NZ, 256)
    own, to_right, to_left = call(
        stage_kernel,
        (labels, conduct_x, conduct_y, conduct_z),
        [(4, R0, *side), (4 * H0 - 2, *side), (4 * H0 - 3, *side)],
        limit=10,
    )
    behind = shift(to_right, "gx", 1)
    ahead = shift(to_left, "gx", -1)
    to_right, to_left = call(edge_kernel, (own, behind, ahead), [(4, GROUPS, *side)] * 2)
    from_left = shift(to_right, "gy", 1)
    from_right = shift(to_left, "gy", -1)
    keep0, ops1, f1, own1, edge_f1, to_right2, to_left2, own3 = call(
        down_kernel,
        (own, behind, ahead, from_left, from_right),
        [(6, 24, NZ, 256), (5, N1, *side), (N1, *side), (8, *side), (2, *side)]
        + [(11, *side)] * 2
        + [(count, *side)],
        [(4, N0, NZ, 256)]
        + [wide] * 9
        + [(4, N1, NZ, 256), (5, N1, *side)]
        + [(N1, *side)] * 4
        + [(5, *side)]
        + [(4, *side)] * 3
        + [pltpu.SemaphoreType.DMA((20,))],
        limit=28,
        apart=(0, 1, 2),
        apart_outs=(0, 1, 2),
    )
    left, right = shift(to_right2, "gy", 1), shift(to_left2, "gy", -1)
    all3 = lax.all_to_all(own3, "gx", 0, 0)
    joined2, joined1, to_right, to_left = call(
        join_kernel,
        (to_right2, own1, edge_f1, left, right),
        [(10, *side), (8, *side)] + [(11 + H1, *side)] * 2,
    )
    behind, ahead = shift(to_right, "gx", 1), shift(to_left, "gx", -1)
    message, further, nearer = call(
        functools.partial(middle_kernel, count),
        (behind, joined2, ahead, all3),
        [(count + 1, *side)] + [(10, *side)] * 2,
        [(12, *side)] * 8,
    )
    left, right = shift(message, "gy", 1), shift(message, "gy", -1)
    behind2, ahead2 = shift(further, "gx", 1), shift(nearer, "gx", -1)
    left_far, right_far = shift(left, "gy", 1), shift(right, "gy", -1)
    near = (message, left, right, left_far, right_far)
    (rhs3,) = call(functools.partial(near_kernel, count), near, [(count, 5, 8, 128)])
    rhs3 = lax.all_to_all(rhs3, "gx", 0, 0)
    behind3, ahead3 = shift(behind2, "gx", 1), shift(ahead2, "gx", -1)
    rows3 = 2 * count + 2 * PAD3
    (e3,) = call(
        functools.partial(solve_kernel, count),
        (rhs3, *near),
        [(10, *side)],
        [(4, rows3, *side)] + [(rows3, *side)] * 3,
    )
    keep0, ops1, f1 = (pltpu.with_memory_space_constraint(x, pltpu.HBM) for x in (keep0, ops1, f1))
    (out,) = call(
        up_kernel,
        (e3, behind3, behind2, behind, joined2, ahead, ahead2, ahead3, joined1, f1, ops1, keep0),
        [(NZ, R0, 128)],
        [(24, *side)] * 8
        + [(N1, *side)] * 3
        + [(24, NZ, 256)] * 2
        + [(10, *side), (10, *side), (11 + H1, *side), (10, *side)]
        + [(11 + H1, *side), (10, *side), (10, *side), (8, *side)]
        + [(5, N1, *side), (6, 24, NZ, 256)]
        + [pltpu.SemaphoreType.DMA((11,))],
        limit=17,
        apart=range(1, 12),
    )
    return out


def solution(mesh):
    in_specs = (P(None, "gx", "gy"),) * 4
    out_specs = P(None, "gx", "gy")
    return jax.shard_map(body, mesh=mesh, in_specs=in_specs, out_specs=out_specs, check_vma=False)
```

```python
import functools

import jax
import jax.numpy as jnp
from jax import lax
from jax.experimental import pallas as pl
from jax.experimental.pallas import tpu as pltpu
from jax.sharding import PartitionSpec as P

NU = 4
COARSE_SWEEPS = 24
OMEGA = 0.8
LEAK = 0.005

NZ = 32
H0 = 13
R0 = 16
N0 = R0 + 2 * H0
GROUPS = (N0 + 7) // 8
H1 = 6
N1 = 8 + 2 * H1
F32 = jnp.float32


def spec():
    return pl.BlockSpec(memory_space=pltpu.VMEM)


def call(kernel, ins, outs, scratch=(), limit=10, apart=(), apart_outs=()):
    def places(count, left, space):
        return [pl.BlockSpec(memory_space=space) if i in left else spec() for i in range(count)]

    return pl.pallas_call(
        kernel,
        out_shape=[
            pltpu.HBM(s, F32) if i in apart_outs else jax.ShapeDtypeStruct(s, F32)
            for i, s in enumerate(outs)
        ],
        in_specs=places(len(ins), apart, pl.ANY),
        out_specs=places(len(outs), apart_outs, pltpu.HBM),
        scratch_shapes=[pltpu.VMEM(s, F32) if isinstance(s, tuple) else s for s in scratch],
        compiler_params=pltpu.CompilerParams(vmem_limit_bytes=limit * 1024 * 1024),
    )(*ins)


def lanes(shape):
    return lax.broadcasted_iota(jnp.int32, shape, len(shape) - 1)


def roll(value, shift, axis):
    size = value.shape[axis]
    shift = shift % size
    return value if shift == 0 else pltpu.roll(value, shift, axis)


def planes(lo, hi, body, step=16):
    whole = (hi - lo) // step

    def chunk(i, carry):
        for k in range(step):
            body(lo + i * step + k)
        return carry

    if whole == 1:
        chunk(0, 0)
    elif whole:
        lax.fori_loop(0, whole, chunk, 0)
    for p in range(lo + whole * step, hi):
        body(p)


def ahead_z(v):
    return jnp.concatenate([v[8:], roll(v[:8], -1, 0)], 0)


def behind_z(v):
    return jnp.concatenate([roll(v[24:], 1, 0), v[:24]], 0)


def neighbours(v_ref, fx, fy, fz, p):
    v = v_ref[p]
    s = fx[p] * v_ref[p + 1] + fx[p - 1] * v_ref[p - 1]
    cy = fy[p]
    s = s + cy * roll(v, -1, 1) + roll(cy * v, 1, 1)
    cz = fz[p]
    s = s + cz * ahead_z(v) + behind_z(cz * v)
    return v, s


def sweep(src, dst, f, g, fx, fy, fz, lo, hi, step=16):
    def body(p):
        v, s = neighbours(src, fx, fy, fz, p)
        dst[p] = (1.0 - OMEGA) * v + g[p] * (f[p] + s)

    planes(lo, hi, body, step)


def residual(src, dst, f, d, fx, fy, fz, lo, hi, step=16):
    def body(p):
        v, s = neighbours(src, fx, fy, fz, p)
        dst[p] = f[p] - d[p] * v + s

    planes(lo, hi, body, step)


def diagonal(extra, fx, fy, fz, p):
    cy, cz = fy[p], fz[p]
    return extra + fx[p] + fx[p - 1] + cy + roll(cy, 1, 1) + cz + behind_z(cz)


def scale_of(d):
    free = d > 0.0
    return jnp.where(free, OMEGA / jnp.where(free, d, 1.0), 0.0)


def selection(rows, cols, target, odd=False):
    row = lax.broadcasted_iota(jnp.int32, (rows, cols), 0)
    col = lax.broadcasted_iota(jnp.int32, (rows, cols), 1)
    hit = col == target(row)
    if odd:
        hit = hit & (row % 2 == 1)
    return hit.astype(F32)


def dot(a, matrix):
    matrix = matrix.astype(jnp.bfloat16)
    total = None
    for _ in range(3):
        part = a.astype(jnp.bfloat16)
        a = a - part.astype(F32)
        product = jnp.dot(part, matrix, preferred_element_type=F32)
        total = product if total is None else total + product
    return total


BEHIND = (0, H0, 2 * H0, 3 * H0 - 1)
AHEAD = (0, H0, 2 * H0 - 1, 3 * H0 - 2)


def fetch(pairs, sems):
    copies = [pltpu.make_async_copy(src, dst, sems.at[i]) for i, (src, dst) in enumerate(pairs)]
    for copy in copies:
        copy.start()
    return copies


def stage_kernel(
    in0, in1, in2, in3, own, to_right, to_left, labels, cond_x, cond_y, cond_z, sems
):
    copies = fetch(((in0, labels), (in1, cond_x), (in2, cond_y), (in3, cond_z)), sems)
    last_x = lax.axis_index("gx") == lax.axis_size("gx") - 1
    last_y = lax.axis_index("gy") == lax.axis_size("gy") - 1
    shape = (R0, 8, 128)
    row = lax.broadcasted_iota(jnp.int32, shape, 0)
    for a, ref in enumerate((labels, cond_x, cond_y, cond_z)):
        copies[a].wait()
        for b in range(4):
            value = jnp.stack([ref[4 * s + b].astype(F32) for s in range(8)])
            value = jnp.swapaxes(value, 0, 1)
            if a == 1:
                value = jnp.where(last_x & (row == R0 - 1), 0.0, value)
            if a == 2:
                value = jnp.where(last_y & (lanes(shape) == 127), 0.0, value)
            if a == 3 and b == 3:
                last = lax.broadcasted_iota(jnp.int32, shape, 1) == 7
                value = jnp.where(last, 0.0, value)
            part = slice(8 * b, 8 * b + 8)
            own[a, :, part] = value
            first, count = R0 - H0 + (a > 1), H0 - (a > 1)
            to_right[BEHIND[a] : BEHIND[a] + count, part] = value[first:]
            count = H0 - (a > 0)
            to_left[AHEAD[a] : AHEAD[a] + count, part] = value[:count]


def edge_kernel(own, behind, ahead, to_right, to_left):
    lane = lanes((NZ, 128))

    def plane(a, p):
        if p < H0:
            return behind[BEHIND[a] + p - (a > 1)] if p or a < 2 else None
        if p < H0 + R0:
            return own[a, p - H0]
        return ahead[AHEAD[a] + p - H0 - R0] if p < N0 - 1 or a == 0 else None

    for a in range(4):
        for c in range(GROUPS):
            right = left = jnp.zeros((NZ, 128), F32)
            for k in range(8):
                value = plane(a, 8 * c + k) if 8 * c + k < N0 else None
                if value is not None:
                    value = roll(value, 16 * k + 16, 1)
                    right = jnp.where(lane // 16 == k, value, right)
                    left = jnp.where(lane // 16 == (k + 1) % 8, value, left)
            to_right[a, c] = right
            to_left[a, c] = left


def down_kernel(
    own, behind, ahead, from_left, from_right,
    keep0, out_ops1, out_f1, own1, edge_f1, to_right, to_left, own3,
    ext, fx, fy, fz, d, g, f, va, vb, t, t1, ops1, d1, f1, va1, vb1, x2, y2, z2, e2, sems,
):
    lane = lanes((NZ, 128))
    main, pairs = pl.ds(0, 128), []
    for a in range(4):
        skip, count = int(a > 1), H0 - (a > 0)

        def place(lo, size, a=a):
            return ext.at[a, pl.ds(lo, size), :, main]

        pairs.append((behind.at[pl.ds(BEHIND[a], H0 - skip)], place(skip, H0 - skip)))
        pairs.append((own.at[a], place(H0, R0)))
        pairs.append((ahead.at[pl.ds(AHEAD[a], count)], place(H0 + R0, count)))
    copies = fetch(pairs, sems.at[pl.ds(8, 12)])
    for a in range(4):
        for c in range(GROUPS):
            left, right = from_left[a, c], from_right[a, c]
            for k in range(8):
                if 8 * c + k < N0:
                    both = jnp.where(lane // 16 == k, left, right)
                    ext[a, 8 * c + k, :, 128:256] = roll(both, -16 * k - 16, 1)
    for copy in copies:
        copy.wait()

    def cut(value, *kinds):
        for kind in kinds:
            value = jnp.where(kind, value, 0.0)
        return value

    fx[0] = cut(ext[1, 0], ext[0, 0] == 0.0, ext[0, 1] == 0.0)

    def operator0(p):
        label, label_up, label_down = ext[0, p], ext[0, p + 1], ext[0, p - 1]
        cx, cx_back, cy, cz = ext[1, p], ext[1, p - 1], ext[2, p], ext[3, p]
        cy_back, cz_back = roll(cy, 1, 1), behind_z(cz)
        y_up, y_down = roll(label, -1, 1), roll(label, 1, 1)
        z_up, z_down = ahead_z(label), behind_z(label)
        free = label == 0.0
        extra, rhs, diag = LEAK, 0.0, LEAK
        edges = (
            (cx, label_up), (cx_back, label_down), (cy, y_up), (cy_back, y_down), (cz, z_up), (cz_back, z_down),
        )
        for edge, across in edges:
            extra = extra + jnp.where(across == 0.0, 0.0, edge)
            rhs = rhs + jnp.where(across == 1.0, edge, 0.0)
            diag = diag + edge
        rhs, diag = cut(rhs, free), cut(diag, free)
        scale = scale_of(diag)
        fx[p] = cut(cx, free, label_up == 0.0)
        fy[p] = cut(cy, free, y_up == 0.0)
        fz[p] = cut(cz, free, z_up == 0.0)
        d[p], g[p], f[p] = diag, scale, rhs
        va[p] = scale * rhs
        t[p] = cut(extra, free)

    planes(1, N0 - 1, operator0, 4)
    src, dst = va, vb
    for s in range(NU - 1):
        sweep(src, dst, f, g, fx, fy, fz, 2 + s, N0 - 2 - s, N0 // 2 - 2 - s)
        src, dst = dst, src

    part = pl.ds(H0 - 4, 24)
    pairs = [(ref.at[part], keep0.at[i]) for i, ref in enumerate((src, f, g, fx, fy, fz))]
    copies = fetch(pairs, sems)

    def to1(row):
        return jnp.where(row < 192, row // 2, row // 2 - 128) + 32

    pick, pick_odd = selection(256, 128, to1), selection(256, 128, to1, True)

    def coarsen1(q):
        p = 2 * q + 1
        t1[0, q] = fx[p + 1]
        t1[1, q] = fy[p] + fy[p + 1]
        t1[2, q] = fz[p] + fz[p + 1]
        t1[3, q] = t[p] + t[p + 1]

    planes(0, N1, coarsen1, 4)
    for a in range(4):
        for c in range(0, N1, 4):
            value = t1[a, c : c + 4].reshape(4 * NZ, 256)
            ops1[a, c : c + 4] = dot(value, pick_odd if a == 1 else pick).reshape(4, NZ, 128)

    residual(src, dst, f, d, fx, fy, fz, H0 - 8, H0 + R0 + 8)
    f1[0:2] = jnp.zeros((2, NZ, 128), F32)
    f1[N1 - 2 : N1] = jnp.zeros((2, NZ, 128), F32)
    for c in range(2, N1 - 2, 4):
        value = jnp.stack([dst[2 * q + 1] + dst[2 * q + 2] for q in range(c, c + 4)])
        f1[c : c + 4] = dot(value.reshape(4 * NZ, 256), pick).reshape(4, NZ, 128)

    x1, y1, z1, e1, g1 = (ops1.at[a] for a in range(5))
    g1[0] = jnp.where(e1[0] > 0.0, 1.0, 0.0)

    def operator1(q):
        diag = diagonal(e1[q], x1, y1, z1, q)
        d1[q] = diag
        scale = scale_of(diag)
        g1[q] = scale
        va1[q] = scale * f1[q]

    planes(1, N1, operator1)
    copies += fetch(((ops1, out_ops1), (f1, out_f1)), sems.at[pl.ds(6, 2)])
    src, dst = va1, vb1
    for s in range(NU - 1):
        sweep(src, dst, f1, g1, x1, y1, z1, 3 + s, N1 - 3 - s)
        src, dst = dst, src
    own1[...] = src[H1 : H1 + 8]
    edge_f1[0] = f1[H1 + 4]
    edge_f1[1] = f1[H1 + 8 - 5]
    residual(src, dst, f1, d1, x1, y1, z1, H1, H1 + 8)

    half, half_odd = (selection(128, 128, lambda row: row // 2, odd) for odd in (False, True))
    q = [H1 + 2 * k for k in range(4)]
    f2 = dot(jnp.concatenate([dst[i] + dst[i + 1] for i in q]), half).reshape(4, NZ, 128)
    x2[...] = dot(jnp.concatenate([x1[i + 1] for i in [H1 - 2] + q]), half).reshape(5, NZ, 128)
    y2[...] = dot(jnp.concatenate([y1[i] + y1[i + 1] for i in q]), half_odd).reshape(4, NZ, 128)
    z2[...] = dot(jnp.concatenate([z1[i] + z1[i + 1] for i in q]), half).reshape(4, NZ, 128)
    e2[...] = dot(jnp.concatenate([e1[i] + e1[i + 1] for i in q]), half).reshape(4, NZ, 128)

    def around(x, x_back, y, z, extra):
        return extra + x + x_back + y + roll(y, 1, 1) + z + behind_z(z)

    for a in range(5):
        for h in range(2):
            pair = []
            for k in (2 * h, 2 * h + 1):
                if a == 4:
                    pair.append(around(x2[k + 1], x2[k], y2[k], z2[k], e2[k]))
                else:
                    pair.append((f2, x2[1:], y2, z2)[a][k])
            both = pair[0] + roll(pair[1], 64, 1)
            to_right[2 * a + h] = both
            to_left[2 * a + h] = both

    right = left = jnp.zeros((NZ, 128), F32)
    for k in range(8):
        here = lane // 8 == k
        right = jnp.where(here, roll(own1[k], 8 * k - 88, 1), right)
        left = jnp.where(here, roll(own1[k], 8 * k - 32, 1), left)
    to_right[10] = right
    to_left[10] = left

    x3 = dot(jnp.concatenate([x2[0], x2[2], x2[4]]), half).reshape(3, NZ, 128)
    y3 = dot(jnp.concatenate([y2[0] + y2[1], y2[2] + y2[3]]), half_odd).reshape(2, NZ, 128)
    z3 = dot(jnp.concatenate([z2[0] + z2[1], z2[2] + z2[3]]), half).reshape(2, NZ, 128)
    e3 = dot(jnp.concatenate([e2[0] + e2[1], e2[2] + e2[3]]), half).reshape(2, NZ, 128)
    total = jnp.zeros((NZ, 128), F32)
    for i in range(2):
        d3 = around(x3[i + 1], x3[i], y3[i], z3[i], e3[i])
        for a, value in enumerate((x3[i + 1], y3[i], z3[i], d3)):
            spot = 32 * a + 16 * i
            total = jnp.where(lane // 16 == spot // 16, roll(value, spot - 8, 1), total)
    for i in range(own3.shape[0]):
        own3[i] = total
    for copy in copies:
        copy.wait()


def join_kernel(own2, own1, edge_f1, left, right, joined2, joined1, to_right, to_left):
    lane = lanes((NZ, 128))
    low, high = lane % 64 < 16, lane % 64 >= 48
    for a in range(10):
        value = jnp.where(high, roll(right[a], 32, 1), own2[a])
        value = jnp.where(low, roll(left[a], -32, 1), value)
        joined2[a] = value
        to_right[a] = value
        to_left[a] = value
    low, high = lane // 8 == 3, lane // 8 == 12
    for k in range(8):
        value = jnp.where(low, roll(left[10], 24 - 8 * k, 1), own1[k])
        value = jnp.where(high, roll(right[10], 96 - 8 * k, 1), value)
        joined1[k] = value
        if k >= 8 - H1:
            to_right[10 + k - 8 + H1] = value
        if k < H1:
            to_left[10 + k] = value
    to_right[10 + H1] = edge_f1[1]
    to_left[10 + H1] = edge_f1[0]


def rows_of(value, odd):
    return roll(value, 64, 1) if odd else value


def middle_kernel(
    count, behind, own, ahead, ops3, message, further, nearer, f, fx, fy, fz, d, g, va, vb
):
    for j in range(12):
        source = (behind, own, ahead)[j // 4]
        for a, ref in enumerate((f, fx, fy, fz, d)):
            ref[j] = rows_of(source[2 * a + j % 4 // 2], j % 2)
        g[j] = scale_of(d[j])
        va[j] = g[j] * f[j]
    src, dst = va, vb
    for s in range(NU - 1):
        sweep(src, dst, f, g, fx, fy, fz, 1 + s, 11 - s)
        src, dst = dst, src
    residual(src, dst, f, d, fx, fy, fz, 4, 8)
    total = None
    for i in range(2):
        matrix = selection(
            128, 128, lambda row: jnp.where((row >= 16) & (row < 48), (row - 16) // 2 + 16 * i, -99)
        )
        part = dot(dst[4 + 2 * i] + dst[5 + 2 * i], matrix)
        total = part if total is None else total + part
    value = total[:8]
    for b in range(1, 4):
        value = value + roll(total[8 * b : 8 * b + 8], 32 * b, 1)
    message[count, 0:8] = value
    message[count, 8:] = jnp.zeros((NZ - 8, 128), F32)
    for i in range(count):
        message[i] = ops3[i]
    further[...] = behind[0:10]
    nearer[...] = ahead[0:10]


def near_kernel(count, own, left, right, left_far, right_far, out):
    rhs = [ref[count, 0:8] for ref in (left_far, left, own, right, right_far)]
    for c in range(count):
        for s in range(5):
            out[c, s] = rhs[s]


PAD3 = 16


def turned(parts):
    slot = lanes(parts[0].shape) // 16
    rolled = [roll(part, 16 * s, 1) for s, part in enumerate(parts)]
    results = []
    for m in range(8):
        total = jnp.zeros_like(parts[0])
        for s, value in enumerate(rolled):
            total = jnp.where(slot == (m + s) % 8, value, total)
        results.append(roll(total, -16 * m, 1))
    return results


def spread3_kernel(count, own, left, right, left_far, right_far, out, ops3, sems):
    def unpack(i, carry):
        values = turned([ref[i] for ref in (left_far, left, own, right, right_far)])
        for m, value in enumerate(values):
            ops3[m // 2, 2 * i + m % 2] = scale_of(value) if m >= 6 else value
        return carry

    lax.fori_loop(0, count, unpack, 0)
    for copy in fetch(((ops3, out),), sems):
        copy.wait()


def solve_kernel(count, gathered, in_ops3, out, ops3, f3, va3, vb3, sems):
    lo, hi = PAD3, PAD3 + 2 * count
    inner = pl.ds(lo, 2 * count)
    copies = fetch([(in_ops3.at[a], ops3.at[a, inner]) for a in range(4)], sems)
    x3, y3, z3, g3 = (ops3.at[a] for a in range(4))
    for ref in (x3, y3, z3, g3, va3, vb3, f3):
        ref[0:lo] = jnp.zeros((PAD3, NZ, 128), F32)
        ref[hi : hi + PAD3] = jnp.zeros((PAD3, NZ, 128), F32)

    def unpack(i, carry):
        p = lo + 2 * i
        for m, value in enumerate(turned([gathered[i, s] for s in range(5)])):
            part = slice(8 * (m // 2), 8 * (m // 2) + 8)
            f3[p + m % 2, part] = value
        return carry

    lax.fori_loop(0, count, unpack, 0)
    for copy in copies:
        copy.wait()

    def first(p):
        va3[p] = g3[p] * f3[p]

    planes(lo, hi, first)

    def two(i, carry):
        sweep(va3, vb3, f3, g3, x3, y3, z3, lo, hi, 32)
        sweep(vb3, va3, f3, g3, x3, y3, z3, lo, hi, 32)
        return carry

    last = 11
    lax.fori_loop(0, (COARSE_SWEEPS - 1 - last) // 2, two, 0)
    start = lo + 2 * lax.axis_index("gx") - 4
    src, dst = va3, vb3
    for k in range(last - 1, -1, -1):
        for i in range(10 + 2 * k):
            p = start - k + i
            v, s = neighbours(src, x3, y3, z3, p)
            dst[p] = (1.0 - OMEGA) * v + g3[p] * (f3[p] + s)
        src, dst = dst, src
    out[...] = src[pl.ds(start, 10)]


def up_kernel(
    e3, in_behind3, in_behind2, in_behind, in_own, in_ahead, in_ahead2, in_ahead3,
    in_joined1, in_f1, in_ops1, in_keep0,
    out,
    f2, x2, y2, z2, d2, g2, va2, vb2, f1, va1, vb1, va0, vb0,
    behind3, behind2, behind, own, ahead, ahead2, ahead3, joined1, ops1, keep0, sems,
):
    pairs = [
        (in_behind3, behind3), (in_behind2, behind2), (in_behind, behind), (in_own, own),
        (in_ahead, ahead), (in_ahead2, ahead2), (in_ahead3, ahead3),
        (in_joined1, joined1), (in_f1, f1), (in_ops1, ops1), (in_keep0, keep0),
    ]
    copies = fetch(pairs, sems)
    sources = [(behind3, 1)]
    sources += [(ref, h) for ref in (behind2, behind, own, ahead, ahead2) for h in range(2)]
    sources += [(ahead3, 0)]
    for n, (source, h) in enumerate(sources):
        if n % 2 or n == 0:
            copies[(n + 1) // 2].wait()
        for a, ref in enumerate((f2, x2, y2, z2, d2)):
            value = source[2 * a + h]
            ref[2 * n] = value
            ref[2 * n + 1] = roll(value, 64, 1)

    def operator2(j):
        g2[j] = scale_of(d2[j])
        va2[j] = g2[j] * f2[j]

    planes(0, 24, operator2, 24)
    src, dst = va2, vb2
    for s in range(NU - 1):
        sweep(src, dst, f2, g2, x2, y2, z2, 1 + s, 23 - s, 32)
        src, dst = dst, src
    col = lax.broadcasted_iota(jnp.int32, (128, 128), 1)
    row = lax.broadcasted_iota(jnp.int32, (128, 128), 0)
    spread = ((row == (col + 128 - 16) // 2 - 64 + 32) & (col < 64)).astype(F32)
    coarse = dot(e3[...].reshape(10 * NZ, 128), spread).reshape(10, NZ, 128)
    for r in range(-7, 11):
        j = r + 10
        src[j] = src[j] + jnp.where(g2[j] > 0.0, coarse[r // 2 + 4], 0.0)
    for s in range(NU):
        sweep(src, dst, f2, g2, x2, y2, z2, 4 + s, 20 - s, 32)
        src, dst = dst, src

    for copy in copies[7:10]:
        copy.wait()
    x1, y1, z1, g1 = ops1.at[0], ops1.at[1], ops1.at[2], ops1.at[4]
    f1[1] = behind[10 + H1]
    f1[N1 - 2] = ahead[10 + H1]
    spread = (row == (col - 32 + 128) // 2 - 64 + 16).astype(F32)
    coarse = dot(src[7:17].reshape(10 * NZ, 128), spread).reshape(10, NZ, 128)
    for q in range(N1):
        if q < H1:
            value = behind[10 + q]
        elif q < H1 + 8:
            value = joined1[q - H1]
        else:
            value = ahead[10 + q - H1 - 8]
        va1[q] = value + jnp.where(g1[q] > 0.0, coarse[q // 2], 0.0)
    src, dst = va1, vb1
    for s in range(NU):
        sweep(src, dst, f1, g1, x1, y1, z1, 1 + s, N1 - 1 - s, 32)
        src, dst = dst, src

    copies[10].wait()
    v0, f0, g0, x0, y0, z0 = (keep0.at[a] for a in range(6))
    col = lax.broadcasted_iota(jnp.int32, (128, 256), 1)
    row = lax.broadcasted_iota(jnp.int32, (128, 256), 0)
    spread = (row == jnp.where(col < 192, col // 2, col // 2 - 128) + 32).astype(F32)
    for c in range(0, 12, 4):
        coarse = dot(src[4 + c : 8 + c].reshape(4 * NZ, 128), spread).reshape(4, NZ, 256)
        for k in range(8):
            i = 2 * c + k
            va0[i] = v0[i] + jnp.where(g0[i] > 0.0, coarse[k // 2], 0.0)
    src, dst = va0, vb0
    for s in range(NU):
        sweep(src, dst, f0, g0, x0, y0, z0, 1 + s, 23 - s, 11 - s)
        src, dst = dst, src
    for b in range(4):
        value = jnp.swapaxes(src[4:20, 8 * b : 8 * b + 8, 0:128], 0, 1)
        for s in range(8):
            out[4 * s + b] = value[s]


def shift(value, axis, distance):
    count = lax.axis_size(axis)
    route = [(i, i + distance) for i in range(count) if 0 <= i + distance < count]
    return lax.ppermute(value, axis, route)


def body(labels, conduct_x, conduct_y, conduct_z):
    count = lax.axis_size("gx")
    side = (NZ, 128)
    wide = (N0, NZ, 256)
    fields = (labels, conduct_x, conduct_y, conduct_z)
    own, to_right, to_left = call(
        stage_kernel,
        [pltpu.with_memory_space_constraint(x, pltpu.HBM) for x in fields],
        [(4, R0, *side), (4 * H0 - 2, *side), (4 * H0 - 3, *side)],
        [pltpu.VMEM(x.shape, x.dtype) for x in fields] + [pltpu.SemaphoreType.DMA((4,))],
        apart=(0, 1, 2, 3),
    )
    behind = shift(to_right, "gx", 1)
    ahead = shift(to_left, "gx", -1)
    to_right, to_left = call(edge_kernel, (own, behind, ahead), [(4, GROUPS, *side)] * 2)
    from_left = shift(to_right, "gy", 1)
    from_right = shift(to_left, "gy", -1)
    keep0, ops1, f1, own1, edge_f1, to_right2, to_left2, own3 = call(
        down_kernel,
        (own, behind, ahead, from_left, from_right),
        [(6, 24, NZ, 256), (5, N1, *side), (N1, *side), (8, *side), (2, *side)]
        + [(11, *side)] * 2
        + [(count, *side)],
        [(4, N0, NZ, 256)]
        + [wide] * 9
        + [(4, N1, NZ, 256), (5, N1, *side)]
        + [(N1, *side)] * 4
        + [(5, *side)]
        + [(4, *side)] * 3
        + [pltpu.SemaphoreType.DMA((20,))],
        limit=28,
        apart=(0, 1, 2),
        apart_outs=(0, 1, 2),
    )
    left, right = shift(to_right2, "gy", 1), shift(to_left2, "gy", -1)
    all3 = lax.all_to_all(own3, "gx", 0, 0)
    joined2, joined1, to_right, to_left = call(
        join_kernel,
        (to_right2, own1, edge_f1, left, right),
        [(10, *side), (8, *side)] + [(11 + H1, *side)] * 2,
    )
    behind, ahead = shift(to_right, "gx", 1), shift(to_left, "gx", -1)
    message, further, nearer = call(
        functools.partial(middle_kernel, count),
        (behind, joined2, ahead, all3),
        [(count + 1, *side)] + [(10, *side)] * 2,
        [(12, *side)] * 8,
    )
    left, right = shift(message, "gy", 1), shift(message, "gy", -1)
    behind2, ahead2 = shift(further, "gx", 1), shift(nearer, "gx", -1)
    left_far, right_far = shift(left, "gy", 1), shift(right, "gy", -1)
    near = (message, left, right, left_far, right_far)
    (rhs3,) = call(functools.partial(near_kernel, count), near, [(count, 5, 8, 128)])
    rhs3 = lax.all_to_all(rhs3, "gx", 0, 0)
    behind3, ahead3 = shift(behind2, "gx", 1), shift(ahead2, "gx", -1)
    rows3 = 2 * count + 2 * PAD3
    (ops3,) = call(
        functools.partial(spread3_kernel, count),
        near,
        [(4, 2 * count, *side)],
        [(4, 2 * count, *side), pltpu.SemaphoreType.DMA((1,))],
        apart_outs=(0,),
    )
    (e3,) = call(
        functools.partial(solve_kernel, count),
        (rhs3, pltpu.with_memory_space_constraint(ops3, pltpu.HBM)),
        [(10, *side)],
        [(4, rows3, *side)] + [(rows3, *side)] * 3 + [pltpu.SemaphoreType.DMA((4,))],
        limit=14,
        apart=(1,),
    )
    keep0, ops1, f1 = (pltpu.with_memory_space_constraint(x, pltpu.HBM) for x in (keep0, ops1, f1))
    (out,) = call(
        up_kernel,
        (e3, behind3, behind2, behind, joined2, ahead, ahead2, ahead3, joined1, f1, ops1, keep0),
        [(NZ, R0, 128)],
        [(24, *side)] * 8
        + [(N1, *side)] * 3
        + [(24, NZ, 256)] * 2
        + [(10, *side), (10, *side), (11 + H1, *side), (10, *side)]
        + [(11 + H1, *side), (10, *side), (10, *side), (8, *side)]
        + [(5, N1, *side), (6, 24, NZ, 256)]
        + [pltpu.SemaphoreType.DMA((11,))],
        limit=17,
        apart=range(1, 12),
    )
    return out


def solution(mesh):
    in_specs = (P(None, "gx", "gy"),) * 4
    out_specs = P(None, "gx", "gy")
    return jax.shard_map(body, mesh=mesh, in_specs=in_specs, out_specs=out_specs, check_vma=False)
```

```python
import functools

import jax
import jax.numpy as jnp
from jax import lax
from jax.experimental import pallas as pl
from jax.experimental.pallas import tpu as pltpu
from jax.sharding import PartitionSpec as P

NU = 4
COARSE_SWEEPS = 24
OMEGA = 0.8
LEAK = 0.005

NZ = 32
H0 = 13
R0 = 16
N0 = R0 + 2 * H0
GROUPS = (N0 + 7) // 8
H1 = 6
N1 = 8 + 2 * H1
F32 = jnp.float32


def spec():
    return pl.BlockSpec(memory_space=pltpu.VMEM)


def call(kernel, ins, outs, scratch=(), limit=10, apart=(), apart_outs=()):
    def places(count, left, space):
        return [pl.BlockSpec(memory_space=space) if i in left else spec() for i in range(count)]

    return pl.pallas_call(
        kernel,
        out_shape=[
            pltpu.HBM(s, F32) if i in apart_outs else jax.ShapeDtypeStruct(s, F32)
            for i, s in enumerate(outs)
        ],
        in_specs=places(len(ins), apart, pl.ANY),
        out_specs=places(len(outs), apart_outs, pltpu.HBM),
        scratch_shapes=[pltpu.VMEM(s, F32) if isinstance(s, tuple) else s for s in scratch],
        compiler_params=pltpu.CompilerParams(vmem_limit_bytes=limit * 1024 * 1024),
    )(*ins)


def lanes(shape):
    return lax.broadcasted_iota(jnp.int32, shape, len(shape) - 1)


def roll(value, shift, axis):
    size = value.shape[axis]
    shift = shift % size
    return value if shift == 0 else pltpu.roll(value, shift, axis)


def planes(lo, hi, body, step=16):
    whole = (hi - lo) // step

    def chunk(i, carry):
        for k in range(step):
            body(lo + i * step + k)
        return carry

    if whole == 1:
        chunk(0, 0)
    elif whole:
        lax.fori_loop(0, whole, chunk, 0)
    for p in range(lo + whole * step, hi):
        body(p)


def ahead_z(v):
    return jnp.concatenate([v[8:], roll(v[:8], -1, 0)], 0)


def behind_z(v):
    return jnp.concatenate([roll(v[24:], 1, 0), v[:24]], 0)


def neighbours(v_ref, fx, fy, fz, p):
    v = v_ref[p]
    s = fx[p] * v_ref[p + 1] + fx[p - 1] * v_ref[p - 1]
    cy = fy[p]
    s = s + cy * roll(v, -1, 1) + roll(cy * v, 1, 1)
    cz = fz[p]
    s = s + cz * ahead_z(v) + behind_z(cz * v)
    return v, s


def sweep(src, dst, f, g, fx, fy, fz, lo, hi, step=16):
    def body(p):
        v, s = neighbours(src, fx, fy, fz, p)
        dst[p] = (1.0 - OMEGA) * v + g[p] * (f[p] + s)

    planes(lo, hi, body, step)


def residual(src, dst, f, d, fx, fy, fz, lo, hi, step=16):
    def body(p):
        v, s = neighbours(src, fx, fy, fz, p)
        dst[p] = f[p] - d[p] * v + s

    planes(lo, hi, body, step)


def diagonal(extra, fx, fy, fz, p):
    cy, cz = fy[p], fz[p]
    return extra + fx[p] + fx[p - 1] + cy + roll(cy, 1, 1) + cz + behind_z(cz)


def scale_of(d):
    free = d > 0.0
    return jnp.where(free, OMEGA / jnp.where(free, d, 1.0), 0.0)


def selection(rows, cols, target, odd=False):
    row = lax.broadcasted_iota(jnp.int32, (rows, cols), 0)
    col = lax.broadcasted_iota(jnp.int32, (rows, cols), 1)
    hit = col == target(row)
    if odd:
        hit = hit & (row % 2 == 1)
    return hit.astype(F32)


def dot(a, matrix):
    matrix = matrix.astype(jnp.bfloat16)
    total = None
    for _ in range(3):
        part = a.astype(jnp.bfloat16)
        a = a - part.astype(F32)
        product = jnp.dot(part, matrix, preferred_element_type=F32)
        total = product if total is None else total + product
    return total


BEHIND = (0, H0, 2 * H0, 3 * H0 - 1)
AHEAD = (0, H0, 2 * H0 - 1, 3 * H0 - 2)


def fetch(pairs, sems):
    copies = [pltpu.make_async_copy(src, dst, sems.at[i]) for i, (src, dst) in enumerate(pairs)]
    for copy in copies:
        copy.start()
    return copies


def stage_kernel(
    in0, in1, in2, in3, own, to_right, to_left, labels, cond_x, cond_y, cond_z, sems
):
    copies = fetch(((in0, labels), (in1, cond_x), (in2, cond_y), (in3, cond_z)), sems)
    last_x = lax.axis_index("gx") == lax.axis_size("gx") - 1
    last_y = lax.axis_index("gy") == lax.axis_size("gy") - 1
    shape = (R0, 8, 128)
    row = lax.broadcasted_iota(jnp.int32, shape, 0)
    for a, ref in enumerate((labels, cond_x, cond_y, cond_z)):
        copies[a].wait()
        for b in range(4):
            value = jnp.stack([ref[4 * s + b].astype(F32) for s in range(8)])
            value = jnp.swapaxes(value, 0, 1)
            if a == 1:
                value = jnp.where(last_x & (row == R0 - 1), 0.0, value)
            if a == 2:
                value = jnp.where(last_y & (lanes(shape) == 127), 0.0, value)
            if a == 3 and b == 3:
                last = lax.broadcasted_iota(jnp.int32, shape, 1) == 7
                value = jnp.where(last, 0.0, value)
            part = slice(8 * b, 8 * b + 8)
            own[a, :, part] = value
            first, count = R0 - H0 + (a > 1), H0 - (a > 1)
            to_right[BEHIND[a] : BEHIND[a] + count, part] = value[first:]
            count = H0 - (a > 0)
            to_left[AHEAD[a] : AHEAD[a] + count, part] = value[:count]


def edge_kernel(own, behind, ahead, to_right, to_left):
    lane = lanes((NZ, 128))

    def plane(a, p):
        if p < H0:
            return behind[BEHIND[a] + p - (a > 1)] if p or a < 2 else None
        if p < H0 + R0:
            return own[a, p - H0]
        return ahead[AHEAD[a] + p - H0 - R0] if p < N0 - 1 or a == 0 else None

    for a in range(4):
        for c in range(GROUPS):
            right = left = jnp.zeros((NZ, 128), F32)
            for k in range(8):
                value = plane(a, 8 * c + k) if 8 * c + k < N0 else None
                if value is not None:
                    value = roll(value, 16 * k + 16, 1)
                    right = jnp.where(lane // 16 == k, value, right)
                    left = jnp.where(lane // 16 == (k + 1) % 8, value, left)
            to_right[a, c] = right
            to_left[a, c] = left


def down_kernel(
    own, behind, ahead, from_left, from_right,
    keep0, out_ops1, out_f1, own1, edge_f1, to_right, to_left, own3,
    ext, fx, fy, fz, d, g, f, va, vb, t, t1, ops1, d1, f1, va1, vb1, x2, y2, z2, e2, sems,
):
    lane = lanes((NZ, 128))
    main, pairs = pl.ds(0, 128), []
    for a in range(4):
        skip, count = int(a > 1), H0 - (a > 0)

        def place(lo, size, a=a):
            return ext.at[a, pl.ds(lo, size), :, main]

        pairs.append((behind.at[pl.ds(BEHIND[a], H0 - skip)], place(skip, H0 - skip)))
        pairs.append((own.at[a], place(H0, R0)))
        pairs.append((ahead.at[pl.ds(AHEAD[a], count)], place(H0 + R0, count)))
    copies = fetch(pairs, sems.at[pl.ds(8, 12)])
    for a in range(4):
        for c in range(GROUPS):
            left, right = from_left[a, c], from_right[a, c]
            for k in range(8):
                if 8 * c + k < N0:
                    both = jnp.where(lane // 16 == k, left, right)
                    ext[a, 8 * c + k, :, 128:256] = roll(both, -16 * k - 16, 1)
    for copy in copies:
        copy.wait()

    def cut(value, *kinds):
        for kind in kinds:
            value = jnp.where(kind, value, 0.0)
        return value

    fx[0] = cut(ext[1, 0], ext[0, 0] == 0.0, ext[0, 1] == 0.0)

    def operator0(p):
        label, label_up, label_down = ext[0, p], ext[0, p + 1], ext[0, p - 1]
        cx, cx_back, cy, cz = ext[1, p], ext[1, p - 1], ext[2, p], ext[3, p]
        cy_back, cz_back = roll(cy, 1, 1), behind_z(cz)
        y_up, y_down = roll(label, -1, 1), roll(label, 1, 1)
        z_up, z_down = ahead_z(label), behind_z(label)
        free = label == 0.0
        extra, rhs, diag = LEAK, 0.0, LEAK
        edges = (
            (cx, label_up), (cx_back, label_down), (cy, y_up), (cy_back, y_down), (cz, z_up), (cz_back, z_down),
        )
        for edge, across in edges:
            extra = extra + jnp.where(across == 0.0, 0.0, edge)
            rhs = rhs + jnp.where(across == 1.0, edge, 0.0)
            diag = diag + edge
        rhs, diag = cut(rhs, free), cut(diag, free)
        scale = scale_of(diag)
        fx[p] = cut(cx, free, label_up == 0.0)
        fy[p] = cut(cy, free, y_up == 0.0)
        fz[p] = cut(cz, free, z_up == 0.0)
        d[p], g[p], f[p] = diag, scale, rhs
        va[p] = scale * rhs
        t[p] = cut(extra, free)

    planes(1, N0 - 1, operator0, 4)
    src, dst = va, vb
    for s in range(NU - 1):
        sweep(src, dst, f, g, fx, fy, fz, 2 + s, N0 - 2 - s, N0 // 2 - 2 - s)
        src, dst = dst, src

    part = pl.ds(H0 - 4, 24)
    pairs = [(ref.at[part], keep0.at[i]) for i, ref in enumerate((src, f, g, fx, fy, fz))]
    copies = fetch(pairs, sems)

    def to1(row):
        return jnp.where(row < 192, row // 2, row // 2 - 128) + 32

    pick, pick_odd = selection(256, 128, to1), selection(256, 128, to1, True)

    def coarsen1(q):
        p = 2 * q + 1
        t1[0, q] = fx[p + 1]
        t1[1, q] = fy[p] + fy[p + 1]
        t1[2, q] = fz[p] + fz[p + 1]
        t1[3, q] = t[p] + t[p + 1]

    planes(0, N1, coarsen1, 4)
    for a in range(4):
        for c in range(0, N1, 4):
            value = t1[a, c : c + 4].reshape(4 * NZ, 256)
            ops1[a, c : c + 4] = dot(value, pick_odd if a == 1 else pick).reshape(4, NZ, 128)

    residual(src, dst, f, d, fx, fy, fz, H0 - 8, H0 + R0 + 8)
    f1[0:2] = jnp.zeros((2, NZ, 128), F32)
    f1[N1 - 2 : N1] = jnp.zeros((2, NZ, 128), F32)
    for c in range(2, N1 - 2, 4):
        value = jnp.stack([dst[2 * q + 1] + dst[2 * q + 2] for q in range(c, c + 4)])
        f1[c : c + 4] = dot(value.reshape(4 * NZ, 256), pick).reshape(4, NZ, 128)

    x1, y1, z1, e1, g1 = (ops1.at[a] for a in range(5))
    g1[0] = jnp.where(e1[0] > 0.0, 1.0, 0.0)

    def operator1(q):
        diag = diagonal(e1[q], x1, y1, z1, q)
        d1[q] = diag
        scale = scale_of(diag)
        g1[q] = scale
        va1[q] = scale * f1[q]

    planes(1, N1, operator1)
    copies += fetch(((ops1, out_ops1), (f1, out_f1)), sems.at[pl.ds(6, 2)])
    src, dst = va1, vb1
    for s in range(NU - 1):
        sweep(src, dst, f1, g1, x1, y1, z1, 3 + s, N1 - 3 - s)
        src, dst = dst, src
    own1[...] = src[H1 : H1 + 8]
    edge_f1[0] = f1[H1 + 4]
    edge_f1[1] = f1[H1 + 8 - 5]
    residual(src, dst, f1, d1, x1, y1, z1, H1, H1 + 8)

    half, half_odd = (selection(128, 128, lambda row: row // 2, odd) for odd in (False, True))
    q = [H1 + 2 * k for k in range(4)]
    f2 = dot(jnp.concatenate([dst[i] + dst[i + 1] for i in q]), half).reshape(4, NZ, 128)
    x2[...] = dot(jnp.concatenate([x1[i + 1] for i in [H1 - 2] + q]), half).reshape(5, NZ, 128)
    y2[...] = dot(jnp.concatenate([y1[i] + y1[i + 1] for i in q]), half_odd).reshape(4, NZ, 128)
    z2[...] = dot(jnp.concatenate([z1[i] + z1[i + 1] for i in q]), half).reshape(4, NZ, 128)
    e2[...] = dot(jnp.concatenate([e1[i] + e1[i + 1] for i in q]), half).reshape(4, NZ, 128)

    def around(x, x_back, y, z, extra):
        return extra + x + x_back + y + roll(y, 1, 1) + z + behind_z(z)

    for a in range(5):
        for h in range(2):
            pair = []
            for k in (2 * h, 2 * h + 1):
                if a == 4:
                    pair.append(around(x2[k + 1], x2[k], y2[k], z2[k], e2[k]))
                else:
                    pair.append((f2, x2[1:], y2, z2)[a][k])
            both = pair[0] + roll(pair[1], 64, 1)
            to_right[2 * a + h] = both
            to_left[2 * a + h] = both

    right = left = jnp.zeros((NZ, 128), F32)
    for k in range(8):
        here = lane // 8 == k
        right = jnp.where(here, roll(own1[k], 8 * k - 88, 1), right)
        left = jnp.where(here, roll(own1[k], 8 * k - 32, 1), left)
    to_right[10] = right
    to_left[10] = left

    x3 = dot(jnp.concatenate([x2[0], x2[2], x2[4]]), half).reshape(3, NZ, 128)
    y3 = dot(jnp.concatenate([y2[0] + y2[1], y2[2] + y2[3]]), half_odd).reshape(2, NZ, 128)
    z3 = dot(jnp.concatenate([z2[0] + z2[1], z2[2] + z2[3]]), half).reshape(2, NZ, 128)
    e3 = dot(jnp.concatenate([e2[0] + e2[1], e2[2] + e2[3]]), half).reshape(2, NZ, 128)
    total = jnp.zeros((NZ, 128), F32)
    for i in range(2):
        d3 = around(x3[i + 1], x3[i], y3[i], z3[i], e3[i])
        for a, value in enumerate((x3[i + 1], y3[i], z3[i], d3)):
            spot = 32 * a + 16 * i
            total = jnp.where(lane // 16 == spot // 16, roll(value, spot - 8, 1), total)
    for i in range(own3.shape[0]):
        own3[i] = total
    for copy in copies:
        copy.wait()


def join_kernel(own2, own1, edge_f1, left, right, joined2, joined1, to_right, to_left):
    lane = lanes((NZ, 128))
    low, high = lane % 64 < 16, lane % 64 >= 48
    for a in range(10):
        value = jnp.where(high, roll(right[a], 32, 1), own2[a])
        value = jnp.where(low, roll(left[a], -32, 1), value)
        joined2[a] = value
        to_right[a] = value
        to_left[a] = value
    low, high = lane // 8 == 3, lane // 8 == 12
    for k in range(8):
        value = jnp.where(low, roll(left[10], 24 - 8 * k, 1), own1[k])
        value = jnp.where(high, roll(right[10], 96 - 8 * k, 1), value)
        joined1[k] = value
        if k >= 8 - H1:
            to_right[10 + k - 8 + H1] = value
        if k < H1:
            to_left[10 + k] = value
    to_right[10 + H1] = edge_f1[1]
    to_left[10 + H1] = edge_f1[0]


def rows_of(value, odd):
    return roll(value, 64, 1) if odd else value


def middle_kernel(
    count, behind, own, ahead, ops3, message, f, fx, fy, fz, d, g, va, vb
):
    for j in range(12):
        source = (behind, own, ahead)[j // 4]
        for a, ref in enumerate((f, fx, fy, fz, d)):
            ref[j] = rows_of(source[2 * a + j % 4 // 2], j % 2)
        g[j] = scale_of(d[j])
        va[j] = g[j] * f[j]
    src, dst = va, vb
    for s in range(NU - 1):
        sweep(src, dst, f, g, fx, fy, fz, 1 + s, 11 - s)
        src, dst = dst, src
    residual(src, dst, f, d, fx, fy, fz, 4, 8)
    total = None
    for i in range(2):
        matrix = selection(
            128, 128, lambda row: jnp.where((row >= 16) & (row < 48), (row - 16) // 2 + 16 * i, -99)
        )
        part = dot(dst[4 + 2 * i] + dst[5 + 2 * i], matrix)
        total = part if total is None else total + part
    value = total[:8]
    for b in range(1, 4):
        value = value + roll(total[8 * b : 8 * b + 8], 32 * b, 1)
    message[count, 0:8] = value
    message[count, 8:] = jnp.zeros((NZ - 8, 128), F32)
    for i in range(count):
        message[i] = ops3[i]


def near_kernel(count, own, left, right, left_far, right_far, out):
    rhs = [ref[count, 0:8] for ref in (left_far, left, own, right, right_far)]
    for c in range(count):
        for s in range(5):
            out[c, s] = rhs[s]


PAD3 = 16


def turned(parts):
    slot = lanes(parts[0].shape) // 16
    rolled = [roll(part, 16 * s, 1) for s, part in enumerate(parts)]
    results = []
    for m in range(8):
        total = jnp.zeros_like(parts[0])
        for s, value in enumerate(rolled):
            total = jnp.where(slot == (m + s) % 8, value, total)
        results.append(roll(total, -16 * m, 1))
    return results


def spread3_kernel(count, own, left, right, left_far, right_far, out, ops3, sems):
    def unpack(i, carry):
        values = turned([ref[i] for ref in (left_far, left, own, right, right_far)])
        for m, value in enumerate(values):
            ops3[m // 2, 2 * i + m % 2] = scale_of(value) if m >= 6 else value
        return carry

    lax.fori_loop(0, count, unpack, 0)
    for copy in fetch(((ops3, out),), sems):
        copy.wait()


def solve_kernel(count, gathered, in_ops3, out, ops3, f3, va3, vb3, sems):
    lo, hi = PAD3, PAD3 + 2 * count
    inner = pl.ds(lo, 2 * count)
    copies = fetch([(in_ops3.at[a], ops3.at[a, inner]) for a in range(4)], sems)
    x3, y3, z3, g3 = (ops3.at[a] for a in range(4))
    for ref in (x3, y3, z3, g3, va3, vb3, f3):
        ref[0:lo] = jnp.zeros((PAD3, NZ, 128), F32)
        ref[hi : hi + PAD3] = jnp.zeros((PAD3, NZ, 128), F32)

    def unpack(i, carry):
        p = lo + 2 * i
        for m, value in enumerate(turned([gathered[i, s] for s in range(5)])):
            part = slice(8 * (m // 2), 8 * (m // 2) + 8)
            f3[p + m % 2, part] = value
        return carry

    lax.fori_loop(0, count, unpack, 0)
    for copy in copies:
        copy.wait()

    def first(p):
        va3[p] = g3[p] * f3[p]

    planes(lo, hi, first)

    def two(i, carry):
        sweep(va3, vb3, f3, g3, x3, y3, z3, lo, hi, 32)
        sweep(vb3, va3, f3, g3, x3, y3, z3, lo, hi, 32)
        return carry

    last = 11
    lax.fori_loop(0, (COARSE_SWEEPS - 1 - last) // 2, two, 0)
    start = lo + 2 * lax.axis_index("gx") - 4
    src, dst = va3, vb3
    for k in range(last - 1, -1, -1):
        for i in range(10 + 2 * k):
            p = start - k + i
            v, s = neighbours(src, x3, y3, z3, p)
            dst[p] = (1.0 - OMEGA) * v + g3[p] * (f3[p] + s)
        src, dst = dst, src
    out[...] = src[pl.ds(start, 10)]


def up_kernel(
    e3, all2, in_behind, in_ahead, in_joined1, in_f1, in_ops1, in_keep0,
    out,
    f2, x2, y2, z2, d2, g2, va2, vb2, f1, va1, vb1, va0, vb0,
    wide2, behind, ahead, joined1, ops1, keep0, sems,
):
    me, ends = lax.axis_index("gx"), lax.axis_size("gx") - 1
    pairs = [(all2.at[jnp.clip(me + n - 3, 0, ends)], wide2.at[n]) for n in range(7)]
    pairs += [(in_behind, behind), (in_ahead, ahead), (in_joined1, joined1)]
    pairs += [(in_f1, f1), (in_ops1, ops1), (in_keep0, keep0)]
    copies = fetch(pairs, sems)
    for n in range(7):
        copies[n].wait()
        inside = (me + n - 3 >= 0) & (me + n - 3 <= ends)
        for h in range(2):
            j = 4 * n + 2 * h - 2
            if 0 <= j < 24:
                for a, ref in enumerate((f2, x2, y2, z2, d2)):
                    value = jnp.where(inside, wide2[n, 2 * a + h], 0.0)
                    ref[j] = value
                    ref[j + 1] = roll(value, 64, 1)

    def operator2(j):
        g2[j] = scale_of(d2[j])
        va2[j] = g2[j] * f2[j]

    planes(0, 24, operator2, 24)
    src, dst = va2, vb2
    for s in range(NU - 1):
        sweep(src, dst, f2, g2, x2, y2, z2, 1 + s, 23 - s, 32)
        src, dst = dst, src
    col = lax.broadcasted_iota(jnp.int32, (128, 128), 1)
    row = lax.broadcasted_iota(jnp.int32, (128, 128), 0)
    spread = ((row == (col + 128 - 16) // 2 - 64 + 32) & (col < 64)).astype(F32)
    coarse = dot(e3[...].reshape(10 * NZ, 128), spread).reshape(10, NZ, 128)
    for r in range(-7, 11):
        j = r + 10
        src[j] = src[j] + jnp.where(g2[j] > 0.0, coarse[r // 2 + 4], 0.0)
    for s in range(NU):
        sweep(src, dst, f2, g2, x2, y2, z2, 4 + s, 20 - s, 32)
        src, dst = dst, src

    for copy in copies[7:12]:
        copy.wait()
    x1, y1, z1, g1 = ops1.at[0], ops1.at[1], ops1.at[2], ops1.at[4]
    f1[1] = behind[10 + H1]
    f1[N1 - 2] = ahead[10 + H1]
    spread = (row == (col - 32 + 128) // 2 - 64 + 16).astype(F32)
    coarse = dot(src[7:17].reshape(10 * NZ, 128), spread).reshape(10, NZ, 128)
    for q in range(N1):
        if q < H1:
            value = behind[10 + q]
        elif q < H1 + 8:
            value = joined1[q - H1]
        else:
            value = ahead[10 + q - H1 - 8]
        va1[q] = value + jnp.where(g1[q] > 0.0, coarse[q // 2], 0.0)
    src, dst = va1, vb1
    for s in range(NU):
        sweep(src, dst, f1, g1, x1, y1, z1, 1 + s, N1 - 1 - s, 32)
        src, dst = dst, src

    copies[12].wait()
    v0, f0, g0, x0, y0, z0 = (keep0.at[a] for a in range(6))
    col = lax.broadcasted_iota(jnp.int32, (128, 256), 1)
    row = lax.broadcasted_iota(jnp.int32, (128, 256), 0)
    spread = (row == jnp.where(col < 192, col // 2, col // 2 - 128) + 32).astype(F32)
    for c in range(0, 12, 4):
        coarse = dot(src[4 + c : 8 + c].reshape(4 * NZ, 128), spread).reshape(4, NZ, 256)
        for k in range(8):
            i = 2 * c + k
            va0[i] = v0[i] + jnp.where(g0[i] > 0.0, coarse[k // 2], 0.0)
    src, dst = va0, vb0
    for s in range(NU):
        sweep(src, dst, f0, g0, x0, y0, z0, 1 + s, 23 - s, 11 - s)
        src, dst = dst, src
    for b in range(4):
        value = jnp.swapaxes(src[4:20, 8 * b : 8 * b + 8, 0:128], 0, 1)
        for s in range(8):
            out[4 * s + b] = value[s]


def to_hbm(value):
    return pltpu.with_memory_space_constraint(value, pltpu.HBM)


def shift(value, axis, distance):
    count = lax.axis_size(axis)
    route = [(i, i + distance) for i in range(count) if 0 <= i + distance < count]
    return lax.ppermute(value, axis, route)


def body(labels, conduct_x, conduct_y, conduct_z):
    count = lax.axis_size("gx")
    side = (NZ, 128)
    wide = (N0, NZ, 256)
    fields = (labels, conduct_x, conduct_y, conduct_z)
    own, to_right, to_left = call(
        stage_kernel,
        [pltpu.with_memory_space_constraint(x, pltpu.HBM) for x in fields],
        [(4, R0, *side), (4 * H0 - 2, *side), (4 * H0 - 3, *side)],
        [pltpu.VMEM(x.shape, x.dtype) for x in fields] + [pltpu.SemaphoreType.DMA((4,))],
        apart=(0, 1, 2, 3),
    )
    behind = shift(to_right, "gx", 1)
    ahead = shift(to_left, "gx", -1)
    to_right, to_left = call(edge_kernel, (own, behind, ahead), [(4, GROUPS, *side)] * 2)
    from_left = shift(to_right, "gy", 1)
    from_right = shift(to_left, "gy", -1)
    keep0, ops1, f1, own1, edge_f1, to_right2, to_left2, own3 = call(
        down_kernel,
        (own, behind, ahead, from_left, from_right),
        [(6, 24, NZ, 256), (5, N1, *side), (N1, *side), (8, *side), (2, *side)]
        + [(11, *side)] * 2
        + [(count, *side)],
        [(4, N0, NZ, 256)]
        + [wide] * 9
        + [(4, N1, NZ, 256), (5, N1, *side)]
        + [(N1, *side)] * 4
        + [(5, *side)]
        + [(4, *side)] * 3
        + [pltpu.SemaphoreType.DMA((20,))],
        limit=28,
        apart=(0, 1, 2),
        apart_outs=(0, 1, 2),
    )
    left, right = shift(to_right2, "gy", 1), shift(to_left2, "gy", -1)
    all3 = lax.all_to_all(own3, "gx", 0, 0)
    joined2, joined1, to_right, to_left = call(
        join_kernel,
        (to_right2, own1, edge_f1, left, right),
        [(10, *side), (8, *side)] + [(11 + H1, *side)] * 2,
    )
    all2 = lax.all_gather(joined2, "gx")
    behind, ahead = shift(to_right, "gx", 1), shift(to_left, "gx", -1)
    (message,) = call(
        functools.partial(middle_kernel, count),
        (behind, joined2, ahead, all3),
        [(count + 1, *side)],
        [(12, *side)] * 8,
    )
    left, right = shift(message, "gy", 1), shift(message, "gy", -1)
    left_far, right_far = shift(left, "gy", 1), shift(right, "gy", -1)
    near = (message, left, right, left_far, right_far)
    (rhs3,) = call(functools.partial(near_kernel, count), near, [(count, 5, 8, 128)])
    rhs3 = lax.all_to_all(rhs3, "gx", 0, 0)
    rows3 = 2 * count + 2 * PAD3
    (ops3,) = call(
        functools.partial(spread3_kernel, count),
        near,
        [(4, 2 * count, *side)],
        [(4, 2 * count, *side), pltpu.SemaphoreType.DMA((1,))],
        apart_outs=(0,),
    )
    (e3,) = call(
        functools.partial(solve_kernel, count),
        (rhs3, pltpu.with_memory_space_constraint(ops3, pltpu.HBM)),
        [(10, *side)],
        [(4, rows3, *side)] + [(rows3, *side)] * 3 + [pltpu.SemaphoreType.DMA((4,))],
        limit=14,
        apart=(1,),
    )
    kept = (all2, behind, ahead, joined1, f1, ops1, keep0)
    in_hbm = [kept[i] if i in (1, 2, 3) else to_hbm(kept[i]) for i in range(7)]
    (out,) = call(
        up_kernel,
        (e3, *in_hbm),
        [(NZ, R0, 128)],
        [(24, *side)] * 8
        + [(N1, *side)] * 3
        + [(24, NZ, 256)] * 2
        + [(7, 10, *side), (11 + H1, *side), (11 + H1, *side), (8, *side)]
        + [(5, N1, *side), (6, 24, NZ, 256)]
        + [pltpu.SemaphoreType.DMA((13,))],
        limit=17,
        apart=range(1, 8),
    )
    return out


def solution(mesh):
    in_specs = (P(None, "gx", "gy"),) * 4
    out_specs = P(None, "gx", "gy")
    return jax.shard_map(body, mesh=mesh, in_specs=in_specs, out_specs=out_specs, check_vma=False)
```

```python
import functools

import jax
import jax.numpy as jnp
from jax import lax
from jax.experimental import pallas as pl
from jax.experimental.pallas import tpu as pltpu
from jax.sharding import PartitionSpec as P

NU = 4
COARSE_SWEEPS = 24
OMEGA = 0.8
LEAK = 0.005

NZ = 32
H0 = 13
R0 = 16
N0 = R0 + 2 * H0
GROUPS = (N0 + 7) // 8
H1 = 6
N1 = 8 + 2 * H1
F32 = jnp.float32


def spec():
    return pl.BlockSpec(memory_space=pltpu.VMEM)


def call(kernel, ins, outs, scratch=(), limit=10, apart=(), apart_outs=()):
    def places(count, left, space):
        return [pl.BlockSpec(memory_space=space) if i in left else spec() for i in range(count)]

    return pl.pallas_call(
        kernel,
        out_shape=[
            pltpu.HBM(s, F32) if i in apart_outs else jax.ShapeDtypeStruct(s, F32)
            for i, s in enumerate(outs)
        ],
        in_specs=places(len(ins), apart, pl.ANY),
        out_specs=places(len(outs), apart_outs, pltpu.HBM),
        scratch_shapes=[pltpu.VMEM(s, F32) if isinstance(s, tuple) else s for s in scratch],
        compiler_params=pltpu.CompilerParams(vmem_limit_bytes=limit * 1024 * 1024),
    )(*ins)


def lanes(shape):
    return lax.broadcasted_iota(jnp.int32, shape, len(shape) - 1)


def roll(value, shift, axis):
    size = value.shape[axis]
    shift = shift % size
    return value if shift == 0 else pltpu.roll(value, shift, axis)


def planes(lo, hi, body, step=16):
    whole = (hi - lo) // step

    def chunk(i, carry):
        for k in range(step):
            body(lo + i * step + k)
        return carry

    if whole == 1:
        chunk(0, 0)
    elif whole:
        lax.fori_loop(0, whole, chunk, 0)
    for p in range(lo + whole * step, hi):
        body(p)


def ahead_z(v):
    return jnp.concatenate([v[8:], roll(v[:8], -1, 0)], 0)


def behind_z(v):
    return jnp.concatenate([roll(v[24:], 1, 0), v[:24]], 0)


def neighbours(v_ref, fx, fy, fz, p):
    v = v_ref[p]
    s = fx[p] * v_ref[p + 1] + fx[p - 1] * v_ref[p - 1]
    cy = fy[p]
    s = s + cy * roll(v, -1, 1) + roll(cy * v, 1, 1)
    cz = fz[p]
    s = s + cz * ahead_z(v) + behind_z(cz * v)
    return v, s


def sweep(src, dst, f, g, fx, fy, fz, lo, hi, step=16):
    def body(p):
        v, s = neighbours(src, fx, fy, fz, p)
        dst[p] = (1.0 - OMEGA) * v + g[p] * (f[p] + s)

    planes(lo, hi, body, step)


def residual(src, dst, f, d, fx, fy, fz, lo, hi, step=16):
    def body(p):
        v, s = neighbours(src, fx, fy, fz, p)
        dst[p] = f[p] - d[p] * v + s

    planes(lo, hi, body, step)


def diagonal(extra, fx, fy, fz, p):
    cy, cz = fy[p], fz[p]
    return extra + fx[p] + fx[p - 1] + cy + roll(cy, 1, 1) + cz + behind_z(cz)


def scale_of(d):
    free = d > 0.0
    return jnp.where(free, OMEGA / jnp.where(free, d, 1.0), 0.0)


def selection(rows, cols, target, odd=False):
    row = lax.broadcasted_iota(jnp.int32, (rows, cols), 0)
    col = lax.broadcasted_iota(jnp.int32, (rows, cols), 1)
    hit = col == target(row)
    if odd:
        hit = hit & (row % 2 == 1)
    return hit.astype(F32)


def dot(a, matrix):
    matrix = matrix.astype(jnp.bfloat16)
    total = None
    for _ in range(3):
        part = a.astype(jnp.bfloat16)
        a = a - part.astype(F32)
        product = jnp.dot(part, matrix, preferred_element_type=F32)
        total = product if total is None else total + product
    return total


BEHIND = (0, H0, 2 * H0, 3 * H0 - 1)
AHEAD = (0, H0, 2 * H0 - 1, 3 * H0 - 2)


def fetch(pairs, sems):
    copies = [pltpu.make_async_copy(src, dst, sems.at[i]) for i, (src, dst) in enumerate(pairs)]
    for copy in copies:
        copy.start()
    return copies


def stage_kernel(
    in0, in1, in2, in3, own, to_right, to_left, labels, cond_x, cond_y, cond_z, sems
):
    copies = fetch(((in0, labels), (in1, cond_x), (in2, cond_y), (in3, cond_z)), sems)
    last_x = lax.axis_index("gx") == lax.axis_size("gx") - 1
    last_y = lax.axis_index("gy") == lax.axis_size("gy") - 1
    shape = (R0, 8, 128)
    row = lax.broadcasted_iota(jnp.int32, shape, 0)
    for a, ref in enumerate((labels, cond_x, cond_y, cond_z)):
        copies[a].wait()
        for b in range(4):
            value = jnp.stack([ref[4 * s + b].astype(F32) for s in range(8)])
            value = jnp.swapaxes(value, 0, 1)
            if a == 1:
                value = jnp.where(last_x & (row == R0 - 1), 0.0, value)
            if a == 2:
                value = jnp.where(last_y & (lanes(shape) == 127), 0.0, value)
            if a == 3 and b == 3:
                last = lax.broadcasted_iota(jnp.int32, shape, 1) == 7
                value = jnp.where(last, 0.0, value)
            part = slice(8 * b, 8 * b + 8)
            own[a, :, part] = value
            first, count = R0 - H0 + (a > 1), H0 - (a > 1)
            to_right[BEHIND[a] : BEHIND[a] + count, part] = value[first:]
            count = H0 - (a > 0)
            to_left[AHEAD[a] : AHEAD[a] + count, part] = value[:count]


def edge_kernel(own, behind, ahead, to_right, to_left):
    lane = lanes((NZ, 128))

    def plane(a, p):
        if p < H0:
            return behind[BEHIND[a] + p - (a > 1)] if p or a < 2 else None
        if p < H0 + R0:
            return own[a, p - H0]
        return ahead[AHEAD[a] + p - H0 - R0] if p < N0 - 1 or a == 0 else None

    for a in range(4):
        for c in range(GROUPS):
            right = left = jnp.zeros((NZ, 128), F32)
            for k in range(8):
                value = plane(a, 8 * c + k) if 8 * c + k < N0 else None
                if value is not None:
                    value = roll(value, 16 * k + 16, 1)
                    right = jnp.where(lane // 16 == k, value, right)
                    left = jnp.where(lane // 16 == (k + 1) % 8, value, left)
            to_right[a, c] = right
            to_left[a, c] = left


def down_kernel(
    own, behind, ahead, from_left, from_right,
    keep0, out_ops1, out_f1, own1, edge_f1, to_right, to_left, own3,
    ext, fx, fy, fz, d, g, f, va, vb, t, t1, ops1, d1, f1, va1, vb1, x2, y2, z2, e2, sems,
):
    lane = lanes((NZ, 128))
    main, pairs = pl.ds(0, 128), []
    for a in range(4):
        skip, count = int(a > 1), H0 - (a > 0)

        def place(lo, size, a=a):
            return ext.at[a, pl.ds(lo, size), :, main]

        pairs.append((behind.at[pl.ds(BEHIND[a], H0 - skip)], place(skip, H0 - skip)))
        pairs.append((own.at[a], place(H0, R0)))
        pairs.append((ahead.at[pl.ds(AHEAD[a], count)], place(H0 + R0, count)))
    copies = fetch(pairs, sems.at[pl.ds(8, 12)])
    for a in range(4):
        for c in range(GROUPS):
            left, right = from_left[a, c], from_right[a, c]
            for k in range(8):
                if 8 * c + k < N0:
                    both = jnp.where(lane // 16 == k, left, right)
                    ext[a, 8 * c + k, :, 128:256] = roll(both, -16 * k - 16, 1)
    for copy in copies:
        copy.wait()

    def cut(value, *kinds):
        for kind in kinds:
            value = jnp.where(kind, value, 0.0)
        return value

    fx[0] = cut(ext[1, 0], ext[0, 0] == 0.0, ext[0, 1] == 0.0)

    def operator0(p):
        label, label_up, label_down = ext[0, p], ext[0, p + 1], ext[0, p - 1]
        cx, cx_back, cy, cz = ext[1, p], ext[1, p - 1], ext[2, p], ext[3, p]
        cy_back, cz_back = roll(cy, 1, 1), behind_z(cz)
        y_up, y_down = roll(label, -1, 1), roll(label, 1, 1)
        z_up, z_down = ahead_z(label), behind_z(label)
        free = label == 0.0
        extra, rhs, diag = LEAK, 0.0, LEAK
        edges = (
            (cx, label_up), (cx_back, label_down), (cy, y_up), (cy_back, y_down), (cz, z_up), (cz_back, z_down),
        )
        for edge, across in edges:
            extra = extra + jnp.where(across == 0.0, 0.0, edge)
            rhs = rhs + jnp.where(across == 1.0, edge, 0.0)
            diag = diag + edge
        rhs, diag = cut(rhs, free), cut(diag, free)
        scale = scale_of(diag)
        fx[p] = cut(cx, free, label_up == 0.0)
        fy[p] = cut(cy, free, y_up == 0.0)
        fz[p] = cut(cz, free, z_up == 0.0)
        d[p], g[p], f[p] = diag, scale, rhs
        va[p] = scale * rhs
        t[p] = cut(extra, free)

    planes(1, N0 - 1, operator0, 4)
    src, dst = va, vb
    for s in range(NU - 1):
        sweep(src, dst, f, g, fx, fy, fz, 2 + s, N0 - 2 - s, N0 // 2 - 2 - s)
        src, dst = dst, src

    part = pl.ds(H0 - 4, 24)
    pairs = [(ref.at[part], keep0.at[i]) for i, ref in enumerate((src, f, g, fx, fy, fz))]
    copies = fetch(pairs, sems)

    def to1(row):
        return jnp.where(row < 192, row // 2, row // 2 - 128) + 32

    pick, pick_odd = selection(256, 128, to1), selection(256, 128, to1, True)

    def coarsen1(q):
        p = 2 * q + 1
        t1[0, q] = fx[p + 1]
        t1[1, q] = fy[p] + fy[p + 1]
        t1[2, q] = fz[p] + fz[p + 1]
        t1[3, q] = t[p] + t[p + 1]

    planes(0, N1, coarsen1, 4)
    for a in range(4):
        for c in range(0, N1, 4):
            value = t1[a, c : c + 4].reshape(4 * NZ, 256)
            ops1[a, c : c + 4] = dot(value, pick_odd if a == 1 else pick).reshape(4, NZ, 128)

    residual(src, dst, f, d, fx, fy, fz, H0 - 8, H0 + R0 + 8)
    f1[0:2] = jnp.zeros((2, NZ, 128), F32)
    f1[N1 - 2 : N1] = jnp.zeros((2, NZ, 128), F32)
    for c in range(2, N1 - 2, 4):
        value = jnp.stack([dst[2 * q + 1] + dst[2 * q + 2] for q in range(c, c + 4)])
        f1[c : c + 4] = dot(value.reshape(4 * NZ, 256), pick).reshape(4, NZ, 128)

    x1, y1, z1, e1, g1 = (ops1.at[a] for a in range(5))
    g1[0] = jnp.where(e1[0] > 0.0, 1.0, 0.0)

    def operator1(q):
        diag = diagonal(e1[q], x1, y1, z1, q)
        d1[q] = diag
        scale = scale_of(diag)
        g1[q] = scale
        va1[q] = scale * f1[q]

    planes(1, N1, operator1)
    copies += fetch(((ops1, out_ops1), (f1, out_f1)), sems.at[pl.ds(6, 2)])
    src, dst = va1, vb1
    for s in range(NU - 1):
        sweep(src, dst, f1, g1, x1, y1, z1, 3 + s, N1 - 3 - s)
        src, dst = dst, src
    own1[...] = src[H1 : H1 + 8]
    edge_f1[0] = f1[H1 + 4]
    edge_f1[1] = f1[H1 + 8 - 5]
    residual(src, dst, f1, d1, x1, y1, z1, H1, H1 + 8)

    half, half_odd = (selection(128, 128, lambda row: row // 2, odd) for odd in (False, True))
    q = [H1 + 2 * k for k in range(4)]
    f2 = dot(jnp.concatenate([dst[i] + dst[i + 1] for i in q]), half).reshape(4, NZ, 128)
    x2[...] = dot(jnp.concatenate([x1[i + 1] for i in [H1 - 2] + q]), half).reshape(5, NZ, 128)
    y2[...] = dot(jnp.concatenate([y1[i] + y1[i + 1] for i in q]), half_odd).reshape(4, NZ, 128)
    z2[...] = dot(jnp.concatenate([z1[i] + z1[i + 1] for i in q]), half).reshape(4, NZ, 128)
    e2[...] = dot(jnp.concatenate([e1[i] + e1[i + 1] for i in q]), half).reshape(4, NZ, 128)

    def around(x, x_back, y, z, extra):
        return extra + x + x_back + y + roll(y, 1, 1) + z + behind_z(z)

    for a in range(5):
        for h in range(2):
            pair = []
            for k in (2 * h, 2 * h + 1):
                if a == 4:
                    pair.append(around(x2[k + 1], x2[k], y2[k], z2[k], e2[k]))
                else:
                    pair.append((f2, x2[1:], y2, z2)[a][k])
            both = pair[0] + roll(pair[1], 64, 1)
            to_right[2 * a + h] = both
            to_left[2 * a + h] = both

    right = left = jnp.zeros((NZ, 128), F32)
    for k in range(8):
        here = lane // 8 == k
        right = jnp.where(here, roll(own1[k], 8 * k - 88, 1), right)
        left = jnp.where(here, roll(own1[k], 8 * k - 32, 1), left)
    to_right[10] = right
    to_left[10] = left

    x3 = dot(jnp.concatenate([x2[0], x2[2], x2[4]]), half).reshape(3, NZ, 128)
    y3 = dot(jnp.concatenate([y2[0] + y2[1], y2[2] + y2[3]]), half_odd).reshape(2, NZ, 128)
    z3 = dot(jnp.concatenate([z2[0] + z2[1], z2[2] + z2[3]]), half).reshape(2, NZ, 128)
    e3 = dot(jnp.concatenate([e2[0] + e2[1], e2[2] + e2[3]]), half).reshape(2, NZ, 128)
    total = jnp.zeros((NZ, 128), F32)
    for i in range(2):
        d3 = around(x3[i + 1], x3[i], y3[i], z3[i], e3[i])
        for a, value in enumerate((x3[i + 1], y3[i], z3[i], d3)):
            spot = 32 * a + 16 * i
            total = jnp.where(lane // 16 == spot // 16, roll(value, spot - 8, 1), total)
    for i in range(own3.shape[0]):
        own3[i] = total
    for copy in copies:
        copy.wait()


def join_kernel(own2, own1, edge_f1, left, right, joined2, joined1, to_right, to_left):
    lane = lanes((NZ, 128))
    low, high = lane % 64 < 16, lane % 64 >= 48
    for a in range(10):
        value = jnp.where(high, roll(right[a], 32, 1), own2[a])
        value = jnp.where(low, roll(left[a], -32, 1), value)
        joined2[a] = value
        to_right[a] = value
        to_left[a] = value
    low, high = lane // 8 == 3, lane // 8 == 12
    for k in range(8):
        value = jnp.where(low, roll(left[10], 24 - 8 * k, 1), own1[k])
        value = jnp.where(high, roll(right[10], 96 - 8 * k, 1), value)
        joined1[k] = value
        if k >= 8 - H1:
            to_right[10 + k - 8 + H1] = value
        if k < H1:
            to_left[10 + k] = value
    to_right[10 + H1] = edge_f1[1]
    to_left[10 + H1] = edge_f1[0]


def rows_of(value, odd):
    return roll(value, 64, 1) if odd else value


def middle_kernel(
    count, behind, own, ahead, ops3, message, further, nearer, f, fx, fy, fz, d, g, va, vb
):
    for j in range(12):
        source = (behind, own, ahead)[j // 4]
        for a, ref in enumerate((f, fx, fy, fz, d)):
            ref[j] = rows_of(source[2 * a + j % 4 // 2], j % 2)
        g[j] = scale_of(d[j])
        va[j] = g[j] * f[j]
    src, dst = va, vb
    for s in range(NU - 1):
        sweep(src, dst, f, g, fx, fy, fz, 1 + s, 11 - s)
        src, dst = dst, src
    residual(src, dst, f, d, fx, fy, fz, 4, 8)
    total = None
    for i in range(2):
        matrix = selection(
            128, 128, lambda row: jnp.where((row >= 16) & (row < 48), (row - 16) // 2 + 16 * i, -99)
        )
        part = dot(dst[4 + 2 * i] + dst[5 + 2 * i], matrix)
        total = part if total is None else total + part
    value = total[:8]
    for b in range(1, 4):
        value = value + roll(total[8 * b : 8 * b + 8], 32 * b, 1)
    message[count, 0:8] = value
    message[count, 8:] = jnp.zeros((NZ - 8, 128), F32)
    for i in range(count):
        message[i] = ops3[i]
    further[...] = behind[0:10]
    nearer[...] = ahead[0:10]


def near_kernel(count, own, left, right, left_far, right_far, out):
    rhs = [ref[count, 0:8] for ref in (left_far, left, own, right, right_far)]
    for c in range(count):
        for s in range(5):
            out[c, s] = rhs[s]


PAD3 = 16


def turned(parts):
    slot = lanes(parts[0].shape) // 16
    rolled = [roll(part, 16 * s, 1) for s, part in enumerate(parts)]
    results = []
    for m in range(8):
        total = jnp.zeros_like(parts[0])
        for s, value in enumerate(rolled):
            total = jnp.where(slot == (m + s) % 8, value, total)
        results.append(roll(total, -16 * m, 1))
    return results


def spread3_kernel(count, own, left, right, left_far, right_far, out, ops3, sems):
    def unpack(i):
        values = turned([ref[i] for ref in (left_far, left, own, right, right_far)])
        for m, value in enumerate(values):
            ops3[m // 2, 2 * i + m % 2] = scale_of(value) if m >= 6 else value

    planes(0, count, unpack, 4)
    for copy in fetch(((ops3, out),), sems):
        copy.wait()


def solve_kernel(count, gathered, in_ops3, out, ops3, f3, va3, vb3, sems):
    lo, hi = PAD3, PAD3 + 2 * count
    inner = pl.ds(lo, 2 * count)
    copies = fetch([(in_ops3.at[a], ops3.at[a, inner]) for a in range(4)], sems)
    x3, y3, z3, g3 = (ops3.at[a] for a in range(4))
    for ref in (x3, y3, z3, g3, va3, vb3, f3):
        ref[0:lo] = jnp.zeros((PAD3, NZ, 128), F32)
        ref[hi : hi + PAD3] = jnp.zeros((PAD3, NZ, 128), F32)

    def unpack(i):
        p = lo + 2 * i
        for m, value in enumerate(turned([gathered[i, s] for s in range(5)])):
            part = slice(8 * (m // 2), 8 * (m // 2) + 8)
            f3[p + m % 2, part] = value

    planes(0, count, unpack, 8)
    for copy in copies:
        copy.wait()

    def first(p):
        va3[p] = g3[p] * f3[p]

    planes(lo, hi, first)

    def two(i, carry):
        sweep(va3, vb3, f3, g3, x3, y3, z3, lo, hi, 32)
        sweep(vb3, va3, f3, g3, x3, y3, z3, lo, hi, 32)
        return carry

    last = 11
    lax.fori_loop(0, (COARSE_SWEEPS - 1 - last) // 2, two, 0)
    start = lo + 2 * lax.axis_index("gx") - 4
    src, dst = va3, vb3
    for k in range(last - 1, -1, -1):
        for i in range(10 + 2 * k):
            p = start - k + i
            v, s = neighbours(src, x3, y3, z3, p)
            dst[p] = (1.0 - OMEGA) * v + g3[p] * (f3[p] + s)
        src, dst = dst, src
    out[...] = src[pl.ds(start, 10)]


def up_kernel(
    e3, in_behind3, in_behind2, in_behind, in_own, in_ahead, in_ahead2, in_ahead3,
    in_joined1, in_f1, in_ops1, in_keep0,
    out,
    f2, x2, y2, z2, d2, g2, va2, vb2, f1, va1, vb1, va0, vb0,
    behind3, behind2, behind, own, ahead, ahead2, ahead3, joined1, ops1, keep0, sems,
):
    pairs = [
        (in_behind3, behind3), (in_behind2, behind2), (in_behind, behind), (in_own, own),
        (in_ahead, ahead), (in_ahead2, ahead2), (in_ahead3, ahead3),
        (in_joined1, joined1), (in_f1, f1), (in_ops1, ops1), (in_keep0, keep0),
    ]
    copies = fetch(pairs, sems)
    sources = [(behind3, 1)]
    sources += [(ref, h) for ref in (behind2, behind, own, ahead, ahead2) for h in range(2)]
    sources += [(ahead3, 0)]
    for n, (source, h) in enumerate(sources):
        if n % 2 or n == 0:
            copies[(n + 1) // 2].wait()
        for a, ref in enumerate((f2, x2, y2, z2, d2)):
            value = source[2 * a + h]
            ref[2 * n] = value
            ref[2 * n + 1] = roll(value, 64, 1)

    def operator2(j):
        g2[j] = scale_of(d2[j])
        va2[j] = g2[j] * f2[j]

    planes(0, 24, operator2, 24)
    src, dst = va2, vb2
    for s in range(NU - 1):
        sweep(src, dst, f2, g2, x2, y2, z2, 1 + s, 23 - s, 32)
        src, dst = dst, src
    col = lax.broadcasted_iota(jnp.int32, (128, 128), 1)
    row = lax.broadcasted_iota(jnp.int32, (128, 128), 0)
    spread = ((row == (col + 128 - 16) // 2 - 64 + 32) & (col < 64)).astype(F32)
    coarse = dot(e3[...].reshape(10 * NZ, 128), spread).reshape(10, NZ, 128)
    for r in range(-7, 11):
        j = r + 10
        src[j] = src[j] + jnp.where(g2[j] > 0.0, coarse[r // 2 + 4], 0.0)
    for s in range(NU):
        sweep(src, dst, f2, g2, x2, y2, z2, 4 + s, 20 - s, 32)
        src, dst = dst, src

    for copy in copies[7:10]:
        copy.wait()
    x1, y1, z1, g1 = ops1.at[0], ops1.at[1], ops1.at[2], ops1.at[4]
    f1[1] = behind[10 + H1]
    f1[N1 - 2] = ahead[10 + H1]
    spread = (row == (col - 32 + 128) // 2 - 64 + 16).astype(F32)
    coarse = dot(src[7:17].reshape(10 * NZ, 128), spread).reshape(10, NZ, 128)
    for q in range(N1):
        if q < H1:
            value = behind[10 + q]
        elif q < H1 + 8:
            value = joined1[q - H1]
        else:
            value = ahead[10 + q - H1 - 8]
        va1[q] = value + jnp.where(g1[q] > 0.0, coarse[q // 2], 0.0)
    src, dst = va1, vb1
    for s in range(NU):
        sweep(src, dst, f1, g1, x1, y1, z1, 1 + s, N1 - 1 - s, 32)
        src, dst = dst, src

    copies[10].wait()
    v0, f0, g0, x0, y0, z0 = (keep0.at[a] for a in range(6))
    col = lax.broadcasted_iota(jnp.int32, (128, 256), 1)
    row = lax.broadcasted_iota(jnp.int32, (128, 256), 0)
    spread = (row == jnp.where(col < 192, col // 2, col // 2 - 128) + 32).astype(F32)
    for c in range(0, 12, 4):
        coarse = dot(src[4 + c : 8 + c].reshape(4 * NZ, 128), spread).reshape(4, NZ, 256)
        for k in range(8):
            i = 2 * c + k
            va0[i] = v0[i] + jnp.where(g0[i] > 0.0, coarse[k // 2], 0.0)
    src, dst = va0, vb0
    for s in range(NU):
        sweep(src, dst, f0, g0, x0, y0, z0, 1 + s, 23 - s, 11 - s)
        src, dst = dst, src
    for b in range(4):
        value = jnp.swapaxes(src[4:20, 8 * b : 8 * b + 8, 0:128], 0, 1)
        for s in range(8):
            out[4 * s + b] = value[s]


def shift(value, axis, distance):
    count = lax.axis_size(axis)
    route = [(i, i + distance) for i in range(count) if 0 <= i + distance < count]
    return lax.ppermute(value, axis, route)


def body(labels, conduct_x, conduct_y, conduct_z):
    count = lax.axis_size("gx")
    side = (NZ, 128)
    wide = (N0, NZ, 256)
    fields = (labels, conduct_x, conduct_y, conduct_z)
    own, to_right, to_left = call(
        stage_kernel,
        [pltpu.with_memory_space_constraint(x, pltpu.HBM) for x in fields],
        [(4, R0, *side), (4 * H0 - 2, *side), (4 * H0 - 3, *side)],
        [pltpu.VMEM(x.shape, x.dtype) for x in fields] + [pltpu.SemaphoreType.DMA((4,))],
        apart=(0, 1, 2, 3),
    )
    behind = shift(to_right, "gx", 1)
    ahead = shift(to_left, "gx", -1)
    to_right, to_left = call(edge_kernel, (own, behind, ahead), [(4, GROUPS, *side)] * 2)
    from_left = shift(to_right, "gy", 1)
    from_right = shift(to_left, "gy", -1)
    keep0, ops1, f1, own1, edge_f1, to_right2, to_left2, own3 = call(
        down_kernel,
        (own, behind, ahead, from_left, from_right),
        [(6, 24, NZ, 256), (5, N1, *side), (N1, *side), (8, *side), (2, *side)]
        + [(11, *side)] * 2
        + [(count, *side)],
        [(4, N0, NZ, 256)]
        + [wide] * 9
        + [(4, N1, NZ, 256), (5, N1, *side)]
        + [(N1, *side)] * 4
        + [(5, *side)]
        + [(4, *side)] * 3
        + [pltpu.SemaphoreType.DMA((20,))],
        limit=28,
        apart=(0, 1, 2),
        apart_outs=(0, 1, 2),
    )
    left, right = shift(to_right2, "gy", 1), shift(to_left2, "gy", -1)
    all3 = lax.all_to_all(own3, "gx", 0, 0)
    joined2, joined1, to_right, to_left = call(
        join_kernel,
        (to_right2, own1, edge_f1, left, right),
        [(10, *side), (8, *side)] + [(11 + H1, *side)] * 2,
    )
    behind, ahead = shift(to_right, "gx", 1), shift(to_left, "gx", -1)
    message, further, nearer = call(
        functools.partial(middle_kernel, count),
        (behind, joined2, ahead, all3),
        [(count + 1, *side)] + [(10, *side)] * 2,
        [(12, *side)] * 8,
    )
    left, right = shift(message, "gy", 1), shift(message, "gy", -1)
    behind2, ahead2 = shift(further, "gx", 1), shift(nearer, "gx", -1)
    left_far, right_far = shift(left, "gy", 1), shift(right, "gy", -1)
    near = (message, left, right, left_far, right_far)
    (rhs3,) = call(functools.partial(near_kernel, count), near, [(count, 5, 8, 128)])
    rhs3 = lax.all_to_all(rhs3, "gx", 0, 0)
    behind3, ahead3 = shift(behind2, "gx", 1), shift(ahead2, "gx", -1)
    rows3 = 2 * count + 2 * PAD3
    (ops3,) = call(
        functools.partial(spread3_kernel, count),
        near,
        [(4, 2 * count, *side)],
        [(4, 2 * count, *side), pltpu.SemaphoreType.DMA((1,))],
        apart_outs=(0,),
    )
    (e3,) = call(
        functools.partial(solve_kernel, count),
        (rhs3, pltpu.with_memory_space_constraint(ops3, pltpu.HBM)),
        [(10, *side)],
        [(4, rows3, *side)] + [(rows3, *side)] * 3 + [pltpu.SemaphoreType.DMA((4,))],
        limit=14,
        apart=(1,),
    )
    keep0, ops1, f1 = (pltpu.with_memory_space_constraint(x, pltpu.HBM) for x in (keep0, ops1, f1))
    (out,) = call(
        up_kernel,
        (e3, behind3, behind2, behind, joined2, ahead, ahead2, ahead3, joined1, f1, ops1, keep0),
        [(NZ, R0, 128)],
        [(24, *side)] * 8
        + [(N1, *side)] * 3
        + [(24, NZ, 256)] * 2
        + [(10, *side), (10, *side), (11 + H1, *side), (10, *side)]
        + [(11 + H1, *side), (10, *side), (10, *side), (8, *side)]
        + [(5, N1, *side), (6, 24, NZ, 256)]
        + [pltpu.SemaphoreType.DMA((11,))],
        limit=17,
        apart=range(1, 12),
    )
    return out


def solution(mesh):
    in_specs = (P(None, "gx", "gy"),) * 4
    out_specs = P(None, "gx", "gy")
    return jax.shard_map(body, mesh=mesh, in_specs=in_specs, out_specs=out_specs, check_vma=False)
```

```python
import functools

import jax
import jax.numpy as jnp
from jax import lax
from jax.experimental import pallas as pl
from jax.experimental.pallas import tpu as pltpu
from jax.sharding import PartitionSpec as P

NU = 4
COARSE_SWEEPS = 24
OMEGA = 0.8
LEAK = 0.005

NZ = 32
H0 = 13
R0 = 16
N0 = R0 + 2 * H0
GROUPS = (N0 + 7) // 8
H1 = 6
N1 = 8 + 2 * H1
F32 = jnp.float32


def spec():
    return pl.BlockSpec(memory_space=pltpu.VMEM)


def call(kernel, ins, outs, scratch=(), limit=10, apart=(), apart_outs=()):
    def places(count, left, space):
        return [pl.BlockSpec(memory_space=space) if i in left else spec() for i in range(count)]

    return pl.pallas_call(
        kernel,
        out_shape=[
            pltpu.HBM(s, F32) if i in apart_outs else jax.ShapeDtypeStruct(s, F32)
            for i, s in enumerate(outs)
        ],
        in_specs=places(len(ins), apart, pl.ANY),
        out_specs=places(len(outs), apart_outs, pltpu.HBM),
        scratch_shapes=[pltpu.VMEM(s, F32) if isinstance(s, tuple) else s for s in scratch],
        compiler_params=pltpu.CompilerParams(vmem_limit_bytes=limit * 1024 * 1024),
    )(*ins)


def lanes(shape):
    return lax.broadcasted_iota(jnp.int32, shape, len(shape) - 1)


def roll(value, shift, axis):
    size = value.shape[axis]
    shift = shift % size
    return value if shift == 0 else pltpu.roll(value, shift, axis)


def planes(lo, hi, body, step=16):
    whole = (hi - lo) // step

    def chunk(i, carry):
        for k in range(step):
            body(lo + i * step + k)
        return carry

    if whole == 1:
        chunk(0, 0)
    elif whole:
        lax.fori_loop(0, whole, chunk, 0)
    for p in range(lo + whole * step, hi):
        body(p)


def ahead_z(v):
    return jnp.concatenate([v[8:], roll(v[:8], -1, 0)], 0)


def behind_z(v):
    return jnp.concatenate([roll(v[24:], 1, 0), v[:24]], 0)


def neighbours(v_ref, fx, fy, fz, p):
    v = v_ref[p]
    s = fx[p] * v_ref[p + 1] + fx[p - 1] * v_ref[p - 1]
    cy = fy[p]
    s = s + cy * roll(v, -1, 1) + roll(cy * v, 1, 1)
    cz = fz[p]
    s = s + cz * ahead_z(v) + behind_z(cz * v)
    return v, s


def sweep(src, dst, f, g, fx, fy, fz, lo, hi, step=16):
    def body(p):
        v, s = neighbours(src, fx, fy, fz, p)
        dst[p] = (1.0 - OMEGA) * v + g[p] * (f[p] + s)

    planes(lo, hi, body, step)


def residual(src, dst, f, d, fx, fy, fz, lo, hi, step=16):
    def body(p):
        v, s = neighbours(src, fx, fy, fz, p)
        dst[p] = f[p] - d[p] * v + s

    planes(lo, hi, body, step)


def diagonal(extra, fx, fy, fz, p):
    cy, cz = fy[p], fz[p]
    return extra + fx[p] + fx[p - 1] + cy + roll(cy, 1, 1) + cz + behind_z(cz)


def scale_of(d):
    free = d > 0.0
    return jnp.where(free, OMEGA / jnp.where(free, d, 1.0), 0.0)


def selection(rows, cols, target, odd=False):
    row = lax.broadcasted_iota(jnp.int32, (rows, cols), 0)
    col = lax.broadcasted_iota(jnp.int32, (rows, cols), 1)
    hit = col == target(row)
    if odd:
        hit = hit & (row % 2 == 1)
    return hit.astype(F32)


def dot(a, matrix):
    matrix = matrix.astype(jnp.bfloat16)
    total = None
    for _ in range(3):
        part = a.astype(jnp.bfloat16)
        a = a - part.astype(F32)
        product = jnp.dot(part, matrix, preferred_element_type=F32)
        total = product if total is None else total + product
    return total


BEHIND = (0, H0, 2 * H0, 3 * H0 - 1)
AHEAD = (0, H0, 2 * H0 - 1, 3 * H0 - 2)


def fetch(pairs, sems):
    copies = [pltpu.make_async_copy(src, dst, sems.at[i]) for i, (src, dst) in enumerate(pairs)]
    for copy in copies:
        copy.start()
    return copies


def stage_kernel(
    in0, in1, in2, in3, own, to_right, to_left, labels, cond_x, cond_y, cond_z, sems
):
    copies = fetch(((in0, labels), (in1, cond_x), (in2, cond_y), (in3, cond_z)), sems)
    last_x = lax.axis_index("gx") == lax.axis_size("gx") - 1
    last_y = lax.axis_index("gy") == lax.axis_size("gy") - 1
    shape = (R0, 8, 128)
    row = lax.broadcasted_iota(jnp.int32, shape, 0)
    for a, ref in enumerate((labels, cond_x, cond_y, cond_z)):
        copies[a].wait()
        for b in range(4):
            value = jnp.stack([ref[4 * s + b].astype(F32) for s in range(8)])
            value = jnp.swapaxes(value, 0, 1)
            if a == 1:
                value = jnp.where(last_x & (row == R0 - 1), 0.0, value)
            if a == 2:
                value = jnp.where(last_y & (lanes(shape) == 127), 0.0, value)
            if a == 3 and b == 3:
                last = lax.broadcasted_iota(jnp.int32, shape, 1) == 7
                value = jnp.where(last, 0.0, value)
            part = slice(8 * b, 8 * b + 8)
            own[a, :, part] = value
            first, count = R0 - H0 + (a > 1), H0 - (a > 1)
            to_right[BEHIND[a] : BEHIND[a] + count, part] = value[first:]
            count = H0 - (a > 0)
            to_left[AHEAD[a] : AHEAD[a] + count, part] = value[:count]


def edge_kernel(own, behind, ahead, to_right, to_left):
    lane = lanes((NZ, 128))

    def plane(a, p):
        if p < H0:
            return behind[BEHIND[a] + p - (a > 1)] if p or a < 2 else None
        if p < H0 + R0:
            return own[a, p - H0]
        return ahead[AHEAD[a] + p - H0 - R0] if p < N0 - 1 or a == 0 else None

    for a in range(4):
        for c in range(GROUPS):
            right = left = jnp.zeros((NZ, 128), F32)
            for k in range(8):
                value = plane(a, 8 * c + k) if 8 * c + k < N0 else None
                if value is not None:
                    value = roll(value, 16 * k + 16, 1)
                    right = jnp.where(lane // 16 == k, value, right)
                    left = jnp.where(lane // 16 == (k + 1) % 8, value, left)
            to_right[a, c] = right
            to_left[a, c] = left


def down_kernel(
    own, behind, ahead, from_left, from_right,
    keep0, out_ops1, out_f1, own1, edge_f1, to_right, to_left, own3,
    ext, fx, fy, fz, d, g, f, va, vb, t, t1, ops1, d1, f1, va1, vb1, x2, y2, z2, e2, sems,
):
    lane = lanes((NZ, 128))
    main, pairs = pl.ds(0, 128), []
    for a in range(4):
        skip, count = int(a > 1), H0 - (a > 0)

        def place(lo, size, a=a):
            return ext.at[a, pl.ds(lo, size), :, main]

        pairs.append((behind.at[pl.ds(BEHIND[a], H0 - skip)], place(skip, H0 - skip)))
        pairs.append((own.at[a], place(H0, R0)))
        pairs.append((ahead.at[pl.ds(AHEAD[a], count)], place(H0 + R0, count)))
    copies = fetch(pairs, sems.at[pl.ds(8, 12)])
    for a in range(4):
        for c in range(GROUPS):
            left, right = from_left[a, c], from_right[a, c]
            for k in range(8):
                if 8 * c + k < N0:
                    both = jnp.where(lane // 16 == k, left, right)
                    ext[a, 8 * c + k, :, 128:256] = roll(both, -16 * k - 16, 1)
    for copy in copies:
        copy.wait()

    def cut(value, *kinds):
        for kind in kinds:
            value = jnp.where(kind, value, 0.0)
        return value

    fx[0] = cut(ext[1, 0], ext[0, 0] == 0.0, ext[0, 1] == 0.0)

    def operator0(p):
        label, label_up, label_down = ext[0, p], ext[0, p + 1], ext[0, p - 1]
        cx, cx_back, cy, cz = ext[1, p], ext[1, p - 1], ext[2, p], ext[3, p]
        cy_back, cz_back = roll(cy, 1, 1), behind_z(cz)
        y_up, y_down = roll(label, -1, 1), roll(label, 1, 1)
        z_up, z_down = ahead_z(label), behind_z(label)
        free = label == 0.0
        extra, rhs, diag = LEAK, 0.0, LEAK
        edges = (
            (cx, label_up), (cx_back, label_down), (cy, y_up), (cy_back, y_down), (cz, z_up), (cz_back, z_down),
        )
        for edge, across in edges:
            extra = extra + jnp.where(across == 0.0, 0.0, edge)
            rhs = rhs + jnp.where(across == 1.0, edge, 0.0)
            diag = diag + edge
        rhs, diag = cut(rhs, free), cut(diag, free)
        scale = scale_of(diag)
        fx[p] = cut(cx, free, label_up == 0.0)
        fy[p] = cut(cy, free, y_up == 0.0)
        fz[p] = cut(cz, free, z_up == 0.0)
        d[p], g[p], f[p] = diag, scale, rhs
        va[p] = scale * rhs
        t[p] = cut(extra, free)

    planes(1, N0 - 1, operator0, 8)
    src, dst = va, vb
    for s in range(NU - 1):
        sweep(src, dst, f, g, fx, fy, fz, 2 + s, N0 - 2 - s, N0 // 2 - 2 - s)
        src, dst = dst, src

    part = pl.ds(H0 - 4, 24)
    pairs = [(ref.at[part], keep0.at[i]) for i, ref in enumerate((src, f, g, fx, fy, fz))]
    copies = fetch(pairs, sems)

    def to1(row):
        return jnp.where(row < 192, row // 2, row // 2 - 128) + 32

    pick, pick_odd = selection(256, 128, to1), selection(256, 128, to1, True)

    def coarsen1(q):
        p = 2 * q + 1
        t1[0, q] = fx[p + 1]
        t1[1, q] = fy[p] + fy[p + 1]
        t1[2, q] = fz[p] + fz[p + 1]
        t1[3, q] = t[p] + t[p + 1]

    planes(0, N1, coarsen1, 10)
    for a in range(4):
        for c in range(0, N1, 4):
            value = t1[a, c : c + 4].reshape(4 * NZ, 256)
            ops1[a, c : c + 4] = dot(value, pick_odd if a == 1 else pick).reshape(4, NZ, 128)

    residual(src, dst, f, d, fx, fy, fz, H0 - 8, H0 + R0 + 8)
    f1[0:2] = jnp.zeros((2, NZ, 128), F32)
    f1[N1 - 2 : N1] = jnp.zeros((2, NZ, 128), F32)
    for c in range(2, N1 - 2, 4):
        value = jnp.stack([dst[2 * q + 1] + dst[2 * q + 2] for q in range(c, c + 4)])
        f1[c : c + 4] = dot(value.reshape(4 * NZ, 256), pick).reshape(4, NZ, 128)

    x1, y1, z1, e1, g1 = (ops1.at[a] for a in range(5))
    g1[0] = jnp.where(e1[0] > 0.0, 1.0, 0.0)

    def operator1(q):
        diag = diagonal(e1[q], x1, y1, z1, q)
        d1[q] = diag
        scale = scale_of(diag)
        g1[q] = scale
        va1[q] = scale * f1[q]

    planes(1, N1, operator1)
    copies += fetch(((ops1, out_ops1), (f1, out_f1)), sems.at[pl.ds(6, 2)])
    src, dst = va1, vb1
    for s in range(NU - 1):
        sweep(src, dst, f1, g1, x1, y1, z1, 3 + s, N1 - 3 - s)
        src, dst = dst, src
    own1[...] = src[H1 : H1 + 8]
    edge_f1[0] = f1[H1 + 4]
    edge_f1[1] = f1[H1 + 8 - 5]
    residual(src, dst, f1, d1, x1, y1, z1, H1, H1 + 8)

    half, half_odd = (selection(128, 128, lambda row: row // 2, odd) for odd in (False, True))
    q = [H1 + 2 * k for k in range(4)]
    f2 = dot(jnp.concatenate([dst[i] + dst[i + 1] for i in q]), half).reshape(4, NZ, 128)
    x2[...] = dot(jnp.concatenate([x1[i + 1] for i in [H1 - 2] + q]), half).reshape(5, NZ, 128)
    y2[...] = dot(jnp.concatenate([y1[i] + y1[i + 1] for i in q]), half_odd).reshape(4, NZ, 128)
    z2[...] = dot(jnp.concatenate([z1[i] + z1[i + 1] for i in q]), half).reshape(4, NZ, 128)
    e2[...] = dot(jnp.concatenate([e1[i] + e1[i + 1] for i in q]), half).reshape(4, NZ, 128)

    def around(x, x_back, y, z, extra):
        return extra + x + x_back + y + roll(y, 1, 1) + z + behind_z(z)

    for a in range(5):
        for h in range(2):
            pair = []
            for k in (2 * h, 2 * h + 1):
                if a == 4:
                    pair.append(around(x2[k + 1], x2[k], y2[k], z2[k], e2[k]))
                else:
                    pair.append((f2, x2[1:], y2, z2)[a][k])
            both = pair[0] + roll(pair[1], 64, 1)
            to_right[2 * a + h] = both
            to_left[2 * a + h] = both

    right = left = jnp.zeros((NZ, 128), F32)
    for k in range(8):
        here = lane // 8 == k
        right = jnp.where(here, roll(own1[k], 8 * k - 88, 1), right)
        left = jnp.where(here, roll(own1[k], 8 * k - 32, 1), left)
    to_right[10] = right
    to_left[10] = left

    x3 = dot(jnp.concatenate([x2[0], x2[2], x2[4]]), half).reshape(3, NZ, 128)
    y3 = dot(jnp.concatenate([y2[0] + y2[1], y2[2] + y2[3]]), half_odd).reshape(2, NZ, 128)
    z3 = dot(jnp.concatenate([z2[0] + z2[1], z2[2] + z2[3]]), half).reshape(2, NZ, 128)
    e3 = dot(jnp.concatenate([e2[0] + e2[1], e2[2] + e2[3]]), half).reshape(2, NZ, 128)
    total = jnp.zeros((NZ, 128), F32)
    for i in range(2):
        d3 = around(x3[i + 1], x3[i], y3[i], z3[i], e3[i])
        for a, value in enumerate((x3[i + 1], y3[i], z3[i], d3)):
            spot = 32 * a + 16 * i
            total = jnp.where(lane // 16 == spot // 16, roll(value, spot - 8, 1), total)
    for i in range(own3.shape[0]):
        own3[i] = total
    for copy in copies:
        copy.wait()


def join_kernel(own2, own1, edge_f1, left, right, joined2, joined1, to_right, to_left):
    lane = lanes((NZ, 128))
    low, high = lane % 64 < 16, lane % 64 >= 48
    for a in range(10):
        value = jnp.where(high, roll(right[a], 32, 1), own2[a])
        value = jnp.where(low, roll(left[a], -32, 1), value)
        joined2[a] = value
        to_right[a] = value
        to_left[a] = value
    low, high = lane // 8 == 3, lane // 8 == 12
    for k in range(8):
        value = jnp.where(low, roll(left[10], 24 - 8 * k, 1), own1[k])
        value = jnp.where(high, roll(right[10], 96 - 8 * k, 1), value)
        joined1[k] = value
        if k >= 8 - H1:
            to_right[10 + k - 8 + H1] = value
        if k < H1:
            to_left[10 + k] = value
    to_right[10 + H1] = edge_f1[1]
    to_left[10 + H1] = edge_f1[0]


def rows_of(value, odd):
    return roll(value, 64, 1) if odd else value


def middle_kernel(
    count, behind, own, ahead, ops3, message, further, nearer, f, fx, fy, fz, d, g, va, vb
):
    for j in range(12):
        source = (behind, own, ahead)[j // 4]
        for a, ref in enumerate((f, fx, fy, fz, d)):
            ref[j] = rows_of(source[2 * a + j % 4 // 2], j % 2)
        g[j] = scale_of(d[j])
        va[j] = g[j] * f[j]
    src, dst = va, vb
    for s in range(NU - 1):
        sweep(src, dst, f, g, fx, fy, fz, 1 + s, 11 - s)
        src, dst = dst, src
    residual(src, dst, f, d, fx, fy, fz, 4, 8)
    total = None
    for i in range(2):
        matrix = selection(
            128, 128, lambda row: jnp.where((row >= 16) & (row < 48), (row - 16) // 2 + 16 * i, -99)
        )
        part = dot(dst[4 + 2 * i] + dst[5 + 2 * i], matrix)
        total = part if total is None else total + part
    value = total[:8]
    for b in range(1, 4):
        value = value + roll(total[8 * b : 8 * b + 8], 32 * b, 1)
    message[count, 0:8] = value
    message[count, 8:] = jnp.zeros((NZ - 8, 128), F32)
    for i in range(count):
        message[i] = ops3[i]
    further[...] = behind[0:10]
    nearer[...] = ahead[0:10]


def near_kernel(count, own, left, right, left_far, right_far, out):
    rhs = [ref[count, 0:8] for ref in (left_far, left, own, right, right_far)]
    for c in range(count):
        for s in range(5):
            out[c, s] = rhs[s]


PAD3 = 16


def turned(parts):
    slot = lanes(parts[0].shape) // 16
    rolled = [roll(part, 16 * s, 1) for s, part in enumerate(parts)]
    results = []
    for m in range(8):
        total = jnp.zeros_like(parts[0])
        for s, value in enumerate(rolled):
            total = jnp.where(slot == (m + s) % 8, value, total)
        results.append(roll(total, -16 * m, 1))
    return results


def spread3_kernel(count, own, left, right, left_far, right_far, out, ops3, sems):
    def unpack(i):
        values = turned([ref[i] for ref in (left_far, left, own, right, right_far)])
        for m, value in enumerate(values):
            ops3[m // 2, 2 * i + m % 2] = scale_of(value) if m >= 6 else value

    planes(0, count, unpack, 4)
    for copy in fetch(((ops3, out),), sems):
        copy.wait()


def solve_kernel(count, gathered, in_ops3, out, ops3, f3, va3, vb3, sems):
    lo, hi = PAD3, PAD3 + 2 * count
    inner = pl.ds(lo, 2 * count)
    copies = fetch([(in_ops3.at[a], ops3.at[a, inner]) for a in range(4)], sems)
    x3, y3, z3, g3 = (ops3.at[a] for a in range(4))
    for ref in (x3, y3, z3, g3, va3, vb3, f3):
        ref[0:lo] = jnp.zeros((PAD3, NZ, 128), F32)
        ref[hi : hi + PAD3] = jnp.zeros((PAD3, NZ, 128), F32)

    def unpack(i):
        p = lo + 2 * i
        for m, value in enumerate(turned([gathered[i, s] for s in range(5)])):
            part = slice(8 * (m // 2), 8 * (m // 2) + 8)
            f3[p + m % 2, part] = value

    planes(0, count, unpack, 8)
    for copy in copies:
        copy.wait()

    def first(p):
        va3[p] = g3[p] * f3[p]

    planes(lo, hi, first)

    def two(i, carry):
        sweep(va3, vb3, f3, g3, x3, y3, z3, lo, hi, 32)
        sweep(vb3, va3, f3, g3, x3, y3, z3, lo, hi, 32)
        return carry

    last = 11
    lax.fori_loop(0, (COARSE_SWEEPS - 1 - last) // 2, two, 0)
    start = lo + 2 * lax.axis_index("gx") - 4
    src, dst = va3, vb3
    for k in range(last - 1, -1, -1):
        for i in range(10 + 2 * k):
            p = start - k + i
            v, s = neighbours(src, x3, y3, z3, p)
            dst[p] = (1.0 - OMEGA) * v + g3[p] * (f3[p] + s)
        src, dst = dst, src
    out[...] = src[pl.ds(start, 10)]


def up_kernel(
    e3, in_behind3, in_behind2, in_behind, in_own, in_ahead, in_ahead2, in_ahead3,
    in_joined1, in_f1, in_ops1, in_keep0,
    out,
    f2, x2, y2, z2, d2, g2, va2, vb2, f1, va1, vb1, va0, vb0,
    behind3, behind2, behind, own, ahead, ahead2, ahead3, joined1, ops1, keep0, sems,
):
    pairs = [
        (in_behind3, behind3), (in_behind2, behind2), (in_behind, behind), (in_own, own),
        (in_ahead, ahead), (in_ahead2, ahead2), (in_ahead3, ahead3),
        (in_joined1, joined1), (in_f1, f1), (in_ops1, ops1), (in_keep0, keep0),
    ]
    copies = fetch(pairs, sems)
    sources = [(behind3, 1)]
    sources += [(ref, h) for ref in (behind2, behind, own, ahead, ahead2) for h in range(2)]
    sources += [(ahead3, 0)]
    for n, (source, h) in enumerate(sources):
        if n % 2 or n == 0:
            copies[(n + 1) // 2].wait()
        for a, ref in enumerate((f2, x2, y2, z2, d2)):
            value = source[2 * a + h]
            ref[2 * n] = value
            ref[2 * n + 1] = roll(value, 64, 1)

    def operator2(j):
        g2[j] = scale_of(d2[j])
        va2[j] = g2[j] * f2[j]

    planes(0, 24, operator2, 24)
    src, dst = va2, vb2
    for s in range(NU - 1):
        sweep(src, dst, f2, g2, x2, y2, z2, 1 + s, 23 - s, 32)
        src, dst = dst, src
    col = lax.broadcasted_iota(jnp.int32, (128, 128), 1)
    row = lax.broadcasted_iota(jnp.int32, (128, 128), 0)
    spread = ((row == (col + 128 - 16) // 2 - 64 + 32) & (col < 64)).astype(F32)
    coarse = dot(e3[...].reshape(10 * NZ, 128), spread).reshape(10, NZ, 128)
    for r in range(-7, 11):
        j = r + 10
        src[j] = src[j] + jnp.where(g2[j] > 0.0, coarse[r // 2 + 4], 0.0)
    for s in range(NU):
        sweep(src, dst, f2, g2, x2, y2, z2, 4 + s, 20 - s, 32)
        src, dst = dst, src

    for copy in copies[7:10]:
        copy.wait()
    x1, y1, z1, g1 = ops1.at[0], ops1.at[1], ops1.at[2], ops1.at[4]
    f1[1] = behind[10 + H1]
    f1[N1 - 2] = ahead[10 + H1]
    spread = (row == (col - 32 + 128) // 2 - 64 + 16).astype(F32)
    coarse = dot(src[7:17].reshape(10 * NZ, 128), spread).reshape(10, NZ, 128)
    for q in range(N1):
        if q < H1:
            value = behind[10 + q]
        elif q < H1 + 8:
            value = joined1[q - H1]
        else:
            value = ahead[10 + q - H1 - 8]
        va1[q] = value + jnp.where(g1[q] > 0.0, coarse[q // 2], 0.0)
    src, dst = va1, vb1
    for s in range(NU):
        sweep(src, dst, f1, g1, x1, y1, z1, 1 + s, N1 - 1 - s, 32)
        src, dst = dst, src

    copies[10].wait()
    v0, f0, g0, x0, y0, z0 = (keep0.at[a] for a in range(6))
    col = lax.broadcasted_iota(jnp.int32, (128, 256), 1)
    row = lax.broadcasted_iota(jnp.int32, (128, 256), 0)
    spread = (row == jnp.where(col < 192, col // 2, col // 2 - 128) + 32).astype(F32)
    for c in range(0, 12, 4):
        coarse = dot(src[4 + c : 8 + c].reshape(4 * NZ, 128), spread).reshape(4, NZ, 256)
        for k in range(8):
            i = 2 * c + k
            va0[i] = v0[i] + jnp.where(g0[i] > 0.0, coarse[k // 2], 0.0)
    src, dst = va0, vb0
    for s in range(NU):
        sweep(src, dst, f0, g0, x0, y0, z0, 1 + s, 23 - s, 11 - s)
        src, dst = dst, src
    for b in range(4):
        value = jnp.swapaxes(src[4:20, 8 * b : 8 * b + 8, 0:128], 0, 1)
        for s in range(8):
            out[4 * s + b] = value[s]


def shift(value, axis, distance):
    count = lax.axis_size(axis)
    route = [(i, i + distance) for i in range(count) if 0 <= i + distance < count]
    return lax.ppermute(value, axis, route)


def body(labels, conduct_x, conduct_y, conduct_z):
    count = lax.axis_size("gx")
    side = (NZ, 128)
    wide = (N0, NZ, 256)
    fields = (labels, conduct_x, conduct_y, conduct_z)
    own, to_right, to_left = call(
        stage_kernel,
        [pltpu.with_memory_space_constraint(x, pltpu.HBM) for x in fields],
        [(4, R0, *side), (4 * H0 - 2, *side), (4 * H0 - 3, *side)],
        [pltpu.VMEM(x.shape, x.dtype) for x in fields] + [pltpu.SemaphoreType.DMA((4,))],
        apart=(0, 1, 2, 3),
    )
    behind = shift(to_right, "gx", 1)
    ahead = shift(to_left, "gx", -1)
    to_right, to_left = call(edge_kernel, (own, behind, ahead), [(4, GROUPS, *side)] * 2)
    from_left = shift(to_right, "gy", 1)
    from_right = shift(to_left, "gy", -1)
    keep0, ops1, f1, own1, edge_f1, to_right2, to_left2, own3 = call(
        down_kernel,
        (own, behind, ahead, from_left, from_right),
        [(6, 24, NZ, 256), (5, N1, *side), (N1, *side), (8, *side), (2, *side)]
        + [(11, *side)] * 2
        + [(count, *side)],
        [(4, N0, NZ, 256)]
        + [wide] * 9
        + [(4, N1, NZ, 256), (5, N1, *side)]
        + [(N1, *side)] * 4
        + [(5, *side)]
        + [(4, *side)] * 3
        + [pltpu.SemaphoreType.DMA((20,))],
        limit=28,
        apart=(0, 1, 2),
        apart_outs=(0, 1, 2),
    )
    left, right = shift(to_right2, "gy", 1), shift(to_left2, "gy", -1)
    all3 = lax.all_to_all(own3, "gx", 0, 0)
    joined2, joined1, to_right, to_left = call(
        join_kernel,
        (to_right2, own1, edge_f1, left, right),
        [(10, *side), (8, *side)] + [(11 + H1, *side)] * 2,
    )
    behind, ahead = shift(to_right, "gx", 1), shift(to_left, "gx", -1)
    message, further, nearer = call(
        functools.partial(middle_kernel, count),
        (behind, joined2, ahead, all3),
        [(count + 1, *side)] + [(10, *side)] * 2,
        [(12, *side)] * 8,
    )
    left, right = shift(message, "gy", 1), shift(message, "gy", -1)
    behind2, ahead2 = shift(further, "gx", 1), shift(nearer, "gx", -1)
    left_far, right_far = shift(left, "gy", 1), shift(right, "gy", -1)
    near = (message, left, right, left_far, right_far)
    (rhs3,) = call(functools.partial(near_kernel, count), near, [(count, 5, 8, 128)])
    rhs3 = lax.all_to_all(rhs3, "gx", 0, 0)
    behind3, ahead3 = shift(behind2, "gx", 1), shift(ahead2, "gx", -1)
    rows3 = 2 * count + 2 * PAD3
    (ops3,) = call(
        functools.partial(spread3_kernel, count),
        near,
        [(4, 2 * count, *side)],
        [(4, 2 * count, *side), pltpu.SemaphoreType.DMA((1,))],
        apart_outs=(0,),
    )
    (e3,) = call(
        functools.partial(solve_kernel, count),
        (rhs3, pltpu.with_memory_space_constraint(ops3, pltpu.HBM)),
        [(10, *side)],
        [(4, rows3, *side)] + [(rows3, *side)] * 3 + [pltpu.SemaphoreType.DMA((4,))],
        limit=14,
        apart=(1,),
    )
    keep0, ops1, f1 = (pltpu.with_memory_space_constraint(x, pltpu.HBM) for x in (keep0, ops1, f1))
    (out,) = call(
        up_kernel,
        (e3, behind3, behind2, behind, joined2, ahead, ahead2, ahead3, joined1, f1, ops1, keep0),
        [(NZ, R0, 128)],
        [(24, *side)] * 8
        + [(N1, *side)] * 3
        + [(24, NZ, 256)] * 2
        + [(10, *side), (10, *side), (11 + H1, *side), (10, *side)]
        + [(11 + H1, *side), (10, *side), (10, *side), (8, *side)]
        + [(5, N1, *side), (6, 24, NZ, 256)]
        + [pltpu.SemaphoreType.DMA((11,))],
        limit=17,
        apart=range(1, 12),
    )
    return out


def solution(mesh):
    in_specs = (P(None, "gx", "gy"),) * 4
    out_specs = P(None, "gx", "gy")
    return jax.shard_map(body, mesh=mesh, in_specs=in_specs, out_specs=out_specs, check_vma=False)
```
